32 devices in a mesh: dp: 4 (over y, x), expert: 8 (over z, core).
Axes of the slice: x: 2, y: 2, z: 4, core: 2. Of those that a mesh axis runs over, the one named last changes fastest.
Arguments:
- tokens: bfloat16 [2048, 2048], P(('dp', 'expert')), may hold values from -6 to 6
- expert_ids: int32 [2048, 6], P(('dp', 'expert')), may hold values from 0 to 7, as said below
- gate_probs: float32 [2048, 6], P(('dp', 'expert')), may hold values from 0.1 to 0.5
- cotangent: bfloat16 [2048, 2048], P(('dp', 'expert')), may hold values from -6 to 6
- gate_proj: bfloat16 [8, 2048, 768], P('expert', 'dp'), may hold values from -0.125 to 0.125
- up_proj: bfloat16 [8, 2048, 768], P('expert', 'dp'), may hold values from -0.125 to 0.125
- down_proj: bfloat16 [8, 2048, 768], P('expert', 'dp'), may hold values from -0.21875 to 0.21875
Outputs:
- mixed: bfloat16 [2048, 2048], P(('dp', 'expert'))
- token_grads: bfloat16 [2048, 2048], P(('dp', 'expert'))
- prob_grads: float32 [2048, 6], P(('dp', 'expert'))
- grad_gate_proj: float32 [8, 2048, 768], P('expert', 'dp')
- grad_up_proj: float32 [8, 2048, 768], P('expert', 'dp')
- grad_down_proj: float32 [8, 2048, 768], P('expert', 'dp')
The draws below stay inside these ranges and needn't reach their ends.
Inputs may be any that keep to these rules, and one draw needn't show every extreme that they name: `expert_ids`: each row names 6 different experts. Among the 64 rows of one device no expert is named by more than 64 rows, and in every data group some expert is named by exactly 64 rows of every device of that group.
All inputs are finite; a program needn't handle non-finite values.
Results may differ from the reference program's by a relative error of at most 0.0065.
Values may be sent and summed in bfloat16 or wider, within the bound.
No kernel may reach another device: no remote copies, remote signals or barrier semaphores. Data moves between devices by JAX's collectives and lax.ppermute only.
A program may use at most 128 MiB of HBM per device.

```python
import jax
import jax.numpy as jnp
from jax import lax

D = 2048
TOPK = 6
FF = 768
TOK_DEV = 64
EXPERTS = 8
CAP = 64
TOKENS = 2048


def shuffle_order(sub_key):
    return jax.random.permutation(sub_key, TOK_DEV)


def draw_expert_ids(key, part):
    blocks = TOKENS // TOK_DEV
    group_count = blocks // EXPERTS
    candidates = EXPERTS * CAP
    levels = jax.random.randint(jax.random.fold_in(key, 11), (group_count, EXPERTS), 0, 4)
    favoured = jax.random.randint(jax.random.fold_in(key, 12), (group_count,), 0, EXPERTS)
    levels = jnp.where(jnp.arange(EXPERTS, dtype=jnp.int32)[None, :] == favoured[:, None], 8, levels)
    block_group = jnp.arange(blocks, dtype=jnp.int32) // EXPERTS
    block_levels = jnp.take(levels, block_group, axis=0)
    jitter = jax.random.randint(jax.random.fold_in(key, 13), (blocks, EXPERTS, CAP), 0, 4096)
    serial = jnp.arange(candidates, dtype=jnp.int32).reshape(EXPERTS, CAP)
    scores = ((block_levels[:, :, None] * 4096 + jitter) * candidates + serial[None, :, :]).reshape(blocks, candidates)
    unused, chosen = lax.top_k(scores, TOK_DEV * TOPK)
    chosen = jnp.sort(chosen, axis=1)
    table = (chosen // CAP).reshape(blocks, TOPK, TOK_DEV)
    table = jnp.transpose(table, (0, 2, 1))
    perm_keys = jax.random.split(jax.random.fold_in(key, 14), blocks)
    orders = jax.vmap(shuffle_order)(perm_keys)
    table = jnp.take_along_axis(table, orders[:, :, None], axis=1)
    shifts = jax.random.randint(jax.random.fold_in(key, 15), (blocks, TOK_DEV, 1), 0, TOPK)
    rotate = (jnp.arange(TOPK, dtype=jnp.int32)[None, None, :] + shifts) % TOPK
    table = jnp.take_along_axis(table, rotate, axis=2)
    return table.reshape(TOKENS, TOPK).astype(jnp.int32)


def steps_of(key, extent, shards, smallest, largest):
    def one(dim, shards_of):
        steps = jax.random.uniform(jax.random.fold_in(jax.random.fold_in(key, 6), dim), (shards_of,), jnp.float32, smallest / len(shards), largest / len(shards))
        return jnp.repeat(jnp.exp(steps), extent[dim] // shards_of).reshape((-1,) + (1,) * (len(extent) - dim - 1))

    loudness = one(*shards[0])
    for cut in shards[1:]:
        loudness = loudness * one(*cut)
    return loudness


def bell_draw(stream_key, extent, deviation, reach, shards=(), kind=jnp.bfloat16):
    gain = steps_of(stream_key, extent, shards, -0.22, 0.18) if shards else 1.0
    array = jax.random.normal(stream_key, extent, jnp.float32) * deviation * gain
    return jnp.minimum(jnp.maximum(array, -reach), reach).astype(kind)


def setup_inputs(seed: int = 0) -> dict:
    arg_keys = jax.random.split(jax.random.key(seed), 8)
    tokens = bell_draw(arg_keys[0], (TOKENS, D), 1.0, 6.0, ((0, 32),))
    expert_ids = draw_expert_ids(jax.random.fold_in(arg_keys[7], 71), 0)
    gate_probs = jnp.clip(0.1 + 0.4 * jax.random.uniform(arg_keys[2], (TOKENS, TOPK), jnp.float32) ** steps_of(arg_keys[2], (TOKENS, TOPK), ((0, 32),), -0.2, 0.2), 0.1, 0.5)
    cotangent = bell_draw(arg_keys[3], (TOKENS, D), 1.0, 6.0, ((0, 32),))
    gate_proj = bell_draw(arg_keys[4], (EXPERTS, D, FF), D ** -0.5, 0.125, ((0, 8), (1, 4)))
    up_proj = bell_draw(arg_keys[5], (EXPERTS, D, FF), D ** -0.5, 0.125, ((0, 8), (1, 4)))
    down_proj = bell_draw(arg_keys[6], (EXPERTS, D, FF), FF ** -0.5, 0.21875, ((0, 8), (1, 4)))
    return {"tokens": tokens, "expert_ids": expert_ids, "gate_probs": gate_probs, "cotangent": cotangent, "gate_proj": gate_proj, "up_proj": up_proj, "down_proj": down_proj}


def routing_slots(expert_ids):
    onehot = (expert_ids[:, :, None] == jnp.arange(EXPERTS, dtype=jnp.int32)[None, None, :]).astype(jnp.int32)
    per_token = jnp.sum(onehot, axis=1)
    earlier = jnp.cumsum(per_token, axis=0) - per_token
    return jnp.sum(onehot * earlier[:, None, :], axis=2).astype(jnp.int32)


def forward_rows(rows, gate_proj, up_proj, down_proj):
    gate_pre = jnp.dot(rows, gate_proj, preferred_element_type=jnp.float32)
    up_pre = jnp.dot(rows, up_proj, preferred_element_type=jnp.float32)
    hidden = (jax.nn.silu(gate_pre) * up_pre).astype(jnp.bfloat16)
    expert_out = lax.dot_general(hidden, down_proj, (((1,), (1,)), ((), ())), preferred_element_type=jnp.float32).astype(jnp.bfloat16)
    return expert_out, gate_pre, up_pre, hidden


def backward_rows(grad_rows, gate_pre, up_pre, gate_proj, up_proj, down_proj):
    d_hidden = jnp.dot(grad_rows, down_proj, preferred_element_type=jnp.float32)
    sigmoid_gate = jax.nn.sigmoid(gate_pre)
    silu_gate = gate_pre * sigmoid_gate
    d_gate = (d_hidden * up_pre * sigmoid_gate * (1.0 + gate_pre * (1.0 - sigmoid_gate))).astype(jnp.bfloat16)
    d_up = (d_hidden * silu_gate).astype(jnp.bfloat16)
    across = (((1,), (1,)), ((), ()))
    d_rows = lax.dot_general(d_gate, gate_proj, across, preferred_element_type=jnp.float32)
    d_rows = d_rows + lax.dot_general(d_up, up_proj, across, preferred_element_type=jnp.float32)
    return d_rows.astype(jnp.bfloat16), d_gate, d_up


def place_rows(spots, rows):
    empty = jnp.zeros((EXPERTS * CAP, D), rows.dtype)
    return empty.at[spots.reshape(-1)].set(rows.reshape(-1, D))


def pick_rows(source_rows, spots):
    return jnp.take(source_rows, spots.reshape(-1), axis=0)


def reference(tokens, expert_ids, gate_probs, cotangent, gate_proj, up_proj, down_proj):
    blocks = TOKENS // TOK_DEV
    ids_block = expert_ids.reshape(blocks, TOK_DEV, TOPK)
    slot_index = jax.vmap(routing_slots)(ids_block)
    position = (ids_block * CAP + slot_index).astype(jnp.int32)
    token_rows = jnp.broadcast_to(tokens.reshape(blocks, TOK_DEV, 1, D), (blocks, TOK_DEV, TOPK, D))
    scaled = (gate_probs.reshape(blocks, TOK_DEV, TOPK, 1) * cotangent.reshape(blocks, TOK_DEV, 1, D).astype(jnp.float32)).astype(jnp.bfloat16)
    slot_rows = jax.vmap(place_rows)(position, token_rows).reshape(blocks, EXPERTS, CAP, D)
    slot_grads = jax.vmap(place_rows)(position, scaled).reshape(blocks, EXPERTS, CAP, D)
    contract_rows = (((0,), (0,)), ((), ()))

    def one_expert(expert_id):
        rows_in = lax.dynamic_index_in_dim(slot_rows, expert_id, 1, keepdims=False).reshape(blocks * CAP, D)
        grads_in = lax.dynamic_index_in_dim(slot_grads, expert_id, 1, keepdims=False).reshape(blocks * CAP, D)
        gate_one = lax.dynamic_index_in_dim(gate_proj, expert_id, 0, keepdims=False)
        up_one = lax.dynamic_index_in_dim(up_proj, expert_id, 0, keepdims=False)
        down_one = lax.dynamic_index_in_dim(down_proj, expert_id, 0, keepdims=False)
        expert_out, gate_pre, up_pre, hidden = forward_rows(rows_in, gate_one, up_one, down_one)
        d_rows, d_gate, d_up = backward_rows(grads_in, gate_pre, up_pre, gate_one, up_one, down_one)
        grad_gate = lax.dot_general(rows_in, d_gate, contract_rows, preferred_element_type=jnp.float32)
        grad_up = lax.dot_general(rows_in, d_up, contract_rows, preferred_element_type=jnp.float32)
        grad_down = lax.dot_general(grads_in, hidden, contract_rows, preferred_element_type=jnp.float32)
        return expert_out.reshape(blocks, CAP, D), d_rows.reshape(blocks, CAP, D), grad_gate, grad_up, grad_down

    outs_all, rows_all, grad_gate, grad_up, grad_down = lax.map(one_expert, jnp.arange(EXPERTS, dtype=jnp.int32))
    returned = jnp.transpose(outs_all, (1, 0, 2, 3)).reshape(blocks, EXPERTS * CAP, D)
    grad_back = jnp.transpose(rows_all, (1, 0, 2, 3)).reshape(blocks, EXPERTS * CAP, D)
    picked = jax.vmap(pick_rows)(returned, position).reshape(blocks, TOK_DEV, TOPK, D).astype(jnp.float32)
    picked_grads = jax.vmap(pick_rows)(grad_back, position).reshape(blocks, TOK_DEV, TOPK, D).astype(jnp.float32)
    mixed = jnp.sum(gate_probs.reshape(blocks, TOK_DEV, TOPK, 1) * picked, axis=2).astype(jnp.bfloat16).reshape(TOKENS, D)
    prob_grads = jnp.sum(cotangent.reshape(blocks, TOK_DEV, 1, D).astype(jnp.float32) * picked, axis=3).reshape(TOKENS, TOPK)
    token_grads = jnp.sum(picked_grads, axis=2).astype(jnp.bfloat16).reshape(TOKENS, D)
    return (mixed, token_grads, prob_grads, grad_gate, grad_up, grad_down)
```

```python
import jax
import jax.numpy as jnp
from jax import lax
from jax.sharding import PartitionSpec as P

AXES = ("dp", "expert")
ACROSS = (((1,), (1,)), ((), ()))
OVER_ROWS = (((0,), (0,)), ((), ()))


def routing_slots(expert_ids, experts):
    onehot = (expert_ids[:, :, None] == jnp.arange(experts, dtype=jnp.int32)[None, None, :]).astype(
        jnp.int32
    )
    per_token = jnp.sum(onehot, axis=1)
    earlier = jnp.cumsum(per_token, axis=0) - per_token
    return jnp.sum(onehot * earlier[:, None, :], axis=2)


def forward_rows(rows, gate_proj, up_proj, down_proj):
    gate_pre = jnp.dot(rows, gate_proj, preferred_element_type=jnp.float32)
    up_pre = jnp.dot(rows, up_proj, preferred_element_type=jnp.float32)
    hidden = (jax.nn.silu(gate_pre) * up_pre).astype(jnp.bfloat16)
    expert_out = lax.dot_general(
        hidden, down_proj, ACROSS, preferred_element_type=jnp.float32
    ).astype(jnp.bfloat16)
    return (expert_out, gate_pre, up_pre, hidden)


def backward_rows(grad_rows, gate_pre, up_pre, gate_proj, up_proj, down_proj):
    d_hidden = jnp.dot(grad_rows, down_proj, preferred_element_type=jnp.float32)
    sigmoid_gate = jax.nn.sigmoid(gate_pre)
    silu_gate = gate_pre * sigmoid_gate
    d_gate = (d_hidden * up_pre * sigmoid_gate * (1.0 + gate_pre * (1.0 - sigmoid_gate))).astype(
        jnp.bfloat16
    )
    d_up = (d_hidden * silu_gate).astype(jnp.bfloat16)
    d_rows = lax.dot_general(d_gate, gate_proj, ACROSS, preferred_element_type=jnp.float32)
    d_rows = d_rows + lax.dot_general(d_up, up_proj, ACROSS, preferred_element_type=jnp.float32)
    return (d_rows.astype(jnp.bfloat16), d_gate, d_up)


def pick_rows(source_rows, position, top_count):
    chosen = jnp.take(source_rows, position.reshape(-1), axis=0)
    return chosen.reshape(position.shape[0], top_count, source_rows.shape[1])


def capacity_of(tok_dev, top_count, experts):
    return min(tok_dev, (tok_dev * top_count * 4 + 3 * experts - 1) // (3 * experts))


def slot_plan(tokens, expert_ids, gate_probs, cotangent, gate_proj, up_proj, down_proj):
    experts = lax.axis_size("expert")
    tok_dev, top_count = expert_ids.shape
    model_width = tokens.shape[1]
    capacity = capacity_of(tok_dev, top_count, experts)
    slot_index = routing_slots(expert_ids, experts)
    position = expert_ids * capacity + slot_index
    placing = (
        position[None, :, :] == jnp.arange(experts * capacity, dtype=jnp.int32)[:, None, None]
    ).astype(jnp.float32)
    placer = jnp.sum(placing, axis=2)
    weighted = jnp.sum(placing * gate_probs[None, :, :], axis=2)
    row_send = (
        jnp.dot(placer.astype(jnp.bfloat16), tokens, preferred_element_type=jnp.float32)
        .astype(jnp.bfloat16)
        .reshape(experts, capacity, model_width)
    )
    grad_send = (
        jnp.dot(weighted, cotangent.astype(jnp.float32), precision=lax.Precision.HIGHEST)
        .astype(jnp.bfloat16)
        .reshape(experts, capacity, model_width)
    )
    full_gate, full_up, full_down = (
        lax.all_gather(gate_proj[0], "dp", axis=0, tiled=True),
        lax.all_gather(up_proj[0], "dp", axis=0, tiled=True),
        lax.all_gather(down_proj[0], "dp", axis=0, tiled=True),
    )

    def exchange(rows):
        return lax.all_to_all(
            rows.reshape(experts, capacity, model_width),
            "expert",
            split_axis=0,
            concat_axis=0,
            tiled=True,
        ).reshape(-1, model_width)

    rows_flat = exchange(row_send)
    expert_out, gate_pre, up_pre, hidden = forward_rows(rows_flat, full_gate, full_up, full_down)
    returned = exchange(expert_out)
    grads_flat = exchange(grad_send)
    d_rows, d_gate, d_up = backward_rows(
        grads_flat, gate_pre, up_pre, full_gate, full_up, full_down
    )
    grad_back = exchange(d_rows)
    picked = pick_rows(returned, position, top_count).astype(jnp.float32)
    mixed = jnp.sum(gate_probs[:, :, None] * picked, axis=1).astype(jnp.bfloat16)
    prob_grads = jnp.sum(cotangent.astype(jnp.float32)[:, None, :] * picked, axis=2)
    picked_grads = pick_rows(grad_back, position, top_count).astype(jnp.float32)
    token_grads = jnp.sum(picked_grads, axis=1).astype(jnp.bfloat16)
    hidden_units = hidden.shape[1]
    gate_term = lax.dot_general(rows_flat, d_gate, OVER_ROWS, preferred_element_type=jnp.float32)
    up_term = lax.dot_general(rows_flat, d_up, OVER_ROWS, preferred_element_type=jnp.float32)
    down_term = lax.dot_general(grads_flat, hidden, OVER_ROWS, preferred_element_type=jnp.float32)
    shares = lax.psum_scatter(
        jnp.concatenate([gate_term, up_term, down_term], axis=1),
        "dp",
        scatter_dimension=0,
        tiled=True,
    )
    grad_gate = shares[:, :hidden_units]
    grad_up = shares[:, hidden_units : 2 * hidden_units]
    grad_down = shares[:, 2 * hidden_units :]
    return (mixed, token_grads, prob_grads, grad_gate[None], grad_up[None], grad_down[None])


def flat_index(y, x, z, core):
    return ((y * 2 + x) * 4 + z) * 2 + core


def pairs(target):
    found = []
    for y in range(2):
        for x in range(2):
            for z in range(4):
                for core in range(2):
                    there = target(y, x, z, core)
                    if there is not None:
                        found.append((flat_index(y, x, z, core), flat_index(*there)))
    return found


TO_X = pairs(lambda y, x, z, core: (y, 1 - x, z, core))
TO_Y = pairs(lambda y, x, z, core: (1 - y, x, z, core))
TO_CORE = pairs(lambda y, x, z, core: (y, x, z, 1 - core))


def z_up(first, last):
    return pairs(lambda y, x, z, core: (y, x, z + 1, core) if first <= z <= last else None)


def z_down(first, last):
    return pairs(lambda y, x, z, core: (y, x, z - 1, core) if first <= z <= last else None)


def send(array, where):
    return lax.ppermute(array, AXES, where)


def gather_weight(shard):
    half = shard.shape[0] // 2
    from_x = send(shard, TO_X)
    from_y = send(shard, TO_Y)
    corner_first = send(from_x[:half], TO_Y)
    corner_last = send(from_y[half:], TO_X)
    return jnp.concatenate([shard, from_x, from_y, corner_first, corner_last], axis=0)


def reduce_grad(grad):
    block = grad.shape[0] // 4
    half = block // 2
    narrow = jnp.bfloat16
    first = send(grad[3 * block : 3 * block + half].astype(narrow), TO_Y)
    last = send(grad[3 * block + half :].astype(narrow), TO_X)
    for_x = jnp.concatenate(
        [grad[block : block + half] + first.astype(jnp.float32), grad[block + half : 2 * block]]
    ).astype(narrow)
    for_y = jnp.concatenate(
        [grad[2 * block : 2 * block + half], grad[2 * block + half : 3 * block] + last.astype(jnp.float32)]
    ).astype(narrow)
    from_x = send(for_x, TO_X)
    from_y = send(for_y, TO_Y)
    return grad[:block] + from_x.astype(jnp.float32) + from_y.astype(jnp.float32)


def gather_line(own, z):
    ups, downs = [own], [own]
    for step in range(3):
        ups.append(send(ups[-1], z_up(step, 2)))
        downs.append(send(downs[-1], z_down(1, 3 - step)))
    slots = [own] + [jnp.where(z >= s, ups[s], downs[4 - s]) for s in range(1, 4)]
    own_core = jnp.stack(slots)
    other_core = send(own_core, TO_CORE)
    return jnp.concatenate([own_core, other_core])


def reduce_line(partial):
    rest = send(partial[4:].astype(jnp.bfloat16), TO_CORE)
    mine = partial[:4] + rest.astype(jnp.float32)
    going_up = mine[1].astype(jnp.bfloat16)
    going_down = mine[3].astype(jnp.bfloat16)
    for step in range(3):
        arrived_up = send(going_up, z_up(0, step))
        arrived_down = send(going_down, z_down(3 - step, 3))
        if step < 2:
            going_up = (mine[2 + step] + arrived_up.astype(jnp.float32)).astype(jnp.bfloat16)
            going_down = (mine[2 - step] + arrived_down.astype(jnp.float32)).astype(jnp.bfloat16)
    total = mine[0] + arrived_up.astype(jnp.float32) + arrived_down.astype(jnp.float32)
    return total.astype(jnp.bfloat16)


def relative_columns(rows, dp):
    blocks = rows.reshape(rows.shape[0], 4, -1)
    swapped = jnp.where(dp % 2 == 1, blocks[:, jnp.array([1, 0, 3, 2])], blocks)
    swapped = jnp.where(dp >= 2, swapped[:, jnp.array([2, 3, 0, 1])], swapped)
    return swapped.reshape(rows.shape)


def dense_plan(tokens, expert_ids, gate_probs, cotangent, gate_proj, up_proj, down_proj):
    f32 = jnp.float32
    experts = lax.axis_size("expert")
    tok_dev = tokens.shape[0]
    width = tokens.shape[1]
    dp = lax.axis_index("dp")
    me = lax.axis_index("expert")
    z, core = me // 2, me % 2
    chosen = expert_ids[:, :, None] == jnp.arange(experts, dtype=jnp.int32)[None, None, :]
    prob_of = jnp.sum(jnp.where(chosen, gate_probs[:, :, None], 0.0), axis=1)
    prob_all = lax.all_gather(prob_of, "expert", axis=0)
    prob_mine = jnp.sum(
        jnp.where(jnp.arange(experts)[None, None, :] == me, prob_all, 0.0), axis=2
    )
    slot = jnp.arange(8, dtype=jnp.int32)
    origin = ((z - slot % 4) % 4) * 2 + (core + slot // 4) % 2
    origin_hot = origin[:, None] == slot[None, :]
    prob = jnp.sum(jnp.where(origin_hot[:, :, None], prob_mine[None], 0.0), axis=1).reshape(-1, 1)

    full_gate = gather_weight(gate_proj[0])
    full_up = gather_weight(up_proj[0])
    full_down = gather_weight(down_proj[0])

    rows = gather_line(relative_columns(tokens, dp), z).reshape(-1, width)
    grads = gather_line(relative_columns(cotangent, dp), z).reshape(-1, width)

    gate_pre = jnp.dot(rows, full_gate, preferred_element_type=f32)
    up_pre = jnp.dot(rows, full_up, preferred_element_type=f32)
    sigmoid_gate = jax.nn.sigmoid(gate_pre)
    silu_gate = gate_pre * sigmoid_gate
    hidden = silu_gate * up_pre
    hidden_scaled = (hidden * prob).astype(jnp.bfloat16)
    grad_down = reduce_grad(
        lax.dot_general(grads, hidden_scaled, OVER_ROWS, preferred_element_type=f32)
    )
    mixed = reduce_line(
        lax.dot_general(hidden_scaled, full_down, ACROSS, preferred_element_type=f32).reshape(
            8, tok_dev, width
        )
    )
    raw = jnp.dot(grads, full_down, preferred_element_type=f32)
    prob_dots = jnp.sum(raw * hidden, axis=1).reshape(8, tok_dev)
    d_hidden = raw * prob
    d_gate = (d_hidden * up_pre * sigmoid_gate * (1.0 + gate_pre * (1.0 - sigmoid_gate))).astype(
        jnp.bfloat16
    )
    d_up = (d_hidden * silu_gate).astype(jnp.bfloat16)
    grad_gate = reduce_grad(lax.dot_general(rows, d_gate, OVER_ROWS, preferred_element_type=f32))
    grad_up = reduce_grad(lax.dot_general(rows, d_up, OVER_ROWS, preferred_element_type=f32))
    d_rows = lax.dot_general(d_gate, full_gate, ACROSS, preferred_element_type=f32)
    d_rows = d_rows + lax.dot_general(d_up, full_up, ACROSS, preferred_element_type=f32)
    token_grads = reduce_line(d_rows.reshape(8, tok_dev, width))

    by_origin = jnp.sum(jnp.where(origin_hot[:, :, None], prob_dots[:, None, :], 0.0), axis=0)
    dots_all = lax.all_gather(by_origin, "expert", axis=0)
    dots_here = jnp.sum(
        jnp.where(jnp.arange(experts)[None, :, None] == me, dots_all, 0.0), axis=1
    )
    prob_grads = jnp.sum(jnp.where(chosen, dots_here.T[:, None, :], 0.0), axis=2)
    return (
        relative_columns(mixed, dp),
        relative_columns(token_grads, dp),
        prob_grads,
        grad_gate[None],
        grad_up[None],
        grad_down[None],
    )


def on_device(tokens, expert_ids, *rest):
    tok_dev, top_count = expert_ids.shape
    experts = lax.axis_size("expert")
    square_and_line = lax.axis_size("dp") == 4 and experts == 8
    if square_and_line and capacity_of(tok_dev, top_count, experts) == tok_dev:
        return dense_plan(tokens, expert_ids, *rest)
    return slot_plan(tokens, expert_ids, *rest)


def solution(mesh):
    by_token = P(AXES, None)
    by_expert = P("expert", "dp", None)
    return jax.shard_map(
        on_device,
        mesh=mesh,
        in_specs=(by_token,) * 4 + (by_expert,) * 3,
        out_specs=(by_token,) * 3 + (by_expert,) * 3,
        check_vma=False,
    )
```

```python
import jax
import jax.numpy as jnp
from jax import lax
from jax.experimental import pallas as pl
from jax.experimental.pallas import tpu as pltpu
from jax.sharding import PartitionSpec as P

AXES = ("dp", "expert")
ACROSS = (((1,), (1,)), ((), ()))
OVER_ROWS = (((0,), (0,)), ((), ()))


def routing_slots(expert_ids, experts):
    onehot = (expert_ids[:, :, None] == jnp.arange(experts, dtype=jnp.int32)[None, None, :]).astype(
        jnp.int32
    )
    per_token = jnp.sum(onehot, axis=1)
    earlier = jnp.cumsum(per_token, axis=0) - per_token
    return jnp.sum(onehot * earlier[:, None, :], axis=2)


def forward_rows(rows, gate_proj, up_proj, down_proj):
    gate_pre = jnp.dot(rows, gate_proj, preferred_element_type=jnp.float32)
    up_pre = jnp.dot(rows, up_proj, preferred_element_type=jnp.float32)
    hidden = (jax.nn.silu(gate_pre) * up_pre).astype(jnp.bfloat16)
    expert_out = lax.dot_general(
        hidden, down_proj, ACROSS, preferred_element_type=jnp.float32
    ).astype(jnp.bfloat16)
    return (expert_out, gate_pre, up_pre, hidden)


def backward_rows(grad_rows, gate_pre, up_pre, gate_proj, up_proj, down_proj):
    d_hidden = jnp.dot(grad_rows, down_proj, preferred_element_type=jnp.float32)
    sigmoid_gate = jax.nn.sigmoid(gate_pre)
    silu_gate = gate_pre * sigmoid_gate
    d_gate = (d_hidden * up_pre * sigmoid_gate * (1.0 + gate_pre * (1.0 - sigmoid_gate))).astype(
        jnp.bfloat16
    )
    d_up = (d_hidden * silu_gate).astype(jnp.bfloat16)
    d_rows = lax.dot_general(d_gate, gate_proj, ACROSS, preferred_element_type=jnp.float32)
    d_rows = d_rows + lax.dot_general(d_up, up_proj, ACROSS, preferred_element_type=jnp.float32)
    return (d_rows.astype(jnp.bfloat16), d_gate, d_up)


def pick_rows(source_rows, position, top_count):
    chosen = jnp.take(source_rows, position.reshape(-1), axis=0)
    return chosen.reshape(position.shape[0], top_count, source_rows.shape[1])


def capacity_of(tok_dev, top_count, experts):
    return min(tok_dev, (tok_dev * top_count * 4 + 3 * experts - 1) // (3 * experts))


def slot_plan(tokens, expert_ids, gate_probs, cotangent, gate_proj, up_proj, down_proj):
    experts = lax.axis_size("expert")
    tok_dev, top_count = expert_ids.shape
    model_width = tokens.shape[1]
    capacity = capacity_of(tok_dev, top_count, experts)
    slot_index = routing_slots(expert_ids, experts)
    position = expert_ids * capacity + slot_index
    placing = (
        position[None, :, :] == jnp.arange(experts * capacity, dtype=jnp.int32)[:, None, None]
    ).astype(jnp.float32)
    placer = jnp.sum(placing, axis=2)
    weighted = jnp.sum(placing * gate_probs[None, :, :], axis=2)
    row_send = (
        jnp.dot(placer.astype(jnp.bfloat16), tokens, preferred_element_type=jnp.float32)
        .astype(jnp.bfloat16)
        .reshape(experts, capacity, model_width)
    )
    grad_send = (
        jnp.dot(weighted, cotangent.astype(jnp.float32), precision=lax.Precision.HIGHEST)
        .astype(jnp.bfloat16)
        .reshape(experts, capacity, model_width)
    )
    full_gate, full_up, full_down = (
        lax.all_gather(gate_proj[0], "dp", axis=0, tiled=True),
        lax.all_gather(up_proj[0], "dp", axis=0, tiled=True),
        lax.all_gather(down_proj[0], "dp", axis=0, tiled=True),
    )

    def exchange(rows):
        return lax.all_to_all(
            rows.reshape(experts, capacity, model_width),
            "expert",
            split_axis=0,
            concat_axis=0,
            tiled=True,
        ).reshape(-1, model_width)

    rows_flat = exchange(row_send)
    expert_out, gate_pre, up_pre, hidden = forward_rows(rows_flat, full_gate, full_up, full_down)
    returned = exchange(expert_out)
    grads_flat = exchange(grad_send)
    d_rows, d_gate, d_up = backward_rows(
        grads_flat, gate_pre, up_pre, full_gate, full_up, full_down
    )
    grad_back = exchange(d_rows)
    picked = pick_rows(returned, position, top_count).astype(jnp.float32)
    mixed = jnp.sum(gate_probs[:, :, None] * picked, axis=1).astype(jnp.bfloat16)
    prob_grads = jnp.sum(cotangent.astype(jnp.float32)[:, None, :] * picked, axis=2)
    picked_grads = pick_rows(grad_back, position, top_count).astype(jnp.float32)
    token_grads = jnp.sum(picked_grads, axis=1).astype(jnp.bfloat16)
    hidden_units = hidden.shape[1]
    gate_term = lax.dot_general(rows_flat, d_gate, OVER_ROWS, preferred_element_type=jnp.float32)
    up_term = lax.dot_general(rows_flat, d_up, OVER_ROWS, preferred_element_type=jnp.float32)
    down_term = lax.dot_general(grads_flat, hidden, OVER_ROWS, preferred_element_type=jnp.float32)
    shares = lax.psum_scatter(
        jnp.concatenate([gate_term, up_term, down_term], axis=1),
        "dp",
        scatter_dimension=0,
        tiled=True,
    )
    grad_gate = shares[:, :hidden_units]
    grad_up = shares[:, hidden_units : 2 * hidden_units]
    grad_down = shares[:, 2 * hidden_units :]
    return (mixed, token_grads, prob_grads, grad_gate[None], grad_up[None], grad_down[None])


TILE = 256
SIDE = 128
F32 = jnp.float32
BF16 = jnp.bfloat16
VMEM = pl.BlockSpec(memory_space=pltpu.VMEM)


RING = (0, 2, 3, 1)


def flat_index(y, x, z, core):
    return ((y * 2 + x) * 4 + z) * 2 + core


def pairs(target):
    return [
        (flat_index(y, x, z, core), flat_index(*target(y, x, z, core)))
        for y in range(2)
        for x in range(2)
        for z in range(4)
        for core in range(2)
    ]


TO_X = pairs(lambda y, x, z, core: (y, 1 - x, z, core))
TO_Y = pairs(lambda y, x, z, core: (1 - y, x, z, core))
TO_CORE = pairs(lambda y, x, z, core: (y, x, z, 1 - core))
ALONG_Z = pairs(lambda y, x, z, core: (y, x, RING[(RING.index(z) + 1) % 4], core))


def send(array, where):
    return lax.ppermute(array, AXES, where)


def kernel_call(body, out_shape, **spec):
    return pl.pallas_call(
        body,
        out_shape=out_shape,
        compiler_params=pltpu.CompilerParams(vmem_limit_bytes=24 * 1024 * 1024),
        cost_estimate=pl.CostEstimate(flops=0, bytes_accessed=0, transcendentals=0),
        **spec,
    )


def shape(rows, columns, dtype):
    return jax.ShapeDtypeStruct((rows, columns), dtype)


def iota(rows, columns, axis):
    return lax.broadcasted_iota(jnp.int32, (rows, columns), axis)


def exact_parts(values, place):
    first = values.astype(BF16).astype(F32)
    rest = values - first
    second = rest.astype(BF16).astype(F32)
    third = rest - second
    parts = jnp.where(place < 8, first, jnp.where(place < 16, second, third))
    return jnp.where(place < 24, parts, 0.0).astype(BF16)


def block_at(relative, block):
    return pl.ds(pl.multiple_of((lax.axis_index("dp") ^ relative) * block, block), block)


def pack_kernel(tokens_ref, cot_ref, ids_ref, probs_ref, out_ref):
    rows, width = tokens_ref.shape
    block = width // 4
    for r in range(4):
        there = block_at(r, block)
        out_ref[:, r * block : (r + 1) * block] = tokens_ref[:, there]
        out_ref[:, width + r * block : width + (r + 1) * block] = cot_ref[:, there]
    place = iota(SIDE, rows, 0)
    prob = jnp.zeros((SIDE, rows), F32)
    for k in range(ids_ref.shape[0]):
        prob += jnp.where(place % 8 == ids_ref[k : k + 1, :], probs_ref[k : k + 1, :], 0.0)
    same = (iota(rows, rows, 0) == iota(rows, rows, 1)).astype(BF16)
    turned = lax.dot_general(same, exact_parts(prob, place), ACROSS, preferred_element_type=F32)
    out_ref[:, 2 * width :] = turned.astype(BF16)


def pack(tokens, cotangent, expert_ids, gate_probs):
    rows, width = tokens.shape
    return kernel_call(
        pack_kernel,
        shape(rows, 2 * width + SIDE, BF16),
        in_specs=[VMEM] * 4,
        out_specs=VMEM,
    )(tokens, cotangent, expert_ids.T, gate_probs.T)


def unpack_kernel(mixed_ref, back_ref, ids_ref, mixed_out, back_out, prob_out):
    rows, width = mixed_ref.shape
    block = width // 4
    for r in range(4):
        there = block_at(r, block)
        mixed_out[:, there] = mixed_ref[:, r * block : (r + 1) * block]
        back_out[:, there] = back_ref[:, r * block : (r + 1) * block]
    lane = iota(8, SIDE, 1)
    adder = ((lane < 24) & (lane % 8 == iota(8, SIDE, 0))).astype(BF16)
    by_expert = lax.dot_general(adder, back_ref[:, width:], ACROSS, preferred_element_type=F32)
    for k in range(ids_ref.shape[0]):
        hit = iota(8, rows, 0) == ids_ref[k : k + 1, :]
        prob_out[k : k + 1, :] = jnp.sum(jnp.where(hit, by_expert, 0.0), axis=0, keepdims=True)


def unpack(mixed, back, expert_ids):
    mixed, back, prob = kernel_call(
        unpack_kernel,
        (shape(*mixed.shape, BF16), shape(*mixed.shape, BF16), shape(*expert_ids.T.shape, F32)),
        in_specs=[VMEM] * 3,
        out_specs=(VMEM,) * 3,
    )(mixed, back, expert_ids.T)
    return mixed, back, prob.T


def turn_kernel(own_ref, other_ref, out_ref):
    rows = own_ref.shape[0]
    out_ref[:, :rows] = own_ref[...].T
    out_ref[:, rows:] = other_ref[...].T


def turn(whole, width):
    rows = whole[0].shape[0]
    return kernel_call(
        turn_kernel,
        shape(width, 2 * rows, BF16),
        grid=(width // TILE,),
        in_specs=[pl.BlockSpec((rows, TILE), lambda i: (0, i))] * 2,
        out_specs=pl.BlockSpec((TILE, 2 * rows), lambda i: (i, 0)),
    )(*whole)


def times_pieces(rows_ref, pieces):
    total, start = None, 0
    for piece in pieces:
        depth = piece.shape[0]
        term = jnp.dot(rows_ref[:, start : start + depth], piece[...], preferred_element_type=F32)
        total = term if total is None else total + term
        start += depth
    return total


def early_kernel(own_rows, other_rows, own_ref, x_ref, y_ref, out_ref):
    half = own_rows.shape[0]
    out_ref[:half] = times_pieces(own_rows, (own_ref, x_ref, y_ref))
    out_ref[half:] = times_pieces(other_rows, (own_ref, x_ref, y_ref))


def early_products(whole, direct, width):
    half = whole[0].shape[0]
    depth, columns = direct[0].shape
    steps = columns // TILE
    piece = pl.BlockSpec((depth, TILE), lambda j: (0, j))
    return kernel_call(
        early_kernel,
        shape(2 * half, columns, F32),
        grid=(steps,),
        in_specs=[pl.BlockSpec((half, width), lambda j: (0, j // (steps * 2 // 3)))] * 2
        + [piece] * 3,
        out_specs=pl.BlockSpec((2 * half, TILE), lambda j: (0, j)),
    )(*whole, *direct)


def forward_kernel(*refs):
    both_rows, both_parts, earlies, gates, ups = (refs[i : i + 2] for i in range(0, 10, 2))
    scaled_ref, for_gate_ref, for_up_ref, hidden_ref = refs[10:]
    half = both_rows[0].shape[0]
    for index in range(2):
        at = slice(index * half, (index + 1) * half)
        gate_pre = earlies[0][at] + times_pieces(both_rows[index], gates)
        up_pre = earlies[1][at] + times_pieces(both_rows[index], ups)
        lane = iota(half, SIDE, 1)
        mine = (lane < 24) & (lane % 8 == lax.axis_index("expert"))
        parts = both_parts[index][...].astype(F32)
        prob = jnp.sum(jnp.where(mine, parts, 0.0), axis=1, keepdims=True)
        sigmoid_gate = 1.0 / (1.0 + jnp.exp(-gate_pre))
        silu_gate = gate_pre * sigmoid_gate
        hidden = silu_gate * up_pre
        hidden_ref[at] = hidden
        scaled_ref[at] = (hidden * prob).astype(BF16)
        slope = sigmoid_gate * (1.0 + gate_pre * (1.0 - sigmoid_gate))
        for_gate_ref[at] = prob * (up_pre * slope)
        for_up_ref[at] = prob * silu_gate


def forward(whole, early, corner, width, units):
    half = whole[0].shape[0]
    rows = 2 * half
    steps = units // TILE
    block = width // 4
    tile = pl.BlockSpec((rows, TILE), lambda j: (0, j))
    next_tile = pl.BlockSpec((rows, TILE), lambda j: (0, steps + j))
    return kernel_call(
        forward_kernel,
        (shape(rows, units, BF16),) + (shape(rows, units, F32),) * 3,
        grid=(steps,),
        in_specs=[pl.BlockSpec((half, block), lambda j: (0, 3))] * 2
        + [pl.BlockSpec((half, SIDE), lambda j: (0, 2 * width // SIDE))] * 2
        + [tile, next_tile]
        + [pl.BlockSpec((block // 2, TILE), lambda j: (0, j))] * 2
        + [pl.BlockSpec((block // 2, TILE), lambda j: (0, steps + j))] * 2,
        out_specs=(tile,) * 4,
    )(*whole, *whole, early, early, *corner, *corner)


def backward_kernel(own_ref, other_ref, early_ref, first_ref, last_ref, *refs):
    for_gate_ref, for_up_ref, hidden_ref, d_gate_ref, d_up_ref, dots_ref, sum_ref = refs
    step = pl.program_id(0)
    half = own_ref.shape[0]

    @pl.when(step == 0)
    def _():
        sum_ref[...] = jnp.zeros_like(sum_ref)

    for index, grads_ref in enumerate((own_ref, other_ref)):
        at = slice(index * half, (index + 1) * half)
        raw = early_ref[at] + times_pieces(grads_ref, (first_ref, last_ref))
        d_gate_ref[at] = (raw * for_gate_ref[at]).astype(BF16)
        d_up_ref[at] = (raw * for_up_ref[at]).astype(BF16)
        sum_ref[at] += jnp.sum(raw * hidden_ref[at], axis=1, keepdims=True)

    @pl.when(step == pl.num_programs(0) - 1)
    def _():
        lane = iota(2 * half, SIDE, 1)
        mine = lane % 8 == lax.axis_index("expert")
        dots_ref[...] = exact_parts(jnp.where(mine, sum_ref[...], 0.0), lane)


def backward(whole, early, corner, for_gate, for_up, hidden, width):
    rows, units = hidden.shape
    steps = units // TILE
    block = width // 4
    tile = pl.BlockSpec((rows, TILE), lambda j: (0, j))
    return kernel_call(
        backward_kernel,
        (shape(rows, units, BF16),) * 2 + (shape(rows, SIDE, BF16),),
        grid=(steps,),
        in_specs=[pl.BlockSpec((rows // 2, block), lambda j: (0, 7))] * 2
        + [pl.BlockSpec((rows, TILE), lambda j: (0, 2 * steps + j))]
        + [pl.BlockSpec((block // 2, TILE), lambda j: (0, j))] * 2
        + [tile] * 3,
        out_specs=(tile, tile, pl.BlockSpec((rows, SIDE), lambda j: (0, 0))),
        scratch_shapes=[pltpu.VMEM((rows, 1), F32)],
    )(*whole, early, *corner, for_gate, for_up, hidden)


def first_half_blocks(i):
    return jnp.where(i == 3, 4, 7 - 4 * (i % 2) - i // 2)


def later_half_blocks(i):
    return jnp.where(i < 2, 2 + 3 * i, i - 2)


def first_grad_kernel(turned_ref, term_ref, to_x, to_y):
    step = pl.program_id(0)
    part = jnp.dot(turned_ref[...], term_ref[...], preferred_element_type=F32).astype(BF16)

    @pl.when(step < 2)
    def _():
        to_x[...] = part

    @pl.when(step >= 2)
    def _():
        to_y[...] = part


def later_grad_kernel(turned_ref, term_ref, for_x, for_y, own):
    step = pl.program_id(0)
    part = jnp.dot(turned_ref[...], term_ref[...], preferred_element_type=F32)

    @pl.when(step == 0)
    def _():
        for_x[...] = part

    @pl.when(step == 1)
    def _():
        for_y[...] = part

    @pl.when(step >= 2)
    def _():
        own[...] = part


def first_grads(turned, first, width, term):
    rows, units = term.shape
    half = width // 8

    def at(start):
        return pl.BlockSpec((half, units), lambda i: (jnp.clip(i - start, 0, 1), 0))

    return kernel_call(
        first_grad_kernel,
        (shape(2 * half, units, BF16),) * 2,
        grid=(4,),
        in_specs=[
            pl.BlockSpec((half, rows), lambda i: (first + first_half_blocks(i), 0)),
            pl.BlockSpec((rows, units), lambda i: (0, 0)),
        ],
        out_specs=(at(0), at(2)),
    )(turned, term)


def later_grads(turned, first, width, term):
    rows, units = term.shape
    half = width // 8
    once = pl.BlockSpec((half, units), lambda i: (0, 0))
    return kernel_call(
        later_grad_kernel,
        (shape(half, units, F32),) * 2 + (shape(2 * half, units, F32),),
        grid=(4,),
        in_specs=[
            pl.BlockSpec((half, rows), lambda i: (first + later_half_blocks(i), 0)),
            pl.BlockSpec((rows, units), lambda i: (0, 0)),
        ],
        out_specs=(
            once,
            once,
            pl.BlockSpec((half, units), lambda i: (jnp.clip(i - 2, 0, 1), 0)),
        ),
    )(turned, term)


def back_kernel(count, *refs):
    terms, weights, rest = refs[:count], refs[count : count + 5], refs[count + 5 :]
    out_ref = rest[-1]
    units = terms[0].shape[1]
    start = 0
    for weight in weights:
        depth = weight.shape[0]
        total = None
        for index, term in enumerate(terms):
            part = lax.dot_general(
                term[...],
                weight[:, index * units : (index + 1) * units],
                ACROSS,
                preferred_element_type=F32,
            )
            total = part if total is None else total + part
        out_ref[:, start : start + depth] = total.astype(BF16)
        start += depth
    if len(rest) == 2:
        out_ref[:, start:] = rest[0][...]


def whole_rows(piece, start, across):
    return pl.BlockSpec((piece.shape[0], across), lambda i: (0, start // across))


def back_to_rows(terms, direct, start, corner, extra):
    rows, units = terms[0].shape
    across = units * len(terms)
    pieces = [(piece, start) for piece in direct] + [(piece, 0) for piece in corner]
    width = sum(piece.shape[0] for piece, _ in pieces) + sum(e.shape[1] for e in extra)

    def body(*refs):
        back_kernel(len(terms), *refs)

    return kernel_call(
        body,
        shape(rows, width, BF16),
        grid=(rows // TILE,),
        in_specs=[pl.BlockSpec((TILE, units), lambda i: (i, 0)) for _ in terms]
        + [whole_rows(piece, first, across) for piece, first in pieces]
        + [pl.BlockSpec((TILE, e.shape[1]), lambda i: (i, 0)) for e in extra],
        out_specs=pl.BlockSpec((TILE, width), lambda i: (i, 0)),
    )(*terms, *[piece for piece, _ in pieces], *extra)


def total_kernel(own_ref, from_x, from_y, late_x, late_y, out_ref):
    out_ref[0] = own_ref[0] + (from_y[0].astype(F32) + late_x[...].astype(F32))
    out_ref[1] = own_ref[1] + (from_x[0].astype(F32) + late_y[...].astype(F32))


def total(own, from_x, from_y, late_x, late_y):
    block, units = own.shape
    half = block // 2
    step = half // 4
    both = pl.BlockSpec((2, step, units), lambda i: (0, i, 0))
    low = pl.BlockSpec((1, step, units), lambda i: (1, i, 0))
    late = pl.BlockSpec((step, units), lambda i: (i, 0))
    halves = (2, half, units)
    return kernel_call(
        total_kernel,
        jax.ShapeDtypeStruct(halves, F32),
        grid=(half // step,),
        in_specs=[both, low, low, late, late],
        out_specs=both,
    )(own.reshape(halves), from_x.reshape(halves), from_y.reshape(halves), late_x, late_y).reshape(
        1, block, units
    )


def gather_weights(shard, split):
    half = shard.shape[0] // 2
    from_x = send(shard, TO_X)
    from_y = send(shard, TO_Y)
    gate_up = [send(from_x[:half, :split], TO_Y), send(from_y[half:, :split], TO_X)]
    down = [send(from_x[:half, split:], TO_Y), send(from_y[half:, split:], TO_X)]
    return [shard, from_x, from_y], gate_up, down


def send_first(to_x, to_y):
    return send(to_x, TO_X), send(to_y, TO_Y)


def send_later(for_x, for_y, from_x, from_y):
    half = for_x.shape[0]
    late_x = send((for_x + from_y[:half].astype(F32)).astype(BF16), TO_X)
    late_y = send((for_y + from_x[:half].astype(F32)).astype(BF16), TO_Y)
    return late_x, late_y


def gather_rows(own):
    slots = [own]
    for _ in range(3):
        slots.append(send(slots[-1], ALONG_Z))
    return jnp.concatenate(slots)


def sum_over_experts(rows):
    half = rows.shape[0] // 2
    block = half // 4
    arrived = send(rows[half:], TO_CORE)

    def both_cores(slot):
        at = slice(slot * block, (slot + 1) * block)
        return rows[at].astype(F32) + arrived[at].astype(F32)

    moving = send(both_cores(1).astype(BF16), ALONG_Z)
    for slot in (2, 3):
        moving = send((both_cores(slot) + moving.astype(F32)).astype(BF16), ALONG_Z)
    return (both_cores(0) + moving.astype(F32)).astype(BF16)


def after(arrays, *others):
    return lax.optimization_barrier((arrays, others))[0]


def dense_plan(tokens, expert_ids, gate_probs, cotangent, gate_proj, up_proj, down_proj):
    width = tokens.shape[1]
    units = gate_proj.shape[2]
    halves = width // TILE
    shard = jnp.concatenate([gate_proj[0], up_proj[0], down_proj[0]], axis=1)
    direct, gate_up, down = gather_weights(shard, 2 * units)
    packed = pack(tokens, cotangent, expert_ids, gate_probs)
    own_core = gather_rows(packed)
    own_core = after(own_core, direct)
    whole = (own_core, send(own_core, TO_CORE))
    early = early_products(whole, direct, width)
    turned = turn(whole, 2 * width)
    early, turned, gate_up = lax.optimization_barrier((early, turned, gate_up))

    scaled, for_gate, for_up, hidden = forward(whole, early, gate_up, width, units)
    down_first = send_first(*(sent := first_grads(turned, halves, width, scaled)))
    scaled, down = after((scaled, down), sent)
    mixed = sum_over_experts(back_to_rows([scaled], direct, 2 * units, down, []))
    for_x, for_y, down_own = later_grads(turned, halves, width, scaled)
    hidden = after(hidden, for_x)
    d_gate, d_up, dots = backward(whole, early, down, for_gate, for_up, hidden, width)
    down_late = send_later(for_x, for_y, *down_first)
    d_gate, d_up = after((d_gate, d_up), down_first)
    gate_sent = first_grads(turned, 0, width, d_gate)
    up_sent = first_grads(turned, 0, width, d_up)
    gate_first, up_first = send_first(*gate_sent), send_first(*up_sent)
    d_gate, d_up = after((d_gate, d_up), gate_sent, up_sent)
    back = sum_over_experts(back_to_rows([d_gate, d_up], direct, 0, gate_up, [dots]))
    grad_down = total(down_own, *down_first, *down_late)
    d_gate, d_up = after((d_gate, d_up), grad_down)
    *gate_later, gate_own = later_grads(turned, 0, width, d_gate)
    *up_later, up_own = later_grads(turned, 0, width, d_up)
    gate_late = send_later(*gate_later, *gate_first)
    up_late = send_later(*up_later, *up_first)
    outs = unpack(mixed, back, expert_ids)
    gate_late = after(gate_late, outs)
    grad_gate = total(gate_own, *gate_first, *gate_late)
    up_late = after(up_late, grad_gate)
    grad_up = total(up_own, *up_first, *up_late)
    return (*outs, grad_gate, grad_up, grad_down)


def on_device(tokens, expert_ids, *rest):
    tok_dev, top_count = expert_ids.shape
    experts = lax.axis_size("expert")
    square_and_line = lax.axis_size("dp") == 4 and experts == 8
    if square_and_line and capacity_of(tok_dev, top_count, experts) == tok_dev:
        return dense_plan(tokens, expert_ids, *rest)
    return slot_plan(tokens, expert_ids, *rest)


def solution(mesh):
    by_token = P(AXES, None)
    by_expert = P("expert", "dp", None)
    return jax.shard_map(
        on_device,
        mesh=mesh,
        in_specs=(by_token,) * 4 + (by_expert,) * 3,
        out_specs=(by_token,) * 3 + (by_expert,) * 3,
        check_vma=False,
    )
```

```python
import jax
import jax.numpy as jnp
from jax import lax
from jax.experimental import pallas as pl
from jax.experimental.pallas import tpu as pltpu
from jax.sharding import PartitionSpec as P

AXES = ("dp", "expert")
ACROSS = (((1,), (1,)), ((), ()))
OVER_ROWS = (((0,), (0,)), ((), ()))


def routing_slots(expert_ids, experts):
    onehot = (expert_ids[:, :, None] == jnp.arange(experts, dtype=jnp.int32)[None, None, :]).astype(
        jnp.int32
    )
    per_token = jnp.sum(onehot, axis=1)
    earlier = jnp.cumsum(per_token, axis=0) - per_token
    return jnp.sum(onehot * earlier[:, None, :], axis=2)


def forward_rows(rows, gate_proj, up_proj, down_proj):
    gate_pre = jnp.dot(rows, gate_proj, preferred_element_type=jnp.float32)
    up_pre = jnp.dot(rows, up_proj, preferred_element_type=jnp.float32)
    hidden = (jax.nn.silu(gate_pre) * up_pre).astype(jnp.bfloat16)
    expert_out = lax.dot_general(
        hidden, down_proj, ACROSS, preferred_element_type=jnp.float32
    ).astype(jnp.bfloat16)
    return (expert_out, gate_pre, up_pre, hidden)


def backward_rows(grad_rows, gate_pre, up_pre, gate_proj, up_proj, down_proj):
    d_hidden = jnp.dot(grad_rows, down_proj, preferred_element_type=jnp.float32)
    sigmoid_gate = jax.nn.sigmoid(gate_pre)
    silu_gate = gate_pre * sigmoid_gate
    d_gate = (d_hidden * up_pre * sigmoid_gate * (1.0 + gate_pre * (1.0 - sigmoid_gate))).astype(
        jnp.bfloat16
    )
    d_up = (d_hidden * silu_gate).astype(jnp.bfloat16)
    d_rows = lax.dot_general(d_gate, gate_proj, ACROSS, preferred_element_type=jnp.float32)
    d_rows = d_rows + lax.dot_general(d_up, up_proj, ACROSS, preferred_element_type=jnp.float32)
    return (d_rows.astype(jnp.bfloat16), d_gate, d_up)


def pick_rows(source_rows, position, top_count):
    chosen = jnp.take(source_rows, position.reshape(-1), axis=0)
    return chosen.reshape(position.shape[0], top_count, source_rows.shape[1])


def capacity_of(tok_dev, top_count, experts):
    return min(tok_dev, (tok_dev * top_count * 4 + 3 * experts - 1) // (3 * experts))


def slot_plan(tokens, expert_ids, gate_probs, cotangent, gate_proj, up_proj, down_proj):
    experts = lax.axis_size("expert")
    tok_dev, top_count = expert_ids.shape
    model_width = tokens.shape[1]
    capacity = capacity_of(tok_dev, top_count, experts)
    slot_index = routing_slots(expert_ids, experts)
    position = expert_ids * capacity + slot_index
    placing = (
        position[None, :, :] == jnp.arange(experts * capacity, dtype=jnp.int32)[:, None, None]
    ).astype(jnp.float32)
    placer = jnp.sum(placing, axis=2)
    weighted = jnp.sum(placing * gate_probs[None, :, :], axis=2)
    row_send = (
        jnp.dot(placer.astype(jnp.bfloat16), tokens, preferred_element_type=jnp.float32)
        .astype(jnp.bfloat16)
        .reshape(experts, capacity, model_width)
    )
    grad_send = (
        jnp.dot(weighted, cotangent.astype(jnp.float32), precision=lax.Precision.HIGHEST)
        .astype(jnp.bfloat16)
        .reshape(experts, capacity, model_width)
    )
    full_gate, full_up, full_down = (
        lax.all_gather(gate_proj[0], "dp", axis=0, tiled=True),
        lax.all_gather(up_proj[0], "dp", axis=0, tiled=True),
        lax.all_gather(down_proj[0], "dp", axis=0, tiled=True),
    )

    def exchange(rows):
        return lax.all_to_all(
            rows.reshape(experts, capacity, model_width),
            "expert",
            split_axis=0,
            concat_axis=0,
            tiled=True,
        ).reshape(-1, model_width)

    rows_flat = exchange(row_send)
    expert_out, gate_pre, up_pre, hidden = forward_rows(rows_flat, full_gate, full_up, full_down)
    returned = exchange(expert_out)
    grads_flat = exchange(grad_send)
    d_rows, d_gate, d_up = backward_rows(
        grads_flat, gate_pre, up_pre, full_gate, full_up, full_down
    )
    grad_back = exchange(d_rows)
    picked = pick_rows(returned, position, top_count).astype(jnp.float32)
    mixed = jnp.sum(gate_probs[:, :, None] * picked, axis=1).astype(jnp.bfloat16)
    prob_grads = jnp.sum(cotangent.astype(jnp.float32)[:, None, :] * picked, axis=2)
    picked_grads = pick_rows(grad_back, position, top_count).astype(jnp.float32)
    token_grads = jnp.sum(picked_grads, axis=1).astype(jnp.bfloat16)
    hidden_units = hidden.shape[1]
    gate_term = lax.dot_general(rows_flat, d_gate, OVER_ROWS, preferred_element_type=jnp.float32)
    up_term = lax.dot_general(rows_flat, d_up, OVER_ROWS, preferred_element_type=jnp.float32)
    down_term = lax.dot_general(grads_flat, hidden, OVER_ROWS, preferred_element_type=jnp.float32)
    shares = lax.psum_scatter(
        jnp.concatenate([gate_term, up_term, down_term], axis=1),
        "dp",
        scatter_dimension=0,
        tiled=True,
    )
    grad_gate = shares[:, :hidden_units]
    grad_up = shares[:, hidden_units : 2 * hidden_units]
    grad_down = shares[:, 2 * hidden_units :]
    return (mixed, token_grads, prob_grads, grad_gate[None], grad_up[None], grad_down[None])


TILE = 256
SIDE = 128
F32 = jnp.float32
BF16 = jnp.bfloat16
VMEM = pl.BlockSpec(memory_space=pltpu.VMEM)


RING = (0, 2, 3, 1)


def flat_index(y, x, z, core):
    return ((y * 2 + x) * 4 + z) * 2 + core


def pairs(target):
    return [
        (flat_index(y, x, z, core), flat_index(*target(y, x, z, core)))
        for y in range(2)
        for x in range(2)
        for z in range(4)
        for core in range(2)
    ]


TO_X = pairs(lambda y, x, z, core: (y, 1 - x, z, core))
TO_Y = pairs(lambda y, x, z, core: (1 - y, x, z, core))
TO_CORE = pairs(lambda y, x, z, core: (y, x, z, 1 - core))
ALONG_Z = pairs(lambda y, x, z, core: (y, x, RING[(RING.index(z) + 1) % 4], core))


def send(array, where):
    return lax.ppermute(array, AXES, where)


def kernel_call(body, out_shape, **spec):
    return pl.pallas_call(
        body,
        out_shape=out_shape,
        compiler_params=pltpu.CompilerParams(vmem_limit_bytes=24 * 1024 * 1024),
        cost_estimate=pl.CostEstimate(flops=0, bytes_accessed=0, transcendentals=0),
        **spec,
    )


def shape(rows, columns, dtype):
    return jax.ShapeDtypeStruct((rows, columns), dtype)


def iota(rows, columns, axis):
    return lax.broadcasted_iota(jnp.int32, (rows, columns), axis)


def exact_parts(values, place):
    first = values.astype(BF16).astype(F32)
    rest = values - first
    second = rest.astype(BF16).astype(F32)
    third = rest - second
    parts = jnp.where(place < 8, first, jnp.where(place < 16, second, third))
    return jnp.where(place < 24, parts, 0.0).astype(BF16)


def block_at(relative, block):
    return pl.ds(pl.multiple_of((lax.axis_index("dp") ^ relative) * block, block), block)


def pack_kernel(tokens_ref, cot_ref, ids_ref, probs_ref, out_ref):
    rows, width = tokens_ref.shape
    block = width // 4
    for r in range(4):
        there = block_at(r, block)
        out_ref[:, r * block : (r + 1) * block] = tokens_ref[:, there]
        out_ref[:, width + r * block : width + (r + 1) * block] = cot_ref[:, there]
    place = iota(SIDE, rows, 0)
    prob = jnp.zeros((SIDE, rows), F32)
    for k in range(ids_ref.shape[0]):
        prob += jnp.where(place % 8 == ids_ref[k : k + 1, :], probs_ref[k : k + 1, :], 0.0)
    same = (iota(rows, rows, 0) == iota(rows, rows, 1)).astype(BF16)
    turned = lax.dot_general(same, exact_parts(prob, place), ACROSS, preferred_element_type=F32)
    out_ref[:, 2 * width :] = turned.astype(BF16)


def pack(tokens, cotangent, expert_ids, gate_probs):
    rows, width = tokens.shape
    return kernel_call(
        pack_kernel,
        shape(rows, 2 * width + SIDE, BF16),
        in_specs=[VMEM] * 4,
        out_specs=VMEM,
    )(tokens, cotangent, expert_ids.T, gate_probs.T)


def unpack_kernel(sums_ref, ids_ref, mixed_out, back_out, prob_out):
    rows, width = mixed_out.shape
    block = width // 4
    for r in range(4):
        there = block_at(r, block)
        mixed_out[:, there] = sums_ref[:, r * block : (r + 1) * block]
        back_out[:, there] = sums_ref[:, width + r * block : width + (r + 1) * block]
    lane = iota(8, SIDE, 1)
    adder = ((lane < 24) & (lane % 8 == iota(8, SIDE, 0))).astype(BF16)
    by_expert = lax.dot_general(adder, sums_ref[:, 2 * width :], ACROSS, preferred_element_type=F32)
    for k in range(ids_ref.shape[0]):
        hit = iota(8, rows, 0) == ids_ref[k : k + 1, :]
        prob_out[k : k + 1, :] = jnp.sum(jnp.where(hit, by_expert, 0.0), axis=0, keepdims=True)


def unpack(sums, expert_ids, width):
    own = shape(sums.shape[0], width, BF16)
    mixed, back, prob = kernel_call(
        unpack_kernel,
        (own, own, shape(*expert_ids.T.shape, F32)),
        in_specs=[VMEM] * 2,
        out_specs=(VMEM,) * 3,
    )(sums, expert_ids.T)
    return mixed, back, prob.T


def turn_kernel(own_ref, other_ref, out_ref):
    rows = own_ref.shape[0]
    out_ref[:, :rows] = own_ref[...].T
    out_ref[:, rows:] = other_ref[...].T


def turn(whole, width):
    rows = whole[0].shape[0]
    return kernel_call(
        turn_kernel,
        shape(width, 2 * rows, BF16),
        grid=(width // TILE,),
        in_specs=[pl.BlockSpec((rows, TILE), lambda i: (0, i))] * 2,
        out_specs=pl.BlockSpec((TILE, 2 * rows), lambda i: (i, 0)),
    )(*whole)


def times_pieces(rows_ref, pieces):
    total, start = None, 0
    for piece in pieces:
        depth = piece.shape[0]
        term = jnp.dot(rows_ref[:, start : start + depth], piece[...], preferred_element_type=F32)
        total = term if total is None else total + term
        start += depth
    return total


def early_kernel(own_rows, other_rows, own_ref, x_ref, y_ref, out_ref):
    half = own_rows.shape[0]
    out_ref[:half] = times_pieces(own_rows, (own_ref, x_ref, y_ref))
    out_ref[half:] = times_pieces(other_rows, (own_ref, x_ref, y_ref))


def early_products(whole, direct, width, which, start, columns):
    half = whole[0].shape[0]
    piece = pl.BlockSpec((direct[0].shape[0], TILE), lambda j: (0, start // TILE + j))
    return kernel_call(
        early_kernel,
        shape(2 * half, columns, F32),
        grid=(columns // TILE,),
        in_specs=[pl.BlockSpec((half, width), lambda j: (0, which))] * 2 + [piece] * 3,
        out_specs=pl.BlockSpec((2 * half, TILE), lambda j: (0, j)),
    )(*whole, *direct)


def forward_kernel(*refs):
    both_rows, both_parts, earlies, gates, ups = (refs[i : i + 2] for i in range(0, 10, 2))
    scaled_ref, for_gate_ref, for_up_ref, hidden_ref = refs[10:]
    half = both_rows[0].shape[0]
    for index in range(2):
        at = slice(index * half, (index + 1) * half)
        gate_pre = earlies[0][at] + times_pieces(both_rows[index], gates)
        up_pre = earlies[1][at] + times_pieces(both_rows[index], ups)
        lane = iota(half, SIDE, 1)
        mine = (lane < 24) & (lane % 8 == lax.axis_index("expert"))
        parts = both_parts[index][...].astype(F32)
        prob = jnp.sum(jnp.where(mine, parts, 0.0), axis=1, keepdims=True)
        sigmoid_gate = 1.0 / (1.0 + jnp.exp(-gate_pre))
        silu_gate = gate_pre * sigmoid_gate
        hidden = silu_gate * up_pre
        hidden_ref[at] = hidden
        scaled_ref[at] = (hidden * prob).astype(BF16)
        slope = sigmoid_gate * (1.0 + gate_pre * (1.0 - sigmoid_gate))
        for_gate_ref[at] = prob * (up_pre * slope)
        for_up_ref[at] = prob * silu_gate


def forward(whole, early, corner, width, units):
    half = whole[0].shape[0]
    rows = 2 * half
    steps = units // TILE
    block = width // 4
    tile = pl.BlockSpec((rows, TILE), lambda j: (0, j))
    next_tile = pl.BlockSpec((rows, TILE), lambda j: (0, steps + j))
    return kernel_call(
        forward_kernel,
        (shape(rows, units, BF16),) + (shape(rows, units, F32),) * 3,
        grid=(steps,),
        in_specs=[pl.BlockSpec((half, block), lambda j: (0, 3))] * 2
        + [pl.BlockSpec((half, SIDE), lambda j: (0, 2 * width // SIDE))] * 2
        + [tile, next_tile]
        + [pl.BlockSpec((block // 2, TILE), lambda j: (0, j))] * 2
        + [pl.BlockSpec((block // 2, TILE), lambda j: (0, steps + j))] * 2,
        out_specs=(tile,) * 4,
    )(*whole, *whole, early, early, *corner, *corner)


def backward_kernel(own_ref, other_ref, early_ref, first_ref, last_ref, *refs):
    for_gate_ref, for_up_ref, hidden_ref, d_gate_ref, d_up_ref, dots_ref, sum_ref = refs
    step = pl.program_id(0)
    half = own_ref.shape[0]

    @pl.when(step == 0)
    def _():
        sum_ref[...] = jnp.zeros_like(sum_ref)

    for index, grads_ref in enumerate((own_ref, other_ref)):
        at = slice(index * half, (index + 1) * half)
        raw = early_ref[at] + times_pieces(grads_ref, (first_ref, last_ref))
        d_gate_ref[at] = (raw * for_gate_ref[at]).astype(BF16)
        d_up_ref[at] = (raw * for_up_ref[at]).astype(BF16)
        sum_ref[at] += jnp.sum(raw * hidden_ref[at], axis=1, keepdims=True)

    @pl.when(step == pl.num_programs(0) - 1)
    def _():
        lane = iota(2 * half, SIDE, 1)
        mine = lane % 8 == lax.axis_index("expert")
        dots_ref[...] = exact_parts(jnp.where(mine, sum_ref[...], 0.0), lane)


def backward(whole, early, corner, for_gate, for_up, hidden, width):
    rows, units = hidden.shape
    steps = units // TILE
    block = width // 4
    tile = pl.BlockSpec((rows, TILE), lambda j: (0, j))
    return kernel_call(
        backward_kernel,
        (shape(rows, units, BF16),) * 2 + (shape(rows, SIDE, BF16),),
        grid=(steps,),
        in_specs=[pl.BlockSpec((rows // 2, block), lambda j: (0, 7))] * 2
        + [tile]
        + [pl.BlockSpec((block // 2, TILE), lambda j: (0, j))] * 2
        + [tile] * 3,
        out_specs=(tile, tile, pl.BlockSpec((rows, SIDE), lambda j: (0, 0))),
        scratch_shapes=[pltpu.VMEM((rows, 1), F32)],
    )(*whole, early, *corner, for_gate, for_up, hidden)


def first_half_blocks(i):
    return jnp.where(i == 3, 4, 7 - 4 * (i % 2) - i // 2)


def later_half_blocks(i):
    return jnp.where(i < 2, 2 + 3 * i, i - 2)


def first_grad_kernel(turned_ref, term_ref, to_x, to_y):
    step = pl.program_id(0)
    part = jnp.dot(turned_ref[...], term_ref[...], preferred_element_type=F32).astype(BF16)

    @pl.when(step < 2)
    def _():
        to_x[...] = part

    @pl.when(step >= 2)
    def _():
        to_y[...] = part


def later_grad_kernel(turned_ref, term_ref, for_x, for_y, own):
    step = pl.program_id(0)
    part = jnp.dot(turned_ref[...], term_ref[...], preferred_element_type=F32)

    @pl.when(step == 0)
    def _():
        for_x[...] = part

    @pl.when(step == 1)
    def _():
        for_y[...] = part

    @pl.when(step >= 2)
    def _():
        own[...] = part


def first_grads(turned, first, width, term):
    rows, units = term.shape
    half = width // 8

    def at(start):
        return pl.BlockSpec((half, units), lambda i: (jnp.clip(i - start, 0, 1), 0))

    return kernel_call(
        first_grad_kernel,
        (shape(2 * half, units, BF16),) * 2,
        grid=(4,),
        in_specs=[
            pl.BlockSpec((half, rows), lambda i: (first + first_half_blocks(i), 0)),
            pl.BlockSpec((rows, units), lambda i: (0, 0)),
        ],
        out_specs=(at(0), at(2)),
    )(turned, term)


def later_grads(turned, first, width, term):
    rows, units = term.shape
    half = width // 8
    once = pl.BlockSpec((half, units), lambda i: (0, 0))
    return kernel_call(
        later_grad_kernel,
        (shape(half, units, F32),) * 2 + (shape(2 * half, units, F32),),
        grid=(4,),
        in_specs=[
            pl.BlockSpec((half, rows), lambda i: (first + later_half_blocks(i), 0)),
            pl.BlockSpec((rows, units), lambda i: (0, 0)),
        ],
        out_specs=(
            once,
            once,
            pl.BlockSpec((half, units), lambda i: (jnp.clip(i - 2, 0, 1), 0)),
        ),
    )(turned, term)


def back_kernel(scaled_ref, d_gate_ref, d_up_ref, dots_ref, *refs):
    downs, gate_ups, out_ref = refs[:5], refs[5:10], refs[10]
    units = scaled_ref.shape[1]
    width = (out_ref.shape[1] - SIDE) // 2

    def product(term, weight):
        return lax.dot_general(term[...], weight, ACROSS, preferred_element_type=F32)

    start = 0
    for down, gate_up in zip(downs, gate_ups):
        depth = down.shape[0]
        out_ref[:, start : start + depth] = product(scaled_ref, down[...]).astype(BF16)
        total = product(d_gate_ref, gate_up[:, :units]) + product(d_up_ref, gate_up[:, units:])
        out_ref[:, width + start : width + start + depth] = total.astype(BF16)
        start += depth
    out_ref[:, 2 * width :] = dots_ref[...]


def back_to_rows(scaled, d_gate, d_up, dots, direct, down, gate_up, width):
    rows, units = scaled.shape
    depth = direct[0].shape[0]
    term = pl.BlockSpec((TILE, units), lambda i: (i, 0))
    corner = [pl.BlockSpec((depth // 2, n * units), lambda i: (0, 0)) for n in (1, 1, 2, 2)]
    return kernel_call(
        back_kernel,
        shape(rows, 2 * width + SIDE, BF16),
        grid=(rows // TILE,),
        in_specs=[term] * 3
        + [pl.BlockSpec((TILE, SIDE), lambda i: (i, 0))]
        + [pl.BlockSpec((depth, units), lambda i: (0, 2))] * 3
        + corner[:2]
        + [pl.BlockSpec((depth, 2 * units), lambda i: (0, 0))] * 3
        + corner[2:],
        out_specs=pl.BlockSpec((TILE, 2 * width + SIDE), lambda i: (i, 0)),
    )(scaled, d_gate, d_up, dots, *direct, *down, *direct, *gate_up)


def total_kernel(own_ref, from_x, from_y, late_x, late_y, out_ref):
    out_ref[0] = own_ref[0] + (from_y[0].astype(F32) + late_x[...].astype(F32))
    out_ref[1] = own_ref[1] + (from_x[0].astype(F32) + late_y[...].astype(F32))


def total(own, from_x, from_y, late_x, late_y):
    block, units = own.shape
    half = block // 2
    step = half // 4
    both = pl.BlockSpec((2, step, units), lambda i: (0, i, 0))
    low = pl.BlockSpec((1, step, units), lambda i: (1, i, 0))
    late = pl.BlockSpec((step, units), lambda i: (i, 0))
    halves = (2, half, units)
    return kernel_call(
        total_kernel,
        jax.ShapeDtypeStruct(halves, F32),
        grid=(half // step,),
        in_specs=[both, low, low, late, late],
        out_specs=both,
    )(own.reshape(halves), from_x.reshape(halves), from_y.reshape(halves), late_x, late_y).reshape(
        1, block, units
    )


def send_corner(from_x, from_y, columns):
    half = from_x.shape[0] // 2
    return [send(from_x[:half, columns], TO_Y), send(from_y[half:, columns], TO_X)]


def send_first(to_x, to_y):
    return send(to_x, TO_X), send(to_y, TO_Y)


def send_later(for_x, for_y, from_x, from_y):
    half = for_x.shape[0]
    late_x = send((for_x + from_y[:half].astype(F32)).astype(BF16), TO_X)
    late_y = send((for_y + from_x[:half].astype(F32)).astype(BF16), TO_Y)
    return late_x, late_y


def gather_rows(own, before):
    slots = [own]
    for _ in range(3):
        slots.append(send(slots[-1], ALONG_Z))
    own_core = after(jnp.concatenate(slots), before)
    return own_core, send(own_core, TO_CORE)


def sum_over_experts(rows, before):
    half = rows.shape[0] // 2
    block = half // 4
    arrived = send(after(rows[half:], before), TO_CORE)

    def both_cores(slot):
        at = slice(slot * block, (slot + 1) * block)
        return rows[at].astype(F32) + arrived[at].astype(F32)

    steps = [both_cores(1).astype(BF16)]
    for slot in (2, 3, 0):
        moving = send(steps[-1], ALONG_Z)
        steps.append((both_cores(slot) + moving.astype(F32)).astype(BF16))
    return steps


def after(arrays, *others):
    return lax.optimization_barrier((arrays, others))[0]


def dense_plan(tokens, expert_ids, gate_probs, cotangent, gate_proj, up_proj, down_proj):
    width = tokens.shape[1]
    units = gate_proj.shape[2]
    halves = width // TILE

    shard = jnp.concatenate([gate_proj[0], up_proj[0], down_proj[0]], axis=1)
    direct = [shard, send(shard, TO_X), send(shard, TO_Y)]
    whole = gather_rows(pack(tokens, cotangent, expert_ids, gate_probs), direct)
    gate_up_corner = send_corner(*direct[1:], slice(0, 2 * units))
    down_corner = send_corner(*direct[1:], slice(2 * units, 3 * units))
    early_gate_up = early_products(whole, direct, width, 0, 0, 2 * units)
    turned = turn(whole, 2 * width)
    early_down = early_products(whole, direct, width, 1, 2 * units, units)
    early_gate_up, early_down, turned, gate_up_corner = lax.optimization_barrier(
        (early_gate_up, early_down, turned, gate_up_corner)
    )

    scaled, for_gate, for_up, hidden = forward(whole, early_gate_up, gate_up_corner, width, units)
    down_sent = first_grads(turned, halves, width, scaled)
    down_first = send_first(*after(down_sent, down_corner))
    scaled, whole, hidden = after((scaled, whole, hidden), down_sent)
    *down_later, down_own = later_grads(turned, halves, width, scaled)
    hidden = after(hidden, down_own)
    d_gate, d_up, dots = backward(
        whole, early_down, down_corner, for_gate, for_up, hidden, width
    )
    gate_sent = first_grads(turned, 0, width, d_gate)
    gate_first = send_first(*gate_sent)
    d_gate, d_up = after((d_gate, d_up), gate_sent)
    up_sent = first_grads(turned, 0, width, d_up)
    shares = back_to_rows(scaled, d_gate, d_up, dots, direct, down_corner, gate_up_corner, width)
    steps = sum_over_experts(shares, down_first)
    d_gate, d_up = after((d_gate, d_up), shares)
    *gate_later, gate_own = later_grads(turned, 0, width, d_gate)
    *up_later, up_own = later_grads(turned, 0, width, d_up)

    up_first = send_first(*after(up_sent, down_first))
    down_later = after(down_later, gate_first, steps[0])
    down_late = send_later(*down_later, *down_first)
    gate_later = after(gate_later, up_first, steps[1])
    gate_late = send_later(*gate_later, *gate_first)
    grad_down = total(down_own, *down_first, *down_late)
    up_later = after(up_later, grad_down, steps[2])
    up_late = send_later(*up_later, *up_first)
    outs = unpack(steps[3], expert_ids, width)
    grad_gate = total(gate_own, *gate_first, *gate_late)
    up_late = after(up_late, grad_gate, outs)
    grad_up = total(up_own, *up_first, *up_late)
    return (*outs, grad_gate, grad_up, grad_down)


def on_device(tokens, expert_ids, *rest):
    tok_dev, top_count = expert_ids.shape
    experts = lax.axis_size("expert")
    square_and_line = lax.axis_size("dp") == 4 and experts == 8
    if square_and_line and capacity_of(tok_dev, top_count, experts) == tok_dev:
        return dense_plan(tokens, expert_ids, *rest)
    return slot_plan(tokens, expert_ids, *rest)


def solution(mesh):
    by_token = P(AXES, None)
    by_expert = P("expert", "dp", None)
    return jax.shard_map(
        on_device,
        mesh=mesh,
        in_specs=(by_token,) * 4 + (by_expert,) * 3,
        out_specs=(by_token,) * 3 + (by_expert,) * 3,
        check_vma=False,
    )
```

```python
import jax
import jax.numpy as jnp
from jax import lax
from jax.experimental import pallas as pl
from jax.experimental.pallas import tpu as pltpu
from jax.sharding import PartitionSpec as P

AXES = ("dp", "expert")
ACROSS = (((1,), (1,)), ((), ()))
OVER_ROWS = (((0,), (0,)), ((), ()))


def routing_slots(expert_ids, experts):
    onehot = (expert_ids[:, :, None] == jnp.arange(experts, dtype=jnp.int32)[None, None, :]).astype(
        jnp.int32
    )
    per_token = jnp.sum(onehot, axis=1)
    earlier = jnp.cumsum(per_token, axis=0) - per_token
    return jnp.sum(onehot * earlier[:, None, :], axis=2)


def forward_rows(rows, gate_proj, up_proj, down_proj):
    gate_pre = jnp.dot(rows, gate_proj, preferred_element_type=jnp.float32)
    up_pre = jnp.dot(rows, up_proj, preferred_element_type=jnp.float32)
    hidden = (jax.nn.silu(gate_pre) * up_pre).astype(jnp.bfloat16)
    expert_out = lax.dot_general(
        hidden, down_proj, ACROSS, preferred_element_type=jnp.float32
    ).astype(jnp.bfloat16)
    return (expert_out, gate_pre, up_pre, hidden)


def backward_rows(grad_rows, gate_pre, up_pre, gate_proj, up_proj, down_proj):
    d_hidden = jnp.dot(grad_rows, down_proj, preferred_element_type=jnp.float32)
    sigmoid_gate = jax.nn.sigmoid(gate_pre)
    silu_gate = gate_pre * sigmoid_gate
    d_gate = (d_hidden * up_pre * sigmoid_gate * (1.0 + gate_pre * (1.0 - sigmoid_gate))).astype(
        jnp.bfloat16
    )
    d_up = (d_hidden * silu_gate).astype(jnp.bfloat16)
    d_rows = lax.dot_general(d_gate, gate_proj, ACROSS, preferred_element_type=jnp.float32)
    d_rows = d_rows + lax.dot_general(d_up, up_proj, ACROSS, preferred_element_type=jnp.float32)
    return (d_rows.astype(jnp.bfloat16), d_gate, d_up)


def pick_rows(source_rows, position, top_count):
    chosen = jnp.take(source_rows, position.reshape(-1), axis=0)
    return chosen.reshape(position.shape[0], top_count, source_rows.shape[1])


def capacity_of(tok_dev, top_count, experts):
    return min(tok_dev, (tok_dev * top_count * 4 + 3 * experts - 1) // (3 * experts))


def slot_plan(tokens, expert_ids, gate_probs, cotangent, gate_proj, up_proj, down_proj):
    experts = lax.axis_size("expert")
    tok_dev, top_count = expert_ids.shape
    model_width = tokens.shape[1]
    capacity = capacity_of(tok_dev, top_count, experts)
    slot_index = routing_slots(expert_ids, experts)
    position = expert_ids * capacity + slot_index
    placing = (
        position[None, :, :] == jnp.arange(experts * capacity, dtype=jnp.int32)[:, None, None]
    ).astype(jnp.float32)
    placer = jnp.sum(placing, axis=2)
    weighted = jnp.sum(placing * gate_probs[None, :, :], axis=2)
    row_send = (
        jnp.dot(placer.astype(jnp.bfloat16), tokens, preferred_element_type=jnp.float32)
        .astype(jnp.bfloat16)
        .reshape(experts, capacity, model_width)
    )
    grad_send = (
        jnp.dot(weighted, cotangent.astype(jnp.float32), precision=lax.Precision.HIGHEST)
        .astype(jnp.bfloat16)
        .reshape(experts, capacity, model_width)
    )
    full_gate, full_up, full_down = (
        lax.all_gather(gate_proj[0], "dp", axis=0, tiled=True),
        lax.all_gather(up_proj[0], "dp", axis=0, tiled=True),
        lax.all_gather(down_proj[0], "dp", axis=0, tiled=True),
    )

    def exchange(rows):
        return lax.all_to_all(
            rows.reshape(experts, capacity, model_width),
            "expert",
            split_axis=0,
            concat_axis=0,
            tiled=True,
        ).reshape(-1, model_width)

    rows_flat = exchange(row_send)
    expert_out, gate_pre, up_pre, hidden = forward_rows(rows_flat, full_gate, full_up, full_down)
    returned = exchange(expert_out)
    grads_flat = exchange(grad_send)
    d_rows, d_gate, d_up = backward_rows(
        grads_flat, gate_pre, up_pre, full_gate, full_up, full_down
    )
    grad_back = exchange(d_rows)
    picked = pick_rows(returned, position, top_count).astype(jnp.float32)
    mixed = jnp.sum(gate_probs[:, :, None] * picked, axis=1).astype(jnp.bfloat16)
    prob_grads = jnp.sum(cotangent.astype(jnp.float32)[:, None, :] * picked, axis=2)
    picked_grads = pick_rows(grad_back, position, top_count).astype(jnp.float32)
    token_grads = jnp.sum(picked_grads, axis=1).astype(jnp.bfloat16)
    hidden_units = hidden.shape[1]
    gate_term = lax.dot_general(rows_flat, d_gate, OVER_ROWS, preferred_element_type=jnp.float32)
    up_term = lax.dot_general(rows_flat, d_up, OVER_ROWS, preferred_element_type=jnp.float32)
    down_term = lax.dot_general(grads_flat, hidden, OVER_ROWS, preferred_element_type=jnp.float32)
    shares = lax.psum_scatter(
        jnp.concatenate([gate_term, up_term, down_term], axis=1),
        "dp",
        scatter_dimension=0,
        tiled=True,
    )
    grad_gate = shares[:, :hidden_units]
    grad_up = shares[:, hidden_units : 2 * hidden_units]
    grad_down = shares[:, 2 * hidden_units :]
    return (mixed, token_grads, prob_grads, grad_gate[None], grad_up[None], grad_down[None])


TILE = 256
SIDE = 128
F32 = jnp.float32
BF16 = jnp.bfloat16
VMEM = pl.BlockSpec(memory_space=pltpu.VMEM)


RING = (0, 2, 3, 1)


def flat_index(y, x, z, core):
    return ((y * 2 + x) * 4 + z) * 2 + core


def pairs(target):
    return [
        (flat_index(y, x, z, core), flat_index(*target(y, x, z, core)))
        for y in range(2)
        for x in range(2)
        for z in range(4)
        for core in range(2)
    ]


TO_X = pairs(lambda y, x, z, core: (y, 1 - x, z, core))
TO_Y = pairs(lambda y, x, z, core: (1 - y, x, z, core))
TO_CORE = pairs(lambda y, x, z, core: (y, x, z, 1 - core))
ALONG_Z = pairs(lambda y, x, z, core: (y, x, RING[(RING.index(z) + 1) % 4], core))


def send(array, where):
    return lax.ppermute(array, AXES, where)


def kernel_call(body, out_shape, **spec):
    return pl.pallas_call(
        body,
        out_shape=out_shape,
        compiler_params=pltpu.CompilerParams(vmem_limit_bytes=24 * 1024 * 1024),
        cost_estimate=pl.CostEstimate(flops=0, bytes_accessed=0, transcendentals=0),
        **spec,
    )


def shape(rows, columns, dtype):
    return jax.ShapeDtypeStruct((rows, columns), dtype)


def iota(rows, columns, axis):
    return lax.broadcasted_iota(jnp.int32, (rows, columns), axis)


def exact_parts(values, place):
    first = values.astype(BF16).astype(F32)
    rest = values - first
    second = rest.astype(BF16).astype(F32)
    third = rest - second
    parts = jnp.where(place < 8, first, jnp.where(place < 16, second, third))
    return jnp.where(place < 24, parts, 0.0).astype(BF16)


def block_at(relative, block):
    return pl.ds(pl.multiple_of((lax.axis_index("dp") ^ relative) * block, block), block)


def pack_kernel(tokens_ref, cot_ref, ids_ref, probs_ref, out_ref):
    rows, width = tokens_ref.shape
    block = width // 4
    for r in range(4):
        there = block_at(r, block)
        out_ref[:, r * block : (r + 1) * block] = tokens_ref[:, there]
        out_ref[:, width + r * block : width + (r + 1) * block] = cot_ref[:, there]
    place = iota(SIDE, rows, 0)
    prob = jnp.zeros((SIDE, rows), F32)
    for k in range(ids_ref.shape[0]):
        prob += jnp.where(place % 8 == ids_ref[k : k + 1, :], probs_ref[k : k + 1, :], 0.0)
    same = (iota(rows, rows, 0) == iota(rows, rows, 1)).astype(BF16)
    turned = lax.dot_general(same, exact_parts(prob, place), ACROSS, preferred_element_type=F32)
    out_ref[:, 2 * width :] = turned.astype(BF16)


def pack(tokens, cotangent, expert_ids, gate_probs):
    rows, width = tokens.shape
    return kernel_call(
        pack_kernel,
        shape(rows, 2 * width + SIDE, BF16),
        in_specs=[VMEM] * 4,
        out_specs=VMEM,
    )(tokens, cotangent, expert_ids.T, gate_probs.T)


def weights_and_rows(weights, tokens, blocks):
    rows, width = tokens.shape
    dp = lax.axis_index("dp")
    columns = jnp.split(tokens, 4, axis=1)
    wanted = jnp.concatenate([lax.select_n(dp ^ r, *columns) for r in blocks], axis=1)
    wanted = jnp.concatenate([wanted[: rows // 2], wanted[rows // 2 :]], axis=1)
    weights = jnp.concatenate(weights, axis=1)
    spare = weights.shape[1] - width
    return jnp.concatenate([weights, jnp.pad(wanted, ((0, 0), (0, spare)))], axis=0)


def side_rows(arrived, depth, width):
    sides = arrived[depth:]
    return jnp.concatenate([sides[:, : width // 2], sides[:, width // 2 : width]])


def unpack_kernel(own_ref, core_ref, line_ref, ids_ref, mixed_out, back_out, prob_out):
    rows, width = mixed_out.shape
    block = width // 4

    def total(at):
        return own_ref[:, at].astype(F32) + core_ref[:, at].astype(F32) + line_ref[:, at].astype(F32)

    for r in range(4):
        there = block_at(r, block)
        start = r * block
        mixed_out[:, there] = total(slice(start, start + block)).astype(BF16)
        start += width
        back_out[:, there] = total(slice(start, start + block)).astype(BF16)
    lane = iota(8, SIDE, 1)
    adder = ((lane < 24) & (lane % 8 == iota(8, SIDE, 0))).astype(BF16)
    parts = total(slice(2 * width, 2 * width + SIDE)).astype(BF16)
    by_expert = lax.dot_general(adder, parts, ACROSS, preferred_element_type=F32)
    for k in range(ids_ref.shape[0]):
        hit = iota(8, rows, 0) == ids_ref[k : k + 1, :]
        prob_out[k : k + 1, :] = jnp.sum(jnp.where(hit, by_expert, 0.0), axis=0, keepdims=True)


def unpack(shares, arrived, line, expert_ids, width):
    rows, columns = line.shape
    own = shape(rows, width, BF16)
    ids = expert_ids.T
    first = pl.BlockSpec((rows, columns), lambda i: (0, 0))
    wide = pl.BlockSpec((rows, width), lambda i: (0, 0))
    small = pl.BlockSpec(ids.shape, lambda i: (0, 0))
    mixed, back, prob = kernel_call(
        unpack_kernel,
        (own, own, shape(*ids.shape, F32)),
        grid=(1,),
        in_specs=[first] * 3 + [small],
        out_specs=(wide, wide, small),
    )(shares, arrived, line, ids)
    return mixed, back, prob.T


def turn_kernel(own_ref, other_ref, out_ref):
    rows = own_ref.shape[0]
    out_ref[:, :rows] = own_ref[...].T
    out_ref[:, rows:] = other_ref[...].T


def turn(both, tiles, place_of):
    rows = both[0].shape[0]
    return kernel_call(
        turn_kernel,
        shape(tiles * TILE, 2 * rows, BF16),
        grid=(tiles,),
        in_specs=[pl.BlockSpec((rows, TILE), lambda i: (0, place_of(i)))] * 2,
        out_specs=pl.BlockSpec((TILE, 2 * rows), lambda i: (i, 0)),
    )(*both)


def times_pieces(rows_ref, pieces):
    total, start = None, 0
    for piece in pieces:
        depth = piece.shape[0]
        term = jnp.dot(rows_ref[:, start : start + depth], piece[...], preferred_element_type=F32)
        total = term if total is None else total + term
        start += depth
    return total


def early_kernel(own_rows, other_rows, own_ref, x_ref, y_ref, out_ref):
    half = own_rows.shape[0]
    out_ref[:half] = times_pieces(own_rows, (own_ref, x_ref, y_ref))
    out_ref[half:] = times_pieces(other_rows, (own_ref, x_ref, y_ref))


def early_products(whole, direct, width, which, start, columns):
    half = whole[0].shape[0]
    piece = pl.BlockSpec((width // 4, TILE), lambda j: (0, start // TILE + j))
    return kernel_call(
        early_kernel,
        shape(2 * half, columns, F32),
        grid=(columns // TILE,),
        in_specs=[pl.BlockSpec((half, width), lambda j: (0, which))] * 2 + [piece] * 3,
        out_specs=pl.BlockSpec((2 * half, TILE), lambda j: (0, j)),
    )(*whole, *direct)


def forward_kernel(*refs):
    both_rows, both_parts, earlies, gates, ups = (refs[i : i + 2] for i in range(0, 10, 2))
    scaled_ref, for_gate_ref, for_up_ref, hidden_ref = refs[10:]
    half = both_rows[0].shape[0]
    for index in range(2):
        at = slice(index * half, (index + 1) * half)
        gate_pre = earlies[0][at] + times_pieces(both_rows[index], gates)
        up_pre = earlies[1][at] + times_pieces(both_rows[index], ups)
        lane = iota(half, SIDE, 1)
        mine = (lane < 24) & (lane % 8 == lax.axis_index("expert"))
        parts = both_parts[index][...].astype(F32)
        prob = jnp.sum(jnp.where(mine, parts, 0.0), axis=1, keepdims=True)
        sigmoid_gate = 1.0 / (1.0 + jnp.exp(-gate_pre))
        silu_gate = gate_pre * sigmoid_gate
        hidden = silu_gate * up_pre
        hidden_ref[at] = hidden
        scaled_ref[at] = (hidden * prob).astype(BF16)
        slope = sigmoid_gate * (1.0 + gate_pre * (1.0 - sigmoid_gate))
        for_gate_ref[at] = prob * (up_pre * slope)
        for_up_ref[at] = prob * silu_gate


def forward(whole, early, corner, width, units):
    half = whole[0].shape[0]
    rows = 2 * half
    steps = units // TILE
    block = width // 4
    tile = pl.BlockSpec((rows, TILE), lambda j: (0, j))
    next_tile = pl.BlockSpec((rows, TILE), lambda j: (0, steps + j))
    return kernel_call(
        forward_kernel,
        (shape(rows, units, BF16),) + (shape(rows, units, F32),) * 3,
        grid=(steps,),
        in_specs=[pl.BlockSpec((half, block), lambda j: (0, 3))] * 2
        + [pl.BlockSpec((half, SIDE), lambda j: (0, 2 * width // SIDE))] * 2
        + [tile, next_tile]
        + [pl.BlockSpec((block // 2, TILE), lambda j: (0, j))] * 2
        + [pl.BlockSpec((block // 2, TILE), lambda j: (0, steps + j))] * 2,
        out_specs=(tile,) * 4,
    )(*whole, *whole, early, early, *corner, *corner)


def backward_kernel(own_ref, other_ref, early_ref, first_ref, last_ref, *refs):
    for_gate_ref, for_up_ref, hidden_ref, d_gate_ref, d_up_ref, dots_ref, sum_ref = refs
    step = pl.program_id(0)
    half = own_ref.shape[0]

    @pl.when(step == 0)
    def _():
        sum_ref[...] = jnp.zeros_like(sum_ref)

    for index, grads_ref in enumerate((own_ref, other_ref)):
        at = slice(index * half, (index + 1) * half)
        raw = early_ref[at] + times_pieces(grads_ref, (first_ref, last_ref))
        d_gate_ref[at] = (raw * for_gate_ref[at]).astype(BF16)
        d_up_ref[at] = (raw * for_up_ref[at]).astype(BF16)
        sum_ref[at] += jnp.sum(raw * hidden_ref[at], axis=1, keepdims=True)

    @pl.when(step == pl.num_programs(0) - 1)
    def _():
        lane = iota(2 * half, SIDE, 1)
        mine = lane % 8 == lax.axis_index("expert")
        dots_ref[...] = exact_parts(jnp.where(mine, sum_ref[...], 0.0), lane)


def backward(whole, early, corner, for_gate, for_up, hidden, width):
    rows, units = hidden.shape
    steps = units // TILE
    block = width // 4
    tile = pl.BlockSpec((rows, TILE), lambda j: (0, j))
    return kernel_call(
        backward_kernel,
        (shape(rows, units, BF16),) * 2 + (shape(rows, SIDE, BF16),),
        grid=(steps,),
        in_specs=[pl.BlockSpec((rows // 2, block), lambda j: (0, 7))] * 2
        + [tile]
        + [pl.BlockSpec((block // 2, TILE), lambda j: (0, j))] * 2
        + [tile] * 3,
        out_specs=(tile, tile, pl.BlockSpec((rows, SIDE), lambda j: (0, 0))),
        scratch_shapes=[pltpu.VMEM((rows, 1), F32)],
    )(*whole, early, *corner, for_gate, for_up, hidden)


def corner_grad_kernel(turned_ref, term_ref, to_x, to_y):
    step = pl.program_id(0)
    part = jnp.dot(turned_ref[...], term_ref[...], preferred_element_type=F32).astype(BF16)

    @pl.when(step == 0)
    def _():
        to_x[...] = part

    @pl.when(step == 1)
    def _():
        to_y[...] = part


def corner_grads(turned, first, term, width):
    rows, units = term.shape
    half = width // 8
    once = pl.BlockSpec((half, units), lambda i: (0, 0))
    return kernel_call(
        corner_grad_kernel,
        (shape(half, units, BF16),) * 2,
        grid=(2,),
        in_specs=[
            pl.BlockSpec((half, rows), lambda i: (first + 7 - i, 0)),
            pl.BlockSpec((rows, units), lambda i: (0, 0)),
        ],
        out_specs=(once, once),
    )(turned, term)


def later_grad_kernel(turned_ref, term_ref, for_x, for_y, own):
    step = pl.program_id(0)
    part = jnp.dot(turned_ref[...], term_ref[...], preferred_element_type=F32)

    for place, out in enumerate((for_x, for_y, own)):

        @pl.when(step // 2 == place)
        def _(out=out):
            out[...] = part


def later_grads(turned, first, term, width):
    rows, units = term.shape
    half = width // 8

    def at(start):
        return pl.BlockSpec((half, units), lambda i: (jnp.clip(i - start, 0, 1), 0))

    return kernel_call(
        later_grad_kernel,
        (shape(2 * half, units, F32),) * 3,
        grid=(6,),
        in_specs=[
            pl.BlockSpec((half, rows), lambda i: (first + (i + 2) % 6, 0)),
            pl.BlockSpec((rows, units), lambda i: (0, 0)),
        ],
        out_specs=(at(0), at(2), at(4)),
    )(turned, term)


def pair_grad_kernel(turned_ref, other_turned_ref, term_ref, other_term_ref, away, own):
    step = pl.program_id(0)
    part = jnp.dot(turned_ref[...], term_ref[...], preferred_element_type=F32)
    part += jnp.dot(other_turned_ref[...], other_term_ref[...], preferred_element_type=F32)

    @pl.when(step < 2)
    def _():
        away[...] = part.astype(BF16)

    @pl.when(step >= 2)
    def _():
        own[...] = part


def pair_grads(turned, first, gap, other_turned, other_first, term, other_term, width):
    rows, units = term.shape
    half = width // 8

    def at(start):
        return pl.BlockSpec((half, units), lambda i: (jnp.clip(i - start, 0, 1), 0))

    def tile(start, jump):
        return pl.BlockSpec(
            (half, rows), lambda i: (start + i % 2 + jnp.where(i < 2, 2 * jump, 0), 0)
        )

    return kernel_call(
        pair_grad_kernel,
        (shape(2 * half, units, BF16), shape(2 * half, units, F32)),
        grid=(4,),
        in_specs=[tile(first, gap), tile(other_first, 1)]
        + [pl.BlockSpec((rows, units), lambda i: (0, 0))] * 2,
        out_specs=(at(0), at(2)),
    )(turned, other_turned, term, other_term)


def back_kernel(scaled_ref, d_gate_ref, d_up_ref, dots_ref, *refs):
    downs, gate_ups, out_ref = refs[:5], refs[5:10], refs[10]
    units = scaled_ref.shape[1]
    width = (out_ref.shape[1] - SIDE) // 2

    def product(term, weight):
        return lax.dot_general(term[...], weight, ACROSS, preferred_element_type=F32)

    start = 0
    for down, gate_up in zip(downs, gate_ups):
        depth = down.shape[0]
        out_ref[:, start : start + depth] = product(scaled_ref, down[...]).astype(BF16)
        total = product(d_gate_ref, gate_up[:, :units]) + product(d_up_ref, gate_up[:, units:])
        out_ref[:, width + start : width + start + depth] = total.astype(BF16)
        start += depth
    out_ref[:, 2 * width :] = dots_ref[...]


def back_to_rows(scaled, d_gate, d_up, dots, direct, down, gate_up, width):
    rows, units = scaled.shape
    depth = width // 4
    term = pl.BlockSpec((TILE, units), lambda i: (i, 0))
    corner = [pl.BlockSpec((depth // 2, n * units), lambda i: (0, 0)) for n in (1, 1, 2, 2)]
    return kernel_call(
        back_kernel,
        shape(rows, 2 * width + SIDE, BF16),
        grid=(rows // TILE,),
        in_specs=[term] * 3
        + [pl.BlockSpec((TILE, SIDE), lambda i: (i, 0))]
        + [pl.BlockSpec((depth, units), lambda i: (0, 2))] * 3
        + corner[:2]
        + [pl.BlockSpec((depth, 2 * units), lambda i: (0, 0))] * 3
        + corner[2:],
        out_specs=pl.BlockSpec((TILE, 2 * width + SIDE), lambda i: (i, 0)),
    )(scaled, d_gate, d_up, dots, *direct, *down, *direct, *gate_up)


def total_kernel(own_ref, *refs):
    others, out_ref = refs[:-1], refs[-1]
    out_ref[0] = own_ref[...] + sum(other[...].astype(F32) for other in others)


def total(own, *others):
    block, units = own.shape
    step = block // 4
    rows = pl.BlockSpec((step, units), lambda i: (i, 0))
    return kernel_call(
        total_kernel,
        jax.ShapeDtypeStruct((1, block, units), F32),
        grid=(block // step,),
        in_specs=[rows] * (1 + len(others)),
        out_specs=pl.BlockSpec((1, step, units), lambda i: (0, i, 0)),
    )(own, *others)


def send_corner(from_x, from_y, columns, depth):
    half = depth // 2
    return [send(from_x[:half, columns], TO_Y), send(from_y[half:depth, columns], TO_X)]


def along_line(own, before_second=()):
    slots = [own]
    for step in range(3):
        moving = after(slots[-1], before_second) if step == 1 else slots[-1]
        slots.append(send(moving, ALONG_Z))
    return slots


def from_both_cores(slots, before):
    own_core = after(jnp.concatenate(slots), before)
    return own_core, send(own_core, TO_CORE)


def send_down(for_x, for_y, from_x, from_y):
    half = from_x.shape[0]
    for_x = jnp.concatenate([for_x[:half] + from_y.astype(F32), for_x[half:]])
    for_y = jnp.concatenate([for_y[:half], for_y[half:] + from_x.astype(F32)])
    return send(for_x.astype(BF16), TO_X), send(for_y.astype(BF16), TO_Y)


def sum_over_experts(rows, before):
    half = rows.shape[0] // 2
    block = half // 4
    arrived = send(rows[half:], TO_CORE)
    moving = 0.0
    for slot, wait in zip((1, 2, 3), before):
        at = slice(slot * block, (slot + 1) * block)
        total = rows[at].astype(F32) + arrived[at].astype(F32) + moving
        moving = send(after(total.astype(BF16), wait), ALONG_Z).astype(F32)
    return arrived, moving.astype(BF16)


def after(arrays, *others):
    return lax.optimization_barrier((arrays, others))[0]


def dense_plan(tokens, expert_ids, gate_probs, cotangent, gate_proj, up_proj, down_proj):
    width = tokens.shape[1]
    units = gate_proj.shape[2]

    depth = gate_proj.shape[1]
    weights = (gate_proj[0], up_proj[0], down_proj[0])
    to_x = weights_and_rows(weights, tokens, (1, 3))
    to_y = weights_and_rows(weights, tokens, (2, 3))
    packed = pack(tokens, cotangent, expert_ids, gate_probs)
    direct = [to_x, send(to_x, TO_X), send(to_y, TO_Y)]
    whole = from_both_cores(along_line(packed), direct)
    side = [side_rows(direct[2], depth, width), side_rows(direct[1], depth, width)]
    gate_up_corner = send_corner(*direct[1:], slice(0, 2 * units), depth)
    down_corner = send_corner(*direct[1:], slice(2 * units, 3 * units), depth)
    early_gate_up = early_products(whole, direct, width, 0, 0, 2 * units)
    early_down = early_products(whole, direct, width, 1, 2 * units, units)
    turned = turn(whole, 14, lambda i: jnp.where(i < 6, i, i + 2))
    extra = along_line(jnp.concatenate(side, axis=1), (early_gate_up, early_down, turned))
    early_gate_up, early_down, turned, gate_up_corner = lax.optimization_barrier(
        (early_gate_up, early_down, turned, gate_up_corner)
    )

    scaled, for_gate, for_up, hidden = forward(whole, early_gate_up, gate_up_corner, width, units)
    corner_sent = after(corner_grads(turned, 6, scaled, width), down_corner, extra[2])
    corner_x, corner_y = send(corner_sent[0], TO_X), send(corner_sent[1], TO_Y)
    hidden, scaled = after((hidden, scaled), corner_sent)
    d_gate, d_up, dots = backward(whole, early_down, down_corner, for_gate, for_up, hidden, width)
    other_gate = send(d_gate, TO_X)
    other_up = send(d_up, TO_Y)
    shares = back_to_rows(scaled, d_gate, d_up, dots, direct, down_corner, gate_up_corner, width)
    scaled = after(scaled, shares)
    for_x, for_y, down_own = later_grads(turned, 6, scaled, width)
    down_back = send_down(for_x, for_y, corner_x, corner_y)
    shares = after(shares, corner_x, corner_y, extra[3])
    other_turned = turn(from_both_cores(extra, corner_x), 8, lambda i: i)
    gate_away, gate_own = pair_grads(turned, 0, 2, other_turned, 4, d_gate, other_gate, width)
    gate_back = send(gate_away, TO_Y)
    up_away, up_own = pair_grads(turned, 0, 1, other_turned, 0, d_up, other_up, width)
    up_back = send(up_away, TO_X)
    grad_down = total(down_own, *after(down_back, gate_away, up_away))
    arrived, line = sum_over_experts(shares, (other_turned, (other_gate, other_up), grad_down))
    outs = unpack(shares, arrived, line, expert_ids, width)
    gate_back = after(gate_back, outs)
    grad_gate = total(gate_own, gate_back)
    up_back = after(up_back, grad_gate)
    grad_up = total(up_own, up_back)
    return (*outs, grad_gate, grad_up, grad_down)


def on_device(tokens, expert_ids, *rest):
    tok_dev, top_count = expert_ids.shape
    experts = lax.axis_size("expert")
    square_and_line = lax.axis_size("dp") == 4 and experts == 8
    if square_and_line and capacity_of(tok_dev, top_count, experts) == tok_dev:
        return dense_plan(tokens, expert_ids, *rest)
    return slot_plan(tokens, expert_ids, *rest)


def solution(mesh):
    by_token = P(AXES, None)
    by_expert = P("expert", "dp", None)
    return jax.shard_map(
        on_device,
        mesh=mesh,
        in_specs=(by_token,) * 4 + (by_expert,) * 3,
        out_specs=(by_token,) * 3 + (by_expert,) * 3,
        check_vma=False,
    )
```

```python
import jax
import jax.numpy as jnp
from jax import lax
from jax.experimental import pallas as pl
from jax.experimental.pallas import tpu as pltpu
from jax.sharding import PartitionSpec as P

AXES = ("dp", "expert")
ACROSS = (((1,), (1,)), ((), ()))
OVER_ROWS = (((0,), (0,)), ((), ()))


def routing_slots(expert_ids, experts):
    onehot = (expert_ids[:, :, None] == jnp.arange(experts, dtype=jnp.int32)[None, None, :]).astype(
        jnp.int32
    )
    per_token = jnp.sum(onehot, axis=1)
    earlier = jnp.cumsum(per_token, axis=0) - per_token
    return jnp.sum(onehot * earlier[:, None, :], axis=2)


def forward_rows(rows, gate_proj, up_proj, down_proj):
    gate_pre = jnp.dot(rows, gate_proj, preferred_element_type=jnp.float32)
    up_pre = jnp.dot(rows, up_proj, preferred_element_type=jnp.float32)
    hidden = (jax.nn.silu(gate_pre) * up_pre).astype(jnp.bfloat16)
    expert_out = lax.dot_general(
        hidden, down_proj, ACROSS, preferred_element_type=jnp.float32
    ).astype(jnp.bfloat16)
    return (expert_out, gate_pre, up_pre, hidden)


def backward_rows(grad_rows, gate_pre, up_pre, gate_proj, up_proj, down_proj):
    d_hidden = jnp.dot(grad_rows, down_proj, preferred_element_type=jnp.float32)
    sigmoid_gate = jax.nn.sigmoid(gate_pre)
    silu_gate = gate_pre * sigmoid_gate
    d_gate = (d_hidden * up_pre * sigmoid_gate * (1.0 + gate_pre * (1.0 - sigmoid_gate))).astype(
        jnp.bfloat16
    )
    d_up = (d_hidden * silu_gate).astype(jnp.bfloat16)
    d_rows = lax.dot_general(d_gate, gate_proj, ACROSS, preferred_element_type=jnp.float32)
    d_rows = d_rows + lax.dot_general(d_up, up_proj, ACROSS, preferred_element_type=jnp.float32)
    return (d_rows.astype(jnp.bfloat16), d_gate, d_up)


def pick_rows(source_rows, position, top_count):
    chosen = jnp.take(source_rows, position.reshape(-1), axis=0)
    return chosen.reshape(position.shape[0], top_count, source_rows.shape[1])


def capacity_of(tok_dev, top_count, experts):
    return min(tok_dev, (tok_dev * top_count * 4 + 3 * experts - 1) // (3 * experts))


def slot_plan(tokens, expert_ids, gate_probs, cotangent, gate_proj, up_proj, down_proj):
    experts = lax.axis_size("expert")
    tok_dev, top_count = expert_ids.shape
    model_width = tokens.shape[1]
    capacity = capacity_of(tok_dev, top_count, experts)
    slot_index = routing_slots(expert_ids, experts)
    position = expert_ids * capacity + slot_index
    placing = (
        position[None, :, :] == jnp.arange(experts * capacity, dtype=jnp.int32)[:, None, None]
    ).astype(jnp.float32)
    placer = jnp.sum(placing, axis=2)
    weighted = jnp.sum(placing * gate_probs[None, :, :], axis=2)
    row_send = (
        jnp.dot(placer.astype(jnp.bfloat16), tokens, preferred_element_type=jnp.float32)
        .astype(jnp.bfloat16)
        .reshape(experts, capacity, model_width)
    )
    grad_send = (
        jnp.dot(weighted, cotangent.astype(jnp.float32), precision=lax.Precision.HIGHEST)
        .astype(jnp.bfloat16)
        .reshape(experts, capacity, model_width)
    )
    full_gate, full_up, full_down = (
        lax.all_gather(gate_proj[0], "dp", axis=0, tiled=True),
        lax.all_gather(up_proj[0], "dp", axis=0, tiled=True),
        lax.all_gather(down_proj[0], "dp", axis=0, tiled=True),
    )

    def exchange(rows):
        return lax.all_to_all(
            rows.reshape(experts, capacity, model_width),
            "expert",
            split_axis=0,
            concat_axis=0,
            tiled=True,
        ).reshape(-1, model_width)

    rows_flat = exchange(row_send)
    expert_out, gate_pre, up_pre, hidden = forward_rows(rows_flat, full_gate, full_up, full_down)
    returned = exchange(expert_out)
    grads_flat = exchange(grad_send)
    d_rows, d_gate, d_up = backward_rows(
        grads_flat, gate_pre, up_pre, full_gate, full_up, full_down
    )
    grad_back = exchange(d_rows)
    picked = pick_rows(returned, position, top_count).astype(jnp.float32)
    mixed = jnp.sum(gate_probs[:, :, None] * picked, axis=1).astype(jnp.bfloat16)
    prob_grads = jnp.sum(cotangent.astype(jnp.float32)[:, None, :] * picked, axis=2)
    picked_grads = pick_rows(grad_back, position, top_count).astype(jnp.float32)
    token_grads = jnp.sum(picked_grads, axis=1).astype(jnp.bfloat16)
    hidden_units = hidden.shape[1]
    gate_term = lax.dot_general(rows_flat, d_gate, OVER_ROWS, preferred_element_type=jnp.float32)
    up_term = lax.dot_general(rows_flat, d_up, OVER_ROWS, preferred_element_type=jnp.float32)
    down_term = lax.dot_general(grads_flat, hidden, OVER_ROWS, preferred_element_type=jnp.float32)
    shares = lax.psum_scatter(
        jnp.concatenate([gate_term, up_term, down_term], axis=1),
        "dp",
        scatter_dimension=0,
        tiled=True,
    )
    grad_gate = shares[:, :hidden_units]
    grad_up = shares[:, hidden_units : 2 * hidden_units]
    grad_down = shares[:, 2 * hidden_units :]
    return (mixed, token_grads, prob_grads, grad_gate[None], grad_up[None], grad_down[None])


TILE = 256
SIDE = 128
F32 = jnp.float32
BF16 = jnp.bfloat16
VMEM = pl.BlockSpec(memory_space=pltpu.VMEM)


RING = (0, 2, 3, 1)


def flat_index(y, x, z, core):
    return ((y * 2 + x) * 4 + z) * 2 + core


def pairs(target):
    return [
        (flat_index(y, x, z, core), flat_index(*target(y, x, z, core)))
        for y in range(2)
        for x in range(2)
        for z in range(4)
        for core in range(2)
    ]


TO_X = pairs(lambda y, x, z, core: (y, 1 - x, z, core))
TO_Y = pairs(lambda y, x, z, core: (1 - y, x, z, core))
TO_CORE = pairs(lambda y, x, z, core: (y, x, z, 1 - core))
ALONG_Z = pairs(lambda y, x, z, core: (y, x, RING[(RING.index(z) + 1) % 4], core))


def send(array, where):
    return lax.ppermute(array, AXES, where)


def kernel_call(body, out_shape, **spec):
    return pl.pallas_call(
        body,
        out_shape=out_shape,
        compiler_params=pltpu.CompilerParams(vmem_limit_bytes=24 * 1024 * 1024),
        cost_estimate=pl.CostEstimate(flops=0, bytes_accessed=0, transcendentals=0),
        **spec,
    )


def shape(rows, columns, dtype):
    return jax.ShapeDtypeStruct((rows, columns), dtype)


def iota(rows, columns, axis):
    return lax.broadcasted_iota(jnp.int32, (rows, columns), axis)


def exact_parts(values, place):
    first = values.astype(BF16).astype(F32)
    rest = values - first
    second = rest.astype(BF16).astype(F32)
    third = rest - second
    parts = jnp.where(place < 8, first, jnp.where(place < 16, second, third))
    return jnp.where(place < 24, parts, 0.0).astype(BF16)


def block_at(relative, block):
    return pl.ds(pl.multiple_of((lax.axis_index("dp") ^ relative) * block, block), block)


def pack_kernel(tokens_ref, cot_ref, ids_ref, probs_ref, out_ref):
    rows, width = tokens_ref.shape
    block = width // 4
    for r in range(4):
        there = block_at(r, block)
        out_ref[:, r * block : (r + 1) * block] = tokens_ref[:, there]
        out_ref[:, width + r * block : width + (r + 1) * block] = cot_ref[:, there]
    place = iota(SIDE, rows, 0)
    prob = jnp.zeros((SIDE, rows), F32)
    for k in range(ids_ref.shape[0]):
        prob += jnp.where(place % 8 == ids_ref[k : k + 1, :], probs_ref[k : k + 1, :], 0.0)
    same = (iota(rows, rows, 0) == iota(rows, rows, 1)).astype(BF16)
    turned = lax.dot_general(same, exact_parts(prob, place), ACROSS, preferred_element_type=F32)
    out_ref[:, 2 * width :] = turned.astype(BF16)


def pack(tokens, cotangent, expert_ids, gate_probs):
    rows, width = tokens.shape
    return kernel_call(
        pack_kernel,
        shape(rows, 2 * width + SIDE, BF16),
        in_specs=[VMEM] * 4,
        out_specs=VMEM,
    )(tokens, cotangent, expert_ids.T, gate_probs.T)


def weights_and_rows(weights, tokens):
    rows, width = tokens.shape
    dp = lax.axis_index("dp")
    weights = jnp.concatenate(weights, axis=1)
    weights, tokens = lax.optimization_barrier((weights, tokens))
    columns = jnp.split(tokens, 4, axis=1)
    spare = weights.shape[1] - width

    def wanted(blocks):
        two = jnp.concatenate([lax.select_n(dp ^ r, *columns) for r in blocks], axis=1)
        two = jnp.concatenate([two[: rows // 2], two[rows // 2 :]], axis=1)
        return jnp.pad(two, ((0, 0), (0, spare)))

    return (
        jnp.concatenate([weights, wanted((1, 3))]),
        jnp.concatenate([weights, wanted((2, 3))]),
    )


def side_rows(sides, width):
    return jnp.concatenate([sides[:, : width // 2], sides[:, width // 2 : width]])


def unpack_kernel(own_ref, core_ref, line_ref, ids_ref, mixed_out, back_out, prob_out):
    rows, width = mixed_out.shape
    block = width // 4

    def total(at):
        return own_ref[:, at].astype(F32) + core_ref[:, at].astype(F32) + line_ref[:, at].astype(F32)

    for r in range(4):
        there = block_at(r, block)
        start = r * block
        mixed_out[:, there] = total(slice(start, start + block)).astype(BF16)
        start += width
        back_out[:, there] = total(slice(start, start + block)).astype(BF16)
    lane = iota(8, SIDE, 1)
    adder = ((lane < 24) & (lane % 8 == iota(8, SIDE, 0))).astype(BF16)
    parts = total(slice(2 * width, 2 * width + SIDE)).astype(BF16)
    by_expert = lax.dot_general(adder, parts, ACROSS, preferred_element_type=F32)
    for k in range(ids_ref.shape[0]):
        hit = iota(8, rows, 0) == ids_ref[k : k + 1, :]
        prob_out[k : k + 1, :] = jnp.sum(jnp.where(hit, by_expert, 0.0), axis=0, keepdims=True)


def unpack(shares, arrived, line, expert_ids, width):
    rows, columns = line.shape
    own = shape(rows, width, BF16)
    ids = expert_ids.T
    first = pl.BlockSpec((rows, columns), lambda i: (0, 0))
    wide = pl.BlockSpec((rows, width), lambda i: (0, 0))
    small = pl.BlockSpec(ids.shape, lambda i: (0, 0))
    mixed, back, prob = kernel_call(
        unpack_kernel,
        (own, own, shape(*ids.shape, F32)),
        grid=(1,),
        in_specs=[first] * 3 + [small],
        out_specs=(wide, wide, small),
    )(shares, arrived, line, ids)
    return mixed, back, prob.T


def turn_kernel(own_ref, other_ref, out_ref):
    rows = own_ref.shape[0]
    out_ref[:, :rows] = own_ref[...].T
    out_ref[:, rows:] = other_ref[...].T


def turn(both, tiles, place_of):
    rows = both[0].shape[0]
    return kernel_call(
        turn_kernel,
        shape(tiles * TILE, 2 * rows, BF16),
        grid=(tiles,),
        in_specs=[pl.BlockSpec((rows, TILE), lambda i: (0, place_of(i)))] * 2,
        out_specs=pl.BlockSpec((TILE, 2 * rows), lambda i: (i, 0)),
    )(*both)


def times_pieces(rows_ref, pieces):
    total, start = None, 0
    for piece in pieces:
        depth = piece.shape[0]
        term = jnp.dot(rows_ref[:, start : start + depth], piece[...], preferred_element_type=F32)
        total = term if total is None else total + term
        start += depth
    return total


def early_kernel(own_rows, other_rows, own_ref, x_ref, y_ref, out_ref):
    half = own_rows.shape[0]
    out_ref[:half] = times_pieces(own_rows, (own_ref, x_ref, y_ref))
    out_ref[half:] = times_pieces(other_rows, (own_ref, x_ref, y_ref))


def early_products(whole, direct, width, which, start, columns):
    half = whole[0].shape[0]
    piece = pl.BlockSpec((width // 4, TILE), lambda j: (0, start // TILE + j))
    return kernel_call(
        early_kernel,
        shape(2 * half, columns, F32),
        grid=(columns // TILE,),
        in_specs=[pl.BlockSpec((half, width), lambda j: (0, which))] * 2 + [piece] * 3,
        out_specs=pl.BlockSpec((2 * half, TILE), lambda j: (0, j)),
    )(*whole, *direct)


def forward_kernel(*refs):
    both_rows, both_parts, earlies, gates, ups = (refs[i : i + 2] for i in range(0, 10, 2))
    scaled_ref, for_gate_ref, for_up_ref, hidden_ref = refs[10:]
    half = both_rows[0].shape[0]
    for index in range(2):
        at = slice(index * half, (index + 1) * half)
        gate_pre = earlies[0][at] + times_pieces(both_rows[index], gates)
        up_pre = earlies[1][at] + times_pieces(both_rows[index], ups)
        lane = iota(half, SIDE, 1)
        mine = (lane < 24) & (lane % 8 == lax.axis_index("expert"))
        parts = both_parts[index][...].astype(F32)
        prob = jnp.sum(jnp.where(mine, parts, 0.0), axis=1, keepdims=True)
        sigmoid_gate = 1.0 / (1.0 + jnp.exp(-gate_pre))
        silu_gate = gate_pre * sigmoid_gate
        hidden = silu_gate * up_pre
        hidden_ref[at] = hidden
        scaled_ref[at] = (hidden * prob).astype(BF16)
        slope = sigmoid_gate * (1.0 + gate_pre * (1.0 - sigmoid_gate))
        for_gate_ref[at] = prob * (up_pre * slope)
        for_up_ref[at] = prob * silu_gate


def forward(whole, early, corner, width, units):
    half = whole[0].shape[0]
    rows = 2 * half
    steps = units // TILE
    block = width // 4
    tile = pl.BlockSpec((rows, TILE), lambda j: (0, j))
    next_tile = pl.BlockSpec((rows, TILE), lambda j: (0, steps + j))
    return kernel_call(
        forward_kernel,
        (shape(rows, units, BF16),) + (shape(rows, units, F32),) * 3,
        grid=(steps,),
        in_specs=[pl.BlockSpec((half, block), lambda j: (0, 3))] * 2
        + [pl.BlockSpec((half, SIDE), lambda j: (0, 2 * width // SIDE))] * 2
        + [tile, next_tile]
        + [pl.BlockSpec((block // 2, TILE), lambda j: (0, j))] * 2
        + [pl.BlockSpec((block // 2, TILE), lambda j: (0, steps + j))] * 2,
        out_specs=(tile,) * 4,
    )(*whole, *whole, early, early, *corner, *corner)


def backward_kernel(own_ref, other_ref, early_ref, first_ref, last_ref, *refs):
    for_gate_ref, for_up_ref, hidden_ref, d_gate_ref, d_up_ref, dots_ref, sum_ref = refs
    step = pl.program_id(0)
    half = own_ref.shape[0]

    @pl.when(step == 0)
    def _():
        sum_ref[...] = jnp.zeros_like(sum_ref)

    for index, grads_ref in enumerate((own_ref, other_ref)):
        at = slice(index * half, (index + 1) * half)
        raw = early_ref[at] + times_pieces(grads_ref, (first_ref, last_ref))
        d_gate_ref[at] = (raw * for_gate_ref[at]).astype(BF16)
        d_up_ref[at] = (raw * for_up_ref[at]).astype(BF16)
        sum_ref[at] += jnp.sum(raw * hidden_ref[at], axis=1, keepdims=True)

    @pl.when(step == pl.num_programs(0) - 1)
    def _():
        lane = iota(2 * half, SIDE, 1)
        mine = lane % 8 == lax.axis_index("expert")
        dots_ref[...] = exact_parts(jnp.where(mine, sum_ref[...], 0.0), lane)


def backward(whole, early, corner, for_gate, for_up, hidden, width):
    rows, units = hidden.shape
    steps = units // TILE
    block = width // 4
    tile = pl.BlockSpec((rows, TILE), lambda j: (0, j))
    return kernel_call(
        backward_kernel,
        (shape(rows, units, BF16),) * 2 + (shape(rows, SIDE, BF16),),
        grid=(steps,),
        in_specs=[pl.BlockSpec((rows // 2, block), lambda j: (0, 7))] * 2
        + [tile]
        + [pl.BlockSpec((block // 2, TILE), lambda j: (0, j))] * 2
        + [tile] * 3,
        out_specs=(tile, tile, pl.BlockSpec((rows, SIDE), lambda j: (0, 0))),
        scratch_shapes=[pltpu.VMEM((rows, 1), F32)],
    )(*whole, early, *corner, for_gate, for_up, hidden)


def corner_grad_kernel(turned_ref, term_ref, to_x, to_y):
    step = pl.program_id(0)
    part = jnp.dot(turned_ref[...], term_ref[...], preferred_element_type=F32).astype(BF16)

    @pl.when(step == 0)
    def _():
        to_x[...] = part

    @pl.when(step == 1)
    def _():
        to_y[...] = part


def corner_grads(turned, first, term, width):
    rows, units = term.shape
    half = width // 8
    once = pl.BlockSpec((half, units), lambda i: (0, 0))
    return kernel_call(
        corner_grad_kernel,
        (shape(half, units, BF16),) * 2,
        grid=(2,),
        in_specs=[
            pl.BlockSpec((half, rows), lambda i: (first + 7 - i, 0)),
            pl.BlockSpec((rows, units), lambda i: (0, 0)),
        ],
        out_specs=(once, once),
    )(turned, term)


def later_grad_kernel(turned_ref, term_ref, for_x, for_y, own):
    step = pl.program_id(0)
    part = jnp.dot(turned_ref[...], term_ref[...], preferred_element_type=F32)

    for place, out in enumerate((for_x, for_y, own)):

        @pl.when(step // 2 == place)
        def _(out=out):
            out[...] = part


def later_grads(turned, first, term, width):
    rows, units = term.shape
    half = width // 8

    def at(start):
        return pl.BlockSpec((half, units), lambda i: (jnp.clip(i - start, 0, 1), 0))

    return kernel_call(
        later_grad_kernel,
        (shape(2 * half, units, F32),) * 3,
        grid=(6,),
        in_specs=[
            pl.BlockSpec((half, rows), lambda i: (first + (i + 2) % 6, 0)),
            pl.BlockSpec((rows, units), lambda i: (0, 0)),
        ],
        out_specs=(at(0), at(2), at(4)),
    )(turned, term)


def pair_grad_kernel(turned_ref, other_turned_ref, term_ref, other_term_ref, away, own):
    step = pl.program_id(0)
    part = jnp.dot(turned_ref[...], term_ref[...], preferred_element_type=F32)
    part += jnp.dot(other_turned_ref[...], other_term_ref[...], preferred_element_type=F32)

    @pl.when(step < 2)
    def _():
        away[...] = part.astype(BF16)

    @pl.when(step >= 2)
    def _():
        own[...] = part


def pair_grads(turned, first, gap, other_turned, other_first, term, other_term, width):
    rows, units = term.shape
    half = width // 8

    def at(start):
        return pl.BlockSpec((half, units), lambda i: (jnp.clip(i - start, 0, 1), 0))

    def tile(start, jump):
        return pl.BlockSpec(
            (half, rows), lambda i: (start + i % 2 + jnp.where(i < 2, 2 * jump, 0), 0)
        )

    return kernel_call(
        pair_grad_kernel,
        (shape(2 * half, units, BF16), shape(2 * half, units, F32)),
        grid=(4,),
        in_specs=[tile(first, gap), tile(other_first, 1)]
        + [pl.BlockSpec((rows, units), lambda i: (0, 0))] * 2,
        out_specs=(at(0), at(2)),
    )(turned, other_turned, term, other_term)


def back_kernel(scaled_ref, d_gate_ref, d_up_ref, dots_ref, *refs):
    downs, gate_ups, out_ref = refs[:5], refs[5:10], refs[10]
    units = scaled_ref.shape[1]
    width = (out_ref.shape[1] - SIDE) // 2

    def product(term, weight):
        return lax.dot_general(term[...], weight, ACROSS, preferred_element_type=F32)

    start = 0
    for down, gate_up in zip(downs, gate_ups):
        depth = down.shape[0]
        out_ref[:, start : start + depth] = product(scaled_ref, down[...]).astype(BF16)
        total = product(d_gate_ref, gate_up[:, :units]) + product(d_up_ref, gate_up[:, units:])
        out_ref[:, width + start : width + start + depth] = total.astype(BF16)
        start += depth
    out_ref[:, 2 * width :] = dots_ref[...]


def back_to_rows(half, scaled, d_gate, d_up, dots, direct, down, gate_up, width):
    units = scaled.shape[1]
    rows = scaled.shape[0] // 2
    depth = width // 4
    term = pl.BlockSpec((rows, units), lambda i: (half, 0))
    corner = [pl.BlockSpec((depth // 2, n * units), lambda i: (0, 0)) for n in (1, 1, 2, 2)]
    return kernel_call(
        back_kernel,
        shape(rows, 2 * width + SIDE, BF16),
        grid=(1,),
        in_specs=[term] * 3
        + [pl.BlockSpec((rows, SIDE), lambda i: (half, 0))]
        + [pl.BlockSpec((depth, units), lambda i: (0, 2))] * 3
        + corner[:2]
        + [pl.BlockSpec((depth, 2 * units), lambda i: (0, 0))] * 3
        + corner[2:],
        out_specs=pl.BlockSpec((rows, 2 * width + SIDE), lambda i: (0, 0)),
    )(scaled, d_gate, d_up, dots, *direct, *down, *direct, *gate_up)


def total_kernel(counts, *refs):
    outs = refs[-len(counts) :]
    for count, out_ref in zip(counts, outs):
        terms, refs = refs[:count], refs[count:]
        out_ref[0] = terms[0][...] + sum(term[...].astype(F32) for term in terms[1:])


def totals(*groups):
    block, units = groups[0][0].shape
    step = block // 4
    rows = pl.BlockSpec((step, units), lambda i: (i, 0))
    counts = [len(group) for group in groups]

    def body(*refs):
        total_kernel(counts, *refs)

    return kernel_call(
        body,
        (jax.ShapeDtypeStruct((1, block, units), F32),) * len(groups),
        grid=(block // step,),
        in_specs=[rows] * sum(counts),
        out_specs=(pl.BlockSpec((1, step, units), lambda i: (0, i, 0)),) * len(groups),
    )(*[term for group in groups for term in group])


def send_corner(from_x, from_y, columns, depth):
    half = depth // 2
    return [send(from_x[:half, columns], TO_Y), send(from_y[half:depth, columns], TO_X)]


def along_line(own, before=((), (), ())):
    slots = [own]
    for wait in before:
        slots.append(send(after(slots[-1], *wait), ALONG_Z))
    return slots


def from_both_cores(own_core, before):
    return own_core, send(after(own_core, before), TO_CORE)


def send_down(for_x, for_y, from_x, from_y):
    half = from_x.shape[0]
    for_x = jnp.concatenate([for_x[:half] + from_y.astype(F32), for_x[half:]])
    for_y = jnp.concatenate([for_y[:half], for_y[half:] + from_x.astype(F32)])
    return send(for_x.astype(BF16), TO_X), send(for_y.astype(BF16), TO_Y)


def sum_over_experts(own, other, before):
    block = own.shape[0] // 4
    arrived = send(other, TO_CORE)
    moving = 0.0
    for slot, wait in zip((1, 2, 3), before):
        at = slice(slot * block, (slot + 1) * block)
        total = own[at].astype(F32) + arrived[at].astype(F32) + moving
        moving = send(after(total.astype(BF16), wait), ALONG_Z).astype(F32)
    return arrived, moving.astype(BF16)


def after(arrays, *others):
    return lax.optimization_barrier((arrays, others))[0]


def dense_plan(tokens, expert_ids, gate_probs, cotangent, gate_proj, up_proj, down_proj):
    width = tokens.shape[1]
    units = gate_proj.shape[2]

    depth = gate_proj.shape[1]
    weights = (gate_proj[0], up_proj[0], down_proj[0])
    to_x, to_y = weights_and_rows(weights, tokens)
    packed = pack(tokens, cotangent, expert_ids, gate_probs)
    from_x, from_y = send(to_x, TO_X), send(to_y, TO_Y)
    direct = [to_x, from_x, from_y]
    whole = from_both_cores(jnp.concatenate(along_line(packed)), (from_x, from_y))
    side = [side_rows(from_y[depth:], width), side_rows(from_x[depth:], width)]
    gate_up_corner = send_corner(*direct[1:], slice(0, 2 * units), depth)
    down_corner = send_corner(*direct[1:], slice(2 * units, 3 * units), depth)
    early_gate_up = early_products(whole, direct, width, 0, 0, 2 * units)
    early_down = early_products(whole, direct, width, 1, 2 * units, units)
    turned = turn(whole, 14, lambda i: jnp.where(i < 6, i, i + 2))
    extra = along_line(
        jnp.concatenate(side, axis=1), ((), (early_gate_up,), (early_down, turned))
    )
    early_gate_up, early_down, turned, gate_up_corner = lax.optimization_barrier(
        (early_gate_up, early_down, turned, gate_up_corner)
    )

    scaled, for_gate, for_up, hidden = forward(whole, early_gate_up, gate_up_corner, width, units)
    corner_sent = corner_grads(turned, 6, scaled, width)
    corner_x, corner_y = send(corner_sent[0], TO_X), send(corner_sent[1], TO_Y)
    hidden, scaled = after((hidden, scaled), corner_sent)
    d_gate, d_up, dots = backward(whole, early_down, down_corner, for_gate, for_up, hidden, width)
    other_gate = send(d_gate, TO_X)
    other_up = send(d_up, TO_Y)
    back_terms = (scaled, d_gate, d_up, dots, direct, down_corner, gate_up_corner, width)
    other_shares = back_to_rows(1, *back_terms)
    own_shares = back_to_rows(0, *after(back_terms[:4], other_shares), *back_terms[4:])
    scaled = after(scaled, other_shares)
    for_x, for_y, down_own = later_grads(turned, 6, scaled, width)
    down_back = send_down(for_x, for_y, corner_x, corner_y)
    extra = jnp.concatenate(extra[:3] + [after(extra[3], down_corner)])
    other_shares = after(other_shares, corner_x, corner_y, extra)
    other_turned = turn(from_both_cores(extra, corner_x), 8, lambda i: i)
    gate_away, gate_own = pair_grads(turned, 0, 2, other_turned, 4, d_gate, other_gate, width)
    gate_back = send(gate_away, TO_Y)
    up_away, up_own = pair_grads(turned, 0, 1, other_turned, 0, d_up, other_up, width)
    up_back = send(up_away, TO_X)
    down_back = after(down_back, gate_away, up_away)
    arrived, line = sum_over_experts(own_shares, other_shares, (other_turned, (other_gate, other_up), down_back))
    (grad_down,) = totals((down_own, *down_back))
    outs = unpack(own_shares, arrived, line, expert_ids, width)
    gate_back, up_back = after((gate_back, up_back), outs, grad_down)
    grad_gate, grad_up = totals((gate_own, gate_back), (up_own, up_back))
    return (*outs, grad_gate, grad_up, grad_down)


def on_device(tokens, expert_ids, *rest):
    tok_dev, top_count = expert_ids.shape
    experts = lax.axis_size("expert")
    square_and_line = lax.axis_size("dp") == 4 and experts == 8
    if square_and_line and capacity_of(tok_dev, top_count, experts) == tok_dev:
        return dense_plan(tokens, expert_ids, *rest)
    return slot_plan(tokens, expert_ids, *rest)


def solution(mesh):
    by_token = P(AXES, None)
    by_expert = P("expert", "dp", None)
    return jax.shard_map(
        on_device,
        mesh=mesh,
        in_specs=(by_token,) * 4 + (by_expert,) * 3,
        out_specs=(by_token,) * 3 + (by_expert,) * 3,
        check_vma=False,
    )
```

```python
import jax
import jax.numpy as jnp
from jax import lax
from jax.experimental import pallas as pl
from jax.experimental.pallas import tpu as pltpu
from jax.sharding import PartitionSpec as P

AXES = ("dp", "expert")
ACROSS = (((1,), (1,)), ((), ()))
OVER_ROWS = (((0,), (0,)), ((), ()))


def routing_slots(expert_ids, experts):
    onehot = (expert_ids[:, :, None] == jnp.arange(experts, dtype=jnp.int32)[None, None, :]).astype(
        jnp.int32
    )
    per_token = jnp.sum(onehot, axis=1)
    earlier = jnp.cumsum(per_token, axis=0) - per_token
    return jnp.sum(onehot * earlier[:, None, :], axis=2)


def forward_rows(rows, gate_proj, up_proj, down_proj):
    gate_pre = jnp.dot(rows, gate_proj, preferred_element_type=jnp.float32)
    up_pre = jnp.dot(rows, up_proj, preferred_element_type=jnp.float32)
    hidden = (jax.nn.silu(gate_pre) * up_pre).astype(jnp.bfloat16)
    expert_out = lax.dot_general(
        hidden, down_proj, ACROSS, preferred_element_type=jnp.float32
    ).astype(jnp.bfloat16)
    return (expert_out, gate_pre, up_pre, hidden)


def backward_rows(grad_rows, gate_pre, up_pre, gate_proj, up_proj, down_proj):
    d_hidden = jnp.dot(grad_rows, down_proj, preferred_element_type=jnp.float32)
    sigmoid_gate = jax.nn.sigmoid(gate_pre)
    silu_gate = gate_pre * sigmoid_gate
    d_gate = (d_hidden * up_pre * sigmoid_gate * (1.0 + gate_pre * (1.0 - sigmoid_gate))).astype(
        jnp.bfloat16
    )
    d_up = (d_hidden * silu_gate).astype(jnp.bfloat16)
    d_rows = lax.dot_general(d_gate, gate_proj, ACROSS, preferred_element_type=jnp.float32)
    d_rows = d_rows + lax.dot_general(d_up, up_proj, ACROSS, preferred_element_type=jnp.float32)
    return (d_rows.astype(jnp.bfloat16), d_gate, d_up)


def pick_rows(source_rows, position, top_count):
    chosen = jnp.take(source_rows, position.reshape(-1), axis=0)
    return chosen.reshape(position.shape[0], top_count, source_rows.shape[1])


def capacity_of(tok_dev, top_count, experts):
    return min(tok_dev, (tok_dev * top_count * 4 + 3 * experts - 1) // (3 * experts))


def slot_plan(tokens, expert_ids, gate_probs, cotangent, gate_proj, up_proj, down_proj):
    experts = lax.axis_size("expert")
    tok_dev, top_count = expert_ids.shape
    model_width = tokens.shape[1]
    capacity = capacity_of(tok_dev, top_count, experts)
    slot_index = routing_slots(expert_ids, experts)
    position = expert_ids * capacity + slot_index
    placing = (
        position[None, :, :] == jnp.arange(experts * capacity, dtype=jnp.int32)[:, None, None]
    ).astype(jnp.float32)
    placer = jnp.sum(placing, axis=2)
    weighted = jnp.sum(placing * gate_probs[None, :, :], axis=2)
    row_send = (
        jnp.dot(placer.astype(jnp.bfloat16), tokens, preferred_element_type=jnp.float32)
        .astype(jnp.bfloat16)
        .reshape(experts, capacity, model_width)
    )
    grad_send = (
        jnp.dot(weighted, cotangent.astype(jnp.float32), precision=lax.Precision.HIGHEST)
        .astype(jnp.bfloat16)
        .reshape(experts, capacity, model_width)
    )
    full_gate, full_up, full_down = (
        lax.all_gather(gate_proj[0], "dp", axis=0, tiled=True),
        lax.all_gather(up_proj[0], "dp", axis=0, tiled=True),
        lax.all_gather(down_proj[0], "dp", axis=0, tiled=True),
    )

    def exchange(rows):
        return lax.all_to_all(
            rows.reshape(experts, capacity, model_width),
            "expert",
            split_axis=0,
            concat_axis=0,
            tiled=True,
        ).reshape(-1, model_width)

    rows_flat = exchange(row_send)
    expert_out, gate_pre, up_pre, hidden = forward_rows(rows_flat, full_gate, full_up, full_down)
    returned = exchange(expert_out)
    grads_flat = exchange(grad_send)
    d_rows, d_gate, d_up = backward_rows(
        grads_flat, gate_pre, up_pre, full_gate, full_up, full_down
    )
    grad_back = exchange(d_rows)
    picked = pick_rows(returned, position, top_count).astype(jnp.float32)
    mixed = jnp.sum(gate_probs[:, :, None] * picked, axis=1).astype(jnp.bfloat16)
    prob_grads = jnp.sum(cotangent.astype(jnp.float32)[:, None, :] * picked, axis=2)
    picked_grads = pick_rows(grad_back, position, top_count).astype(jnp.float32)
    token_grads = jnp.sum(picked_grads, axis=1).astype(jnp.bfloat16)
    hidden_units = hidden.shape[1]
    gate_term = lax.dot_general(rows_flat, d_gate, OVER_ROWS, preferred_element_type=jnp.float32)
    up_term = lax.dot_general(rows_flat, d_up, OVER_ROWS, preferred_element_type=jnp.float32)
    down_term = lax.dot_general(grads_flat, hidden, OVER_ROWS, preferred_element_type=jnp.float32)
    shares = lax.psum_scatter(
        jnp.concatenate([gate_term, up_term, down_term], axis=1),
        "dp",
        scatter_dimension=0,
        tiled=True,
    )
    grad_gate = shares[:, :hidden_units]
    grad_up = shares[:, hidden_units : 2 * hidden_units]
    grad_down = shares[:, 2 * hidden_units :]
    return (mixed, token_grads, prob_grads, grad_gate[None], grad_up[None], grad_down[None])


TILE = 256
SIDE = 128
F32 = jnp.float32
BF16 = jnp.bfloat16
VMEM = pl.BlockSpec(memory_space=pltpu.VMEM)


RING = (0, 2, 3, 1)


def flat_index(y, x, z, core):
    return ((y * 2 + x) * 4 + z) * 2 + core


def pairs(target):
    return [
        (flat_index(y, x, z, core), flat_index(*target(y, x, z, core)))
        for y in range(2)
        for x in range(2)
        for z in range(4)
        for core in range(2)
    ]


TO_X = pairs(lambda y, x, z, core: (y, 1 - x, z, core))
TO_Y = pairs(lambda y, x, z, core: (1 - y, x, z, core))
TO_CORE = pairs(lambda y, x, z, core: (y, x, z, 1 - core))
ALONG_Z = pairs(lambda y, x, z, core: (y, x, RING[(RING.index(z) + 1) % 4], core))


def send(array, where):
    return lax.ppermute(array, AXES, where)


def kernel_call(body, out_shape, **spec):
    return pl.pallas_call(
        body,
        out_shape=out_shape,
        compiler_params=pltpu.CompilerParams(vmem_limit_bytes=24 * 1024 * 1024),
        cost_estimate=pl.CostEstimate(flops=0, bytes_accessed=0, transcendentals=0),
        **spec,
    )


def shape(rows, columns, dtype):
    return jax.ShapeDtypeStruct((rows, columns), dtype)


def iota(rows, columns, axis):
    return lax.broadcasted_iota(jnp.int32, (rows, columns), axis)


def exact_parts(values, place):
    first = values.astype(BF16).astype(F32)
    rest = values - first
    second = rest.astype(BF16).astype(F32)
    third = rest - second
    parts = jnp.where(place < 8, first, jnp.where(place < 16, second, third))
    return jnp.where(place < 24, parts, 0.0).astype(BF16)


def block_at(relative, block):
    return pl.ds(pl.multiple_of((lax.axis_index("dp") ^ relative) * block, block), block)


def pack_kernel(tokens_ref, cot_ref, ids_ref, probs_ref, out_ref):
    rows, width = tokens_ref.shape
    block = width // 4
    for r in range(4):
        there = block_at(r, block)
        out_ref[:, r * block : (r + 1) * block] = tokens_ref[:, there]
        out_ref[:, width + r * block : width + (r + 1) * block] = cot_ref[:, there]
    place = iota(SIDE, rows, 0)
    prob = jnp.zeros((SIDE, rows), F32)
    for k in range(ids_ref.shape[0]):
        prob += jnp.where(place % 8 == ids_ref[k : k + 1, :], probs_ref[k : k + 1, :], 0.0)
    same = (iota(rows, rows, 0) == iota(rows, rows, 1)).astype(BF16)
    turned = lax.dot_general(same, exact_parts(prob, place), ACROSS, preferred_element_type=F32)
    out_ref[:, 2 * width :] = turned.astype(BF16)


def pack(tokens, cotangent, expert_ids, gate_probs):
    rows, width = tokens.shape
    return kernel_call(
        pack_kernel,
        shape(rows, 2 * width + SIDE, BF16),
        in_specs=[VMEM] * 4,
        out_specs=VMEM,
    )(tokens, cotangent, expert_ids.T, gate_probs.T)


def weights_and_rows(weights, tokens):
    rows, width = tokens.shape
    dp = lax.axis_index("dp")
    weights = jnp.concatenate(weights, axis=1)
    weights, tokens = lax.optimization_barrier((weights, tokens))
    columns = jnp.split(tokens, 4, axis=1)
    spare = weights.shape[1] - width

    def wanted(blocks):
        two = jnp.concatenate([lax.select_n(dp ^ r, *columns) for r in blocks], axis=1)
        two = jnp.concatenate([two[: rows // 2], two[rows // 2 :]], axis=1)
        return jnp.pad(two, ((0, 0), (0, spare)))

    return (
        jnp.concatenate([weights, wanted((1, 3))]),
        jnp.concatenate([weights, wanted((2, 3))]),
    )


def side_rows(sides, width):
    return jnp.concatenate([sides[:, : width // 2], sides[:, width // 2 : width]])


def unpack_kernel(own_ref, core_ref, line_ref, ids_ref, mixed_out, back_out, prob_out):
    rows, width = mixed_out.shape
    block = width // 4

    def total(at):
        return own_ref[:, at].astype(F32) + core_ref[:, at].astype(F32) + line_ref[:, at].astype(F32)

    for r in range(4):
        there = block_at(r, block)
        start = r * block
        mixed_out[:, there] = total(slice(start, start + block)).astype(BF16)
        start += width
        back_out[:, there] = total(slice(start, start + block)).astype(BF16)
    lane = iota(8, SIDE, 1)
    adder = ((lane < 24) & (lane % 8 == iota(8, SIDE, 0))).astype(BF16)
    parts = total(slice(2 * width, 2 * width + SIDE)).astype(BF16)
    by_expert = lax.dot_general(adder, parts, ACROSS, preferred_element_type=F32)
    for k in range(ids_ref.shape[0]):
        hit = iota(8, rows, 0) == ids_ref[k : k + 1, :]
        prob_out[k : k + 1, :] = jnp.sum(jnp.where(hit, by_expert, 0.0), axis=0, keepdims=True)


def unpack(shares, arrived, line, expert_ids, width):
    rows, columns = line.shape
    own = shape(rows, width, BF16)
    ids = expert_ids.T
    first = pl.BlockSpec((rows, columns), lambda i: (0, 0))
    wide = pl.BlockSpec((rows, width), lambda i: (0, 0))
    small = pl.BlockSpec(ids.shape, lambda i: (0, 0))
    mixed, back, prob = kernel_call(
        unpack_kernel,
        (own, own, shape(*ids.shape, F32)),
        grid=(1,),
        in_specs=[first] * 3 + [small],
        out_specs=(wide, wide, small),
    )(shares, arrived, line, ids)
    return mixed, back, prob.T


def turn_kernel(own_ref, other_ref, out_ref):
    rows = own_ref.shape[0]
    out_ref[:, :rows] = own_ref[...].T
    out_ref[:, rows:] = other_ref[...].T


def turn(both, tiles, place_of):
    rows = both[0].shape[0]
    return kernel_call(
        turn_kernel,
        shape(tiles * TILE, 2 * rows, BF16),
        grid=(tiles,),
        in_specs=[pl.BlockSpec((rows, TILE), lambda i: (0, place_of(i)))] * 2,
        out_specs=pl.BlockSpec((TILE, 2 * rows), lambda i: (i, 0)),
    )(*both)


def times_pieces(rows_ref, pieces):
    total, start = None, 0
    for piece in pieces:
        depth = piece.shape[0]
        term = jnp.dot(rows_ref[:, start : start + depth], piece[...], preferred_element_type=F32)
        total = term if total is None else total + term
        start += depth
    return total


def early_kernel(own_rows, other_rows, own_ref, x_ref, y_ref, out_ref):
    half = own_rows.shape[0]
    out_ref[:half] = times_pieces(own_rows, (own_ref, x_ref, y_ref))
    out_ref[half:] = times_pieces(other_rows, (own_ref, x_ref, y_ref))


def early_products(whole, direct, width, which, start, columns):
    half = whole[0].shape[0]
    piece = pl.BlockSpec((width // 4, TILE), lambda j: (0, start // TILE + j))
    return kernel_call(
        early_kernel,
        shape(2 * half, columns, F32),
        grid=(columns // TILE,),
        in_specs=[pl.BlockSpec((half, width), lambda j: (0, which))] * 2 + [piece] * 3,
        out_specs=pl.BlockSpec((2 * half, TILE), lambda j: (0, j)),
    )(*whole, *direct)


def forward_kernel(*refs):
    both_rows, both_parts, earlies, gates, ups = (refs[i : i + 2] for i in range(0, 10, 2))
    scaled_ref, for_gate_ref, for_up_ref, hidden_ref = refs[10:]
    half = both_rows[0].shape[0]
    for index in range(2):
        at = slice(index * half, (index + 1) * half)
        gate_pre = earlies[0][at] + times_pieces(both_rows[index], gates)
        up_pre = earlies[1][at] + times_pieces(both_rows[index], ups)
        lane = iota(half, SIDE, 1)
        mine = (lane < 24) & (lane % 8 == lax.axis_index("expert"))
        parts = both_parts[index][...].astype(F32)
        prob = jnp.sum(jnp.where(mine, parts, 0.0), axis=1, keepdims=True)
        sigmoid_gate = 1.0 / (1.0 + jnp.exp(-gate_pre))
        silu_gate = gate_pre * sigmoid_gate
        hidden = silu_gate * up_pre
        hidden_ref[at] = hidden
        scaled_ref[at] = (hidden * prob).astype(BF16)
        slope = sigmoid_gate * (1.0 + gate_pre * (1.0 - sigmoid_gate))
        for_gate_ref[at] = prob * (up_pre * slope)
        for_up_ref[at] = prob * silu_gate


def forward(whole, early, corner, width, units):
    half = whole[0].shape[0]
    rows = 2 * half
    steps = units // TILE
    block = width // 4
    tile = pl.BlockSpec((rows, TILE), lambda j: (0, j))
    next_tile = pl.BlockSpec((rows, TILE), lambda j: (0, steps + j))
    return kernel_call(
        forward_kernel,
        (shape(rows, units, BF16),) + (shape(rows, units, F32),) * 3,
        grid=(steps,),
        in_specs=[pl.BlockSpec((half, block), lambda j: (0, 3))] * 2
        + [pl.BlockSpec((half, SIDE), lambda j: (0, 2 * width // SIDE))] * 2
        + [tile, next_tile]
        + [pl.BlockSpec((block // 2, TILE), lambda j: (0, j))] * 2
        + [pl.BlockSpec((block // 2, TILE), lambda j: (0, steps + j))] * 2,
        out_specs=(tile,) * 4,
    )(*whole, *whole, early, early, *corner, *corner)


def backward_kernel(own_ref, other_ref, early_ref, first_ref, last_ref, *refs):
    for_gate_ref, for_up_ref, hidden_ref, d_gate_ref, d_up_ref, dots_ref, sum_ref = refs
    step = pl.program_id(0)
    half = own_ref.shape[0]

    @pl.when(step == 0)
    def _():
        sum_ref[...] = jnp.zeros_like(sum_ref)

    for index, grads_ref in enumerate((own_ref, other_ref)):
        at = slice(index * half, (index + 1) * half)
        raw = early_ref[at] + times_pieces(grads_ref, (first_ref, last_ref))
        d_gate_ref[at] = (raw * for_gate_ref[at]).astype(BF16)
        d_up_ref[at] = (raw * for_up_ref[at]).astype(BF16)
        sum_ref[at] += jnp.sum(raw * hidden_ref[at], axis=1, keepdims=True)

    @pl.when(step == pl.num_programs(0) - 1)
    def _():
        lane = iota(2 * half, SIDE, 1)
        mine = lane % 8 == lax.axis_index("expert")
        dots_ref[...] = exact_parts(jnp.where(mine, sum_ref[...], 0.0), lane)


def backward(whole, early, corner, for_gate, for_up, hidden, width):
    rows, units = hidden.shape
    steps = units // TILE
    block = width // 4
    tile = pl.BlockSpec((rows, TILE), lambda j: (0, j))
    return kernel_call(
        backward_kernel,
        (shape(rows, units, BF16),) * 2 + (shape(rows, SIDE, BF16),),
        grid=(steps,),
        in_specs=[pl.BlockSpec((rows // 2, block), lambda j: (0, 7))] * 2
        + [tile]
        + [pl.BlockSpec((block // 2, TILE), lambda j: (0, j))] * 2
        + [tile] * 3,
        out_specs=(tile, tile, pl.BlockSpec((rows, SIDE), lambda j: (0, 0))),
        scratch_shapes=[pltpu.VMEM((rows, 1), F32)],
    )(*whole, early, *corner, for_gate, for_up, hidden)


def corner_grad_kernel(turned_ref, term_ref, to_x, to_y):
    step = pl.program_id(0)
    part = jnp.dot(turned_ref[...], term_ref[...], preferred_element_type=F32).astype(BF16)

    @pl.when(step == 0)
    def _():
        to_x[...] = part

    @pl.when(step == 1)
    def _():
        to_y[...] = part


def corner_grads(turned, first, term, width):
    rows, units = term.shape
    half = width // 8
    once = pl.BlockSpec((half, units), lambda i: (0, 0))
    return kernel_call(
        corner_grad_kernel,
        (shape(half, units, BF16),) * 2,
        grid=(2,),
        in_specs=[
            pl.BlockSpec((half, rows), lambda i: (first + 7 - i, 0)),
            pl.BlockSpec((rows, units), lambda i: (0, 0)),
        ],
        out_specs=(once, once),
    )(turned, term)


def later_grad_kernel(turned_ref, term_ref, for_x, for_y, own):
    step = pl.program_id(0)
    part = jnp.dot(turned_ref[...], term_ref[...], preferred_element_type=F32)

    for place, out in enumerate((for_x, for_y, own)):

        @pl.when(step // 2 == place)
        def _(out=out):
            out[...] = part


def later_grads(turned, first, term, width):
    rows, units = term.shape
    half = width // 8

    def at(start):
        return pl.BlockSpec((half, units), lambda i: (jnp.clip(i - start, 0, 1), 0))

    return kernel_call(
        later_grad_kernel,
        (shape(2 * half, units, F32),) * 3,
        grid=(6,),
        in_specs=[
            pl.BlockSpec((half, rows), lambda i: (first + (i + 2) % 6, 0)),
            pl.BlockSpec((rows, units), lambda i: (0, 0)),
        ],
        out_specs=(at(0), at(2), at(4)),
    )(turned, term)


def pair_grad_kernel(turned_ref, other_turned_ref, term_ref, other_term_ref, away, own):
    step = pl.program_id(0)
    part = jnp.dot(turned_ref[...], term_ref[...], preferred_element_type=F32)
    part += jnp.dot(other_turned_ref[...], other_term_ref[...], preferred_element_type=F32)

    @pl.when(step < 2)
    def _():
        away[...] = part.astype(BF16)

    @pl.when(step >= 2)
    def _():
        own[...] = part


def pair_grads(turned, first, gap, other_turned, other_first, term, other_term, width):
    rows, units = term.shape
    half = width // 8

    def at(start):
        return pl.BlockSpec((half, units), lambda i: (jnp.clip(i - start, 0, 1), 0))

    def tile(start, jump):
        return pl.BlockSpec(
            (half, rows), lambda i: (start + i % 2 + jnp.where(i < 2, 2 * jump, 0), 0)
        )

    return kernel_call(
        pair_grad_kernel,
        (shape(2 * half, units, BF16), shape(2 * half, units, F32)),
        grid=(4,),
        in_specs=[tile(first, gap), tile(other_first, 1)]
        + [pl.BlockSpec((rows, units), lambda i: (0, 0))] * 2,
        out_specs=(at(0), at(2)),
    )(turned, other_turned, term, other_term)


def back_kernel(scaled_ref, d_gate_ref, d_up_ref, dots_ref, *refs):
    downs, gate_ups, out_ref = refs[:5], refs[5:10], refs[10]
    units = scaled_ref.shape[1]
    width = (out_ref.shape[1] - SIDE) // 2

    def product(term, weight):
        return lax.dot_general(term[...], weight, ACROSS, preferred_element_type=F32)

    start = 0
    for down, gate_up in zip(downs, gate_ups):
        depth = down.shape[0]
        out_ref[:, start : start + depth] = product(scaled_ref, down[...]).astype(BF16)
        total = product(d_gate_ref, gate_up[:, :units]) + product(d_up_ref, gate_up[:, units:])
        out_ref[:, width + start : width + start + depth] = total.astype(BF16)
        start += depth
    out_ref[:, 2 * width :] = dots_ref[...]


def back_to_rows(half, scaled, d_gate, d_up, dots, direct, down, gate_up, width):
    units = scaled.shape[1]
    rows = scaled.shape[0] // 2
    depth = width // 4
    term = pl.BlockSpec((rows, units), lambda i: (half, 0))
    corner = [pl.BlockSpec((depth // 2, n * units), lambda i: (0, 0)) for n in (1, 1, 2, 2)]
    return kernel_call(
        back_kernel,
        shape(rows, 2 * width + SIDE, BF16),
        grid=(1,),
        in_specs=[term] * 3
        + [pl.BlockSpec((rows, SIDE), lambda i: (half, 0))]
        + [pl.BlockSpec((depth, units), lambda i: (0, 2))] * 3
        + corner[:2]
        + [pl.BlockSpec((depth, 2 * units), lambda i: (0, 0))] * 3
        + corner[2:],
        out_specs=pl.BlockSpec((rows, 2 * width + SIDE), lambda i: (0, 0)),
    )(scaled, d_gate, d_up, dots, *direct, *down, *direct, *gate_up)


def total_kernel(counts, *refs):
    outs = refs[-len(counts) :]
    for count, out_ref in zip(counts, outs):
        terms, refs = refs[:count], refs[count:]
        out_ref[0] = terms[0][...] + sum(term[...].astype(F32) for term in terms[1:])


def totals(*groups):
    block, units = groups[0][0].shape
    step = block // 2
    rows = pl.BlockSpec((step, units), lambda i: (i, 0))
    counts = [len(group) for group in groups]

    def body(*refs):
        total_kernel(counts, *refs)

    return kernel_call(
        body,
        (jax.ShapeDtypeStruct((1, block, units), F32),) * len(groups),
        grid=(block // step,),
        in_specs=[rows] * sum(counts),
        out_specs=(pl.BlockSpec((1, step, units), lambda i: (0, i, 0)),) * len(groups),
    )(*[term for group in groups for term in group])


def send_corner(from_x, from_y, columns, depth):
    half = depth // 2
    return [send(from_x[:half, columns], TO_Y), send(from_y[half:depth, columns], TO_X)]


def along_line(own, before=((), (), ())):
    slots = [own]
    for wait in before:
        slots.append(send(after(slots[-1], *wait), ALONG_Z))
    return slots


def from_both_cores(own_core, before):
    return own_core, send(after(own_core, before), TO_CORE)


def send_down(for_x, for_y, from_x, from_y):
    half = from_x.shape[0]
    for_x = jnp.concatenate([for_x[:half] + from_y.astype(F32), for_x[half:]])
    for_y = jnp.concatenate([for_y[:half], for_y[half:] + from_x.astype(F32)])
    return send(for_x.astype(BF16), TO_X), send(for_y.astype(BF16), TO_Y)


def swap_cores(own, other, before):
    block = own.shape[0] // 4
    second = send(after(other[block : 2 * block], before), TO_CORE)
    third = send(other[2 * block : 3 * block], TO_CORE)
    rest = send(jnp.concatenate([other[3 * block :], other[:block]]), TO_CORE)
    first = (own[block : 2 * block].astype(F32) + second.astype(F32)).astype(BF16)
    return first, third, rest


def sum_along_line(own, swapped, before):
    block = own.shape[0] // 4
    moving, third, rest = swapped
    for slot, wait in zip((2, 3, 0), before):
        moving = send(after(moving, wait), ALONG_Z)
        if slot:
            piece = third if slot == 2 else rest[:block]
            total = own[slot * block : (slot + 1) * block].astype(F32) + piece.astype(F32)
            moving = (total + moving.astype(F32)).astype(BF16)
    return rest[block:], moving


def after(arrays, *others):
    return lax.optimization_barrier((arrays, others))[0]


def dense_plan(tokens, expert_ids, gate_probs, cotangent, gate_proj, up_proj, down_proj):
    width = tokens.shape[1]
    units = gate_proj.shape[2]

    depth = gate_proj.shape[1]
    weights = (gate_proj[0], up_proj[0], down_proj[0])
    to_x, to_y = weights_and_rows(weights, tokens)
    packed = pack(tokens, cotangent, expert_ids, gate_probs)
    from_x, from_y = send(to_x, TO_X), send(to_y, TO_Y)
    direct = [to_x, from_x, from_y]
    whole = from_both_cores(jnp.concatenate(along_line(packed)), (from_x, from_y))
    side = [side_rows(from_y[depth:], width), side_rows(from_x[depth:], width)]
    gate_up_corner = send_corner(*direct[1:], slice(0, 2 * units), depth)
    down_corner = send_corner(*direct[1:], slice(2 * units, 3 * units), depth)
    early_gate_up = early_products(whole, direct, width, 0, 0, 2 * units)
    early_down = early_products(whole, direct, width, 1, 2 * units, units)
    turned = turn(whole, 14, lambda i: jnp.where(i < 6, i, i + 2))
    extra = along_line(
        jnp.concatenate(side, axis=1), ((), (early_gate_up,), (early_down, turned))
    )
    early_gate_up, early_down, turned, gate_up_corner = lax.optimization_barrier(
        (early_gate_up, early_down, turned, gate_up_corner)
    )

    scaled, for_gate, for_up, hidden = forward(whole, early_gate_up, gate_up_corner, width, units)
    corner_sent = corner_grads(turned, 6, scaled, width)
    corner_x, corner_y = send(corner_sent[0], TO_X), send(corner_sent[1], TO_Y)
    hidden, scaled = after((hidden, scaled), corner_sent)
    d_gate, d_up, dots = backward(whole, early_down, down_corner, for_gate, for_up, hidden, width)
    other_gate = send(d_gate, TO_X)
    other_up = send(d_up, TO_Y)
    extra = jnp.concatenate(extra[:3] + [after(extra[3], down_corner)])
    back_terms = (scaled, d_gate, d_up, dots, direct, down_corner, gate_up_corner, width)
    other_shares = back_to_rows(1, *after(back_terms[:4], extra), *back_terms[4:])
    own_shares = back_to_rows(0, *after(back_terms[:4], other_shares), *back_terms[4:])
    swapped = swap_cores(own_shares, other_shares, (corner_x, corner_y))
    scaled = after(scaled, swapped[0], swapped[2])
    for_x, for_y, down_own = later_grads(turned, 6, scaled, width)
    down_back = send_down(for_x, for_y, corner_x, corner_y)
    other_turned = turn(from_both_cores(extra, corner_x), 8, lambda i: i)
    gate_away, gate_own = pair_grads(turned, 0, 2, other_turned, 4, d_gate, other_gate, width)
    gate_back = send(gate_away, TO_Y)
    up_away, up_own = pair_grads(turned, 0, 1, other_turned, 0, d_up, other_up, width)
    up_back = send(up_away, TO_X)
    down_back = after(down_back, gate_away, up_away)
    arrived, line = sum_along_line(
        own_shares, swapped, (other_turned, (other_gate, other_up), down_back)
    )
    (grad_down,) = totals((down_own, *down_back))
    outs = unpack(own_shares, arrived, line, expert_ids, width)
    gate_back, up_back = after((gate_back, up_back), outs, grad_down)
    grad_gate, grad_up = totals((gate_own, gate_back), (up_own, up_back))
    return (*outs, grad_gate, grad_up, grad_down)


def on_device(tokens, expert_ids, *rest):
    tok_dev, top_count = expert_ids.shape
    experts = lax.axis_size("expert")
    square_and_line = lax.axis_size("dp") == 4 and experts == 8
    if square_and_line and capacity_of(tok_dev, top_count, experts) == tok_dev:
        return dense_plan(tokens, expert_ids, *rest)
    return slot_plan(tokens, expert_ids, *rest)


def solution(mesh):
    by_token = P(AXES, None)
    by_expert = P("expert", "dp", None)
    return jax.shard_map(
        on_device,
        mesh=mesh,
        in_specs=(by_token,) * 4 + (by_expert,) * 3,
        out_specs=(by_token,) * 3 + (by_expert,) * 3,
        check_vma=False,
    )
```

```python
import jax
import jax.numpy as jnp
from jax import lax
from jax.experimental import pallas as pl
from jax.experimental.pallas import tpu as pltpu
from jax.sharding import PartitionSpec as P

AXES = ("dp", "expert")
ACROSS = (((1,), (1,)), ((), ()))
OVER_ROWS = (((0,), (0,)), ((), ()))


def routing_slots(expert_ids, experts):
    onehot = (expert_ids[:, :, None] == jnp.arange(experts, dtype=jnp.int32)[None, None, :]).astype(
        jnp.int32
    )
    per_token = jnp.sum(onehot, axis=1)
    earlier = jnp.cumsum(per_token, axis=0) - per_token
    return jnp.sum(onehot * earlier[:, None, :], axis=2)


def forward_rows(rows, gate_proj, up_proj, down_proj):
    gate_pre = jnp.dot(rows, gate_proj, preferred_element_type=jnp.float32)
    up_pre = jnp.dot(rows, up_proj, preferred_element_type=jnp.float32)
    hidden = (jax.nn.silu(gate_pre) * up_pre).astype(jnp.bfloat16)
    expert_out = lax.dot_general(
        hidden, down_proj, ACROSS, preferred_element_type=jnp.float32
    ).astype(jnp.bfloat16)
    return (expert_out, gate_pre, up_pre, hidden)


def backward_rows(grad_rows, gate_pre, up_pre, gate_proj, up_proj, down_proj):
    d_hidden = jnp.dot(grad_rows, down_proj, preferred_element_type=jnp.float32)
    sigmoid_gate = jax.nn.sigmoid(gate_pre)
    silu_gate = gate_pre * sigmoid_gate
    d_gate = (d_hidden * up_pre * sigmoid_gate * (1.0 + gate_pre * (1.0 - sigmoid_gate))).astype(
        jnp.bfloat16
    )
    d_up = (d_hidden * silu_gate).astype(jnp.bfloat16)
    d_rows = lax.dot_general(d_gate, gate_proj, ACROSS, preferred_element_type=jnp.float32)
    d_rows = d_rows + lax.dot_general(d_up, up_proj, ACROSS, preferred_element_type=jnp.float32)
    return (d_rows.astype(jnp.bfloat16), d_gate, d_up)


def pick_rows(source_rows, position, top_count):
    chosen = jnp.take(source_rows, position.reshape(-1), axis=0)
    return chosen.reshape(position.shape[0], top_count, source_rows.shape[1])


def capacity_of(tok_dev, top_count, experts):
    return min(tok_dev, (tok_dev * top_count * 4 + 3 * experts - 1) // (3 * experts))


def slot_plan(tokens, expert_ids, gate_probs, cotangent, gate_proj, up_proj, down_proj):
    experts = lax.axis_size("expert")
    tok_dev, top_count = expert_ids.shape
    model_width = tokens.shape[1]
    capacity = capacity_of(tok_dev, top_count, experts)
    slot_index = routing_slots(expert_ids, experts)
    position = expert_ids * capacity + slot_index
    placing = (
        position[None, :, :] == jnp.arange(experts * capacity, dtype=jnp.int32)[:, None, None]
    ).astype(jnp.float32)
    placer = jnp.sum(placing, axis=2)
    weighted = jnp.sum(placing * gate_probs[None, :, :], axis=2)
    row_send = (
        jnp.dot(placer.astype(jnp.bfloat16), tokens, preferred_element_type=jnp.float32)
        .astype(jnp.bfloat16)
        .reshape(experts, capacity, model_width)
    )
    grad_send = (
        jnp.dot(weighted, cotangent.astype(jnp.float32), precision=lax.Precision.HIGHEST)
        .astype(jnp.bfloat16)
        .reshape(experts, capacity, model_width)
    )
    full_gate, full_up, full_down = (
        lax.all_gather(gate_proj[0], "dp", axis=0, tiled=True),
        lax.all_gather(up_proj[0], "dp", axis=0, tiled=True),
        lax.all_gather(down_proj[0], "dp", axis=0, tiled=True),
    )

    def exchange(rows):
        return lax.all_to_all(
            rows.reshape(experts, capacity, model_width),
            "expert",
            split_axis=0,
            concat_axis=0,
            tiled=True,
        ).reshape(-1, model_width)

    rows_flat = exchange(row_send)
    expert_out, gate_pre, up_pre, hidden = forward_rows(rows_flat, full_gate, full_up, full_down)
    returned = exchange(expert_out)
    grads_flat = exchange(grad_send)
    d_rows, d_gate, d_up = backward_rows(
        grads_flat, gate_pre, up_pre, full_gate, full_up, full_down
    )
    grad_back = exchange(d_rows)
    picked = pick_rows(returned, position, top_count).astype(jnp.float32)
    mixed = jnp.sum(gate_probs[:, :, None] * picked, axis=1).astype(jnp.bfloat16)
    prob_grads = jnp.sum(cotangent.astype(jnp.float32)[:, None, :] * picked, axis=2)
    picked_grads = pick_rows(grad_back, position, top_count).astype(jnp.float32)
    token_grads = jnp.sum(picked_grads, axis=1).astype(jnp.bfloat16)
    hidden_units = hidden.shape[1]
    gate_term = lax.dot_general(rows_flat, d_gate, OVER_ROWS, preferred_element_type=jnp.float32)
    up_term = lax.dot_general(rows_flat, d_up, OVER_ROWS, preferred_element_type=jnp.float32)
    down_term = lax.dot_general(grads_flat, hidden, OVER_ROWS, preferred_element_type=jnp.float32)
    shares = lax.psum_scatter(
        jnp.concatenate([gate_term, up_term, down_term], axis=1),
        "dp",
        scatter_dimension=0,
        tiled=True,
    )
    grad_gate = shares[:, :hidden_units]
    grad_up = shares[:, hidden_units : 2 * hidden_units]
    grad_down = shares[:, 2 * hidden_units :]
    return (mixed, token_grads, prob_grads, grad_gate[None], grad_up[None], grad_down[None])


TILE = 256
SIDE = 128
F32 = jnp.float32
BF16 = jnp.bfloat16
VMEM = pl.BlockSpec(memory_space=pltpu.VMEM)


RING = (0, 2, 3, 1)


def flat_index(y, x, z, core):
    return ((y * 2 + x) * 4 + z) * 2 + core


def pairs(target):
    return [
        (flat_index(y, x, z, core), flat_index(*target(y, x, z, core)))
        for y in range(2)
        for x in range(2)
        for z in range(4)
        for core in range(2)
    ]


TO_X = pairs(lambda y, x, z, core: (y, 1 - x, z, core))
TO_Y = pairs(lambda y, x, z, core: (1 - y, x, z, core))
TO_CORE = pairs(lambda y, x, z, core: (y, x, z, 1 - core))
ALONG_Z = pairs(lambda y, x, z, core: (y, x, RING[(RING.index(z) + 1) % 4], core))


def send(array, where):
    return lax.ppermute(array, AXES, where)


def kernel_call(body, out_shape, **spec):
    return pl.pallas_call(
        body,
        out_shape=out_shape,
        compiler_params=pltpu.CompilerParams(vmem_limit_bytes=24 * 1024 * 1024),
        cost_estimate=pl.CostEstimate(flops=0, bytes_accessed=0, transcendentals=0),
        **spec,
    )


def shape(rows, columns, dtype):
    return jax.ShapeDtypeStruct((rows, columns), dtype)


def iota(rows, columns, axis):
    return lax.broadcasted_iota(jnp.int32, (rows, columns), axis)


def exact_parts(values, place):
    first = values.astype(BF16).astype(F32)
    rest = values - first
    second = rest.astype(BF16).astype(F32)
    third = rest - second
    parts = jnp.where(place < 8, first, jnp.where(place < 16, second, third))
    return jnp.where(place < 24, parts, 0.0).astype(BF16)


def block_at(relative, block):
    return pl.ds(pl.multiple_of((lax.axis_index("dp") ^ relative) * block, block), block)


def pack_kernel(tokens_ref, cot_ref, ids_ref, probs_ref, out_ref, for_x_ref, for_y_ref):
    rows, width = tokens_ref.shape
    block = width // 4
    for r in range(4):
        there = block_at(r, block)
        out_ref[:, r * block : (r + 1) * block] = tokens_ref[:, there]
        out_ref[:, width + r * block : width + (r + 1) * block] = cot_ref[:, there]
    place = iota(SIDE, rows, 0)
    prob = jnp.zeros((SIDE, rows), F32)
    for k in range(ids_ref.shape[0]):
        prob += jnp.where(place % 8 == ids_ref[k : k + 1, :], probs_ref[k : k + 1, :], 0.0)
    same = (iota(rows, rows, 0) == iota(rows, rows, 1)).astype(BF16)
    turned = lax.dot_general(same, exact_parts(prob, place), ACROSS, preferred_element_type=F32)
    out_ref[:, 2 * width :] = turned.astype(BF16)
    band = rows // 4
    across = for_x_ref.shape[1] // block
    for out, blocks in ((for_x_ref, (1, 3)), (for_y_ref, (2, 3))):
        out[...] = jnp.zeros_like(out)
        for index in range(8):
            down, right = index // across * band, index % across * block
            q = index // 2 * band
            out[down : down + band, right : right + block] = tokens_ref[
                q : q + band, block_at(blocks[index % 2], block)
            ]


def pack(tokens, cotangent, expert_ids, gate_probs, columns):
    rows, width = tokens.shape
    across = columns // (width // 4)
    side = shape(-(-8 // across) * (rows // 4), columns, BF16)
    return kernel_call(
        pack_kernel,
        (shape(rows, 2 * width + SIDE, BF16), side, side),
        in_specs=[VMEM] * 4,
        out_specs=(VMEM,) * 3,
    )(tokens, cotangent, expert_ids.T, gate_probs.T)


def side_rows(sides, rows, width):
    band, block = rows // 4, width // 4
    across = sides.shape[1] // block

    def at(index):
        down, right = index // across * band, index % across * block
        return sides[down : down + band, right : right + block]

    return jnp.concatenate([jnp.concatenate([at(2 * q), at(2 * q + 1)], axis=1) for q in range(4)])


def unpack_kernel(own_ref, core_ref, line_ref, ids_ref, mixed_out, back_out, prob_out):
    rows, width = mixed_out.shape
    block = width // 4

    def total(at):
        return own_ref[:, at].astype(F32) + core_ref[:, at].astype(F32) + line_ref[:, at].astype(F32)

    for r in range(4):
        there = block_at(r, block)
        start = r * block
        mixed_out[:, there] = total(slice(start, start + block)).astype(BF16)
        start += width
        back_out[:, there] = total(slice(start, start + block)).astype(BF16)
    lane = iota(8, SIDE, 1)
    adder = ((lane < 24) & (lane % 8 == iota(8, SIDE, 0))).astype(BF16)
    parts = total(slice(2 * width, 2 * width + SIDE)).astype(BF16)
    by_expert = lax.dot_general(adder, parts, ACROSS, preferred_element_type=F32)
    for k in range(ids_ref.shape[0]):
        hit = iota(8, rows, 0) == ids_ref[k : k + 1, :]
        prob_out[k : k + 1, :] = jnp.sum(jnp.where(hit, by_expert, 0.0), axis=0, keepdims=True)


def unpack(shares, arrived, line, expert_ids, width):
    rows, columns = line.shape
    own = shape(rows, width, BF16)
    ids = expert_ids.T
    first = pl.BlockSpec((rows, columns), lambda i: (0, 0))
    wide = pl.BlockSpec((rows, width), lambda i: (0, 0))
    small = pl.BlockSpec(ids.shape, lambda i: (0, 0))
    mixed, back, prob = kernel_call(
        unpack_kernel,
        (own, own, shape(*ids.shape, F32)),
        grid=(1,),
        in_specs=[first] * 3 + [small],
        out_specs=(wide, wide, small),
    )(shares, arrived, line, ids)
    return mixed, back, prob.T


def turn_kernel(own_ref, other_ref, out_ref):
    rows = own_ref.shape[0]
    out_ref[:, :rows] = own_ref[...].T
    out_ref[:, rows:] = other_ref[...].T


def turn(both, tiles, place_of):
    rows = both[0].shape[0]
    return kernel_call(
        turn_kernel,
        shape(tiles * TILE, 2 * rows, BF16),
        grid=(tiles,),
        in_specs=[pl.BlockSpec((rows, TILE), lambda i: (0, place_of(i)))] * 2,
        out_specs=pl.BlockSpec((TILE, 2 * rows), lambda i: (i, 0)),
    )(*both)


def times_pieces(rows_ref, pieces):
    total, start = None, 0
    for piece in pieces:
        depth = piece.shape[0]
        term = jnp.dot(rows_ref[:, start : start + depth], piece[...], preferred_element_type=F32)
        total = term if total is None else total + term
        start += depth
    return total


def early_kernel(own_rows, other_rows, own_ref, x_ref, y_ref, out_ref):
    half = own_rows.shape[0]
    out_ref[:half] = times_pieces(own_rows, (own_ref, x_ref, y_ref))
    out_ref[half:] = times_pieces(other_rows, (own_ref, x_ref, y_ref))


def early_products(whole, direct, width, which, columns):
    half = whole[0].shape[0]
    piece = pl.BlockSpec((width // 4, TILE), lambda j: (0, j))
    return kernel_call(
        early_kernel,
        shape(2 * half, columns, F32),
        grid=(columns // TILE,),
        in_specs=[pl.BlockSpec((half, width), lambda j: (0, which))] * 2 + [piece] * 3,
        out_specs=pl.BlockSpec((2 * half, TILE), lambda j: (0, j)),
    )(*whole, *direct)


def forward_kernel(*refs):
    both_rows, both_parts, earlies, gates, ups = (refs[i : i + 2] for i in range(0, 10, 2))
    scaled_ref, for_gate_ref, for_up_ref, hidden_ref = refs[10:]
    half = both_rows[0].shape[0]
    for index in range(2):
        at = slice(index * half, (index + 1) * half)
        gate_pre = earlies[0][at] + times_pieces(both_rows[index], gates)
        up_pre = earlies[1][at] + times_pieces(both_rows[index], ups)
        lane = iota(half, SIDE, 1)
        mine = (lane < 24) & (lane % 8 == lax.axis_index("expert"))
        parts = both_parts[index][...].astype(F32)
        prob = jnp.sum(jnp.where(mine, parts, 0.0), axis=1, keepdims=True)
        sigmoid_gate = 1.0 / (1.0 + jnp.exp(-gate_pre))
        silu_gate = gate_pre * sigmoid_gate
        hidden = silu_gate * up_pre
        hidden_ref[at] = hidden
        scaled_ref[at] = (hidden * prob).astype(BF16)
        slope = sigmoid_gate * (1.0 + gate_pre * (1.0 - sigmoid_gate))
        for_gate_ref[at] = prob * (up_pre * slope)
        for_up_ref[at] = prob * silu_gate


def forward(whole, early, corner, width, units):
    half = whole[0].shape[0]
    rows = 2 * half
    steps = units // TILE
    block = width // 4
    tile = pl.BlockSpec((rows, TILE), lambda j: (0, j))
    next_tile = pl.BlockSpec((rows, TILE), lambda j: (0, steps + j))
    return kernel_call(
        forward_kernel,
        (shape(rows, units, BF16),) + (shape(rows, units, F32),) * 3,
        grid=(steps,),
        in_specs=[pl.BlockSpec((half, block), lambda j: (0, 3))] * 2
        + [pl.BlockSpec((half, SIDE), lambda j: (0, 2 * width // SIDE))] * 2
        + [tile, next_tile]
        + [pl.BlockSpec((block // 2, TILE), lambda j: (0, j))] * 2
        + [pl.BlockSpec((block // 2, TILE), lambda j: (0, steps + j))] * 2,
        out_specs=(tile,) * 4,
    )(*whole, *whole, early, early, *corner, *corner)


def backward_kernel(own_ref, other_ref, early_ref, first_ref, last_ref, *refs):
    for_gate_ref, for_up_ref, hidden_ref, d_gate_ref, d_up_ref, dots_ref, sum_ref = refs
    step = pl.program_id(0)
    half = own_ref.shape[0]

    @pl.when(step == 0)
    def _():
        sum_ref[...] = jnp.zeros_like(sum_ref)

    for index, grads_ref in enumerate((own_ref, other_ref)):
        at = slice(index * half, (index + 1) * half)
        raw = early_ref[at] + times_pieces(grads_ref, (first_ref, last_ref))
        d_gate_ref[at] = (raw * for_gate_ref[at]).astype(BF16)
        d_up_ref[at] = (raw * for_up_ref[at]).astype(BF16)
        sum_ref[at] += jnp.sum(raw * hidden_ref[at], axis=1, keepdims=True)

    @pl.when(step == pl.num_programs(0) - 1)
    def _():
        lane = iota(2 * half, SIDE, 1)
        mine = lane % 8 == lax.axis_index("expert")
        dots_ref[...] = exact_parts(jnp.where(mine, sum_ref[...], 0.0), lane)


def backward(whole, early, corner, for_gate, for_up, hidden, width):
    rows, units = hidden.shape
    steps = units // TILE
    block = width // 4
    tile = pl.BlockSpec((rows, TILE), lambda j: (0, j))
    return kernel_call(
        backward_kernel,
        (shape(rows, units, BF16),) * 2 + (shape(rows, SIDE, BF16),),
        grid=(steps,),
        in_specs=[pl.BlockSpec((rows // 2, block), lambda j: (0, 7))] * 2
        + [tile]
        + [pl.BlockSpec((block // 2, TILE), lambda j: (0, j))] * 2
        + [tile] * 3,
        out_specs=(tile, tile, pl.BlockSpec((rows, SIDE), lambda j: (0, 0))),
        scratch_shapes=[pltpu.VMEM((rows, 1), F32)],
    )(*whole, early, *corner, for_gate, for_up, hidden)


def corner_grad_kernel(turned_ref, term_ref, to_x, to_y):
    step = pl.program_id(0)
    part = jnp.dot(turned_ref[...], term_ref[...], preferred_element_type=F32).astype(BF16)

    @pl.when(step == 0)
    def _():
        to_x[...] = part

    @pl.when(step == 1)
    def _():
        to_y[...] = part


def corner_grads(turned, first, term, width):
    rows, units = term.shape
    half = width // 8
    once = pl.BlockSpec((half, units), lambda i: (0, 0))
    return kernel_call(
        corner_grad_kernel,
        (shape(half, units, BF16),) * 2,
        grid=(2,),
        in_specs=[
            pl.BlockSpec((half, rows), lambda i: (first + 7 - i, 0)),
            pl.BlockSpec((rows, units), lambda i: (0, 0)),
        ],
        out_specs=(once, once),
    )(turned, term)


def later_grad_kernel(turned_ref, term_ref, for_x, for_y, own):
    step = pl.program_id(0)
    part = jnp.dot(turned_ref[...], term_ref[...], preferred_element_type=F32)

    for place, out in enumerate((for_x, for_y, own)):

        @pl.when(step // 2 == place)
        def _(out=out):
            out[...] = part


def later_grads(turned, first, term, width):
    rows, units = term.shape
    half = width // 8

    def at(start):
        return pl.BlockSpec((half, units), lambda i: (jnp.clip(i - start, 0, 1), 0))

    return kernel_call(
        later_grad_kernel,
        (shape(2 * half, units, F32),) * 3,
        grid=(6,),
        in_specs=[
            pl.BlockSpec((half, rows), lambda i: (first + (i + 2) % 6, 0)),
            pl.BlockSpec((rows, units), lambda i: (0, 0)),
        ],
        out_specs=(at(0), at(2), at(4)),
    )(turned, term)


def pair_grad_kernel(turned_ref, other_turned_ref, term_ref, other_term_ref, away, own):
    step = pl.program_id(0)
    part = jnp.dot(turned_ref[...], term_ref[...], preferred_element_type=F32)
    part += jnp.dot(other_turned_ref[...], other_term_ref[...], preferred_element_type=F32)

    @pl.when(step < 2)
    def _():
        away[...] = part.astype(BF16)

    @pl.when(step >= 2)
    def _():
        own[...] = part


def pair_grads(turned, first, gap, other_turned, other_first, term, other_term, width):
    rows, units = term.shape
    half = width // 8

    def at(start):
        return pl.BlockSpec((half, units), lambda i: (jnp.clip(i - start, 0, 1), 0))

    def tile(start, jump):
        return pl.BlockSpec(
            (half, rows), lambda i: (start + i % 2 + jnp.where(i < 2, 2 * jump, 0), 0)
        )

    return kernel_call(
        pair_grad_kernel,
        (shape(2 * half, units, BF16), shape(2 * half, units, F32)),
        grid=(4,),
        in_specs=[tile(first, gap), tile(other_first, 1)]
        + [pl.BlockSpec((rows, units), lambda i: (0, 0))] * 2,
        out_specs=(at(0), at(2)),
    )(turned, other_turned, term, other_term)


def back_kernel(scaled_ref, d_gate_ref, d_up_ref, dots_ref, *refs):
    downs, gate_ups, out_ref = refs[:5], refs[5:10], refs[10]
    units = scaled_ref.shape[1]
    width = (out_ref.shape[1] - SIDE) // 2

    def product(term, weight):
        return lax.dot_general(term[...], weight, ACROSS, preferred_element_type=F32)

    start = 0
    for down, gate_up in zip(downs, gate_ups):
        depth = down.shape[0]
        out_ref[:, start : start + depth] = product(scaled_ref, down[...]).astype(BF16)
        total = product(d_gate_ref, gate_up[:, :units]) + product(d_up_ref, gate_up[:, units:])
        out_ref[:, width + start : width + start + depth] = total.astype(BF16)
        start += depth
    out_ref[:, 2 * width :] = dots_ref[...]


def back_to_rows(half, scaled, d_gate, d_up, dots, downs, gate_ups, width):
    units = scaled.shape[1]
    rows = scaled.shape[0] // 2
    depth = width // 4
    term = pl.BlockSpec((rows, units), lambda i: (half, 0))

    def pieces(columns):
        return [
            pl.BlockSpec((part, columns), lambda i: (0, 0))
            for part in (depth, depth, depth, depth // 2, depth // 2)
        ]

    return kernel_call(
        back_kernel,
        shape(rows, 2 * width + SIDE, BF16),
        grid=(1,),
        in_specs=[term] * 3
        + [pl.BlockSpec((rows, SIDE), lambda i: (half, 0))]
        + pieces(units)
        + pieces(2 * units),
        out_specs=pl.BlockSpec((rows, 2 * width + SIDE), lambda i: (0, 0)),
    )(scaled, d_gate, d_up, dots, *downs, *gate_ups)


def total_kernel(counts, *refs):
    outs = refs[-len(counts) :]
    for count, out_ref in zip(counts, outs):
        terms, refs = refs[:count], refs[count:]
        out_ref[0] = terms[0][...] + sum(term[...].astype(F32) for term in terms[1:])


def totals(*groups):
    block, units = groups[0][0].shape
    step = block // 2
    rows = pl.BlockSpec((step, units), lambda i: (i, 0))
    counts = [len(group) for group in groups]

    def body(*refs):
        total_kernel(counts, *refs)

    return kernel_call(
        body,
        (jax.ShapeDtypeStruct((1, block, units), F32),) * len(groups),
        grid=(block // step,),
        in_specs=[rows] * sum(counts),
        out_specs=(pl.BlockSpec((1, step, units), lambda i: (0, i, 0)),) * len(groups),
    )(*[term for group in groups for term in group])


def send_corner(from_x, from_y, depth):
    half = depth // 2
    return [send(from_x[:half], TO_Y), send(from_y[half:depth], TO_X)]


def along_line(own, before=((), (), ())):
    slots = [own]
    for wait in before:
        slots.append(send(after(slots[-1], *wait), ALONG_Z))
    return slots


def from_both_cores(own_core, before):
    return own_core, send(after(own_core, before), TO_CORE)


def send_down(for_x, for_y, from_x, from_y):
    half = from_x.shape[0]
    for_x = jnp.concatenate([for_x[:half] + from_y.astype(F32), for_x[half:]])
    for_y = jnp.concatenate([for_y[:half], for_y[half:] + from_x.astype(F32)])
    return send(for_x.astype(BF16), TO_X), send(for_y.astype(BF16), TO_Y)


def swap_cores(own, other, before):
    block = own.shape[0] // 4
    second = send(after(other[block : 2 * block], before), TO_CORE)
    third = send(other[2 * block : 3 * block], TO_CORE)
    rest = send(jnp.concatenate([other[3 * block :], other[:block]]), TO_CORE)
    first = (own[block : 2 * block].astype(F32) + second.astype(F32)).astype(BF16)
    return first, third, rest


def sum_along_line(own, swapped, before):
    block = own.shape[0] // 4
    moving, third, rest = swapped
    for slot, wait in zip((2, 3, 0), before):
        moving = send(after(moving, wait), ALONG_Z)
        if slot:
            piece = third if slot == 2 else rest[:block]
            total = own[slot * block : (slot + 1) * block].astype(F32) + piece.astype(F32)
            moving = (total + moving.astype(F32)).astype(BF16)
    return rest[block:], moving


def after(arrays, *others):
    return lax.optimization_barrier((arrays, others))[0]


def dense_plan(tokens, expert_ids, gate_probs, cotangent, gate_proj, up_proj, down_proj):
    width = tokens.shape[1]
    units = gate_proj.shape[2]

    depth = gate_proj.shape[1]
    rows = tokens.shape[0]
    down = [down_proj[0], send(down_proj[0], TO_X), send(down_proj[0], TO_Y)]
    packed, for_x, for_y = pack(tokens, cotangent, expert_ids, gate_probs, 2 * units)
    gate_up = jnp.concatenate([gate_proj[0], up_proj[0]], axis=1)
    gate_up = lax.optimization_barrier(gate_up)
    to_x, to_y = jnp.concatenate([gate_up, for_x]), jnp.concatenate([gate_up, for_y])
    from_x, from_y = send(to_x, TO_X), send(to_y, TO_Y)
    direct = [to_x, from_x, from_y]
    line = along_line(packed, ((), (down,), ()))
    whole = from_both_cores(jnp.concatenate(line), (from_x, from_y))
    side = [side_rows(from_y[depth:], rows, width), side_rows(from_x[depth:], rows, width)]
    gate_up_corner = send_corner(from_x, from_y, depth)
    down_corner = send_corner(*down[1:], depth)
    early_gate_up = early_products(whole, direct, width, 0, 2 * units)
    early_down = early_products(whole, down, width, 1, units)
    turned = turn(whole, 14, lambda i: jnp.where(i < 6, i, i + 2))
    extra = along_line(
        jnp.concatenate(side, axis=1), ((), (early_gate_up,), (early_down, turned))
    )
    early_gate_up, early_down, turned, gate_up_corner = lax.optimization_barrier(
        (early_gate_up, early_down, turned, gate_up_corner)
    )

    scaled, for_gate, for_up, hidden = forward(whole, early_gate_up, gate_up_corner, width, units)
    corner_sent = corner_grads(turned, 6, scaled, width)
    corner_x, corner_y = send(corner_sent[0], TO_X), send(corner_sent[1], TO_Y)
    hidden, scaled = after((hidden, scaled), corner_sent)
    d_gate, d_up, dots = backward(whole, early_down, down_corner, for_gate, for_up, hidden, width)
    other_gate = send(d_gate, TO_X)
    other_up = send(d_up, TO_Y)
    extra = jnp.concatenate(extra[:3] + [after(extra[3], down_corner)])
    pieces = (down + down_corner, direct + gate_up_corner)
    back_terms = (scaled, d_gate, d_up, dots, *pieces, width)
    other_shares = back_to_rows(1, *after(back_terms[:4], extra), *back_terms[4:])
    own_shares = back_to_rows(0, *after(back_terms[:4], other_shares), *back_terms[4:])
    swapped = swap_cores(own_shares, other_shares, (corner_x, corner_y))
    scaled = after(scaled, swapped[0], swapped[2])
    for_x, for_y, down_own = later_grads(turned, 6, scaled, width)
    down_back = send_down(for_x, for_y, corner_x, corner_y)
    other_turned = turn(from_both_cores(extra, corner_x), 8, lambda i: i)
    gate_away, gate_own = pair_grads(turned, 0, 2, other_turned, 4, d_gate, other_gate, width)
    gate_back = send(gate_away, TO_Y)
    up_away, up_own = pair_grads(turned, 0, 1, other_turned, 0, d_up, other_up, width)
    up_back = send(up_away, TO_X)
    down_back = after(down_back, gate_away, up_away)
    arrived, line = sum_along_line(
        own_shares, swapped, (other_turned, (other_gate, other_up), down_back)
    )
    (grad_down,) = totals((down_own, *down_back))
    outs = unpack(own_shares, arrived, line, expert_ids, width)
    gate_back, up_back = after((gate_back, up_back), outs, grad_down)
    grad_gate, grad_up = totals((gate_own, gate_back), (up_own, up_back))
    return (*outs, grad_gate, grad_up, grad_down)


def on_device(tokens, expert_ids, *rest):
    tok_dev, top_count = expert_ids.shape
    experts = lax.axis_size("expert")
    square_and_line = lax.axis_size("dp") == 4 and experts == 8
    if square_and_line and capacity_of(tok_dev, top_count, experts) == tok_dev:
        return dense_plan(tokens, expert_ids, *rest)
    return slot_plan(tokens, expert_ids, *rest)


def solution(mesh):
    by_token = P(AXES, None)
    by_expert = P("expert", "dp", None)
    return jax.shard_map(
        on_device,
        mesh=mesh,
        in_specs=(by_token,) * 4 + (by_expert,) * 3,
        out_specs=(by_token,) * 3 + (by_expert,) * 3,
        check_vma=False,
    )
```

```python
import jax
import jax.numpy as jnp
from jax import lax
from jax.experimental import pallas as pl
from jax.experimental.pallas import tpu as pltpu
from jax.sharding import PartitionSpec as P

AXES = ("dp", "expert")
ACROSS = (((1,), (1,)), ((), ()))
OVER_ROWS = (((0,), (0,)), ((), ()))


def routing_slots(expert_ids, experts):
    onehot = (expert_ids[:, :, None] == jnp.arange(experts, dtype=jnp.int32)[None, None, :]).astype(
        jnp.int32
    )
    per_token = jnp.sum(onehot, axis=1)
    earlier = jnp.cumsum(per_token, axis=0) - per_token
    return jnp.sum(onehot * earlier[:, None, :], axis=2)


def forward_rows(rows, gate_proj, up_proj, down_proj):
    gate_pre = jnp.dot(rows, gate_proj, preferred_element_type=jnp.float32)
    up_pre = jnp.dot(rows, up_proj, preferred_element_type=jnp.float32)
    hidden = (jax.nn.silu(gate_pre) * up_pre).astype(jnp.bfloat16)
    expert_out = lax.dot_general(
        hidden, down_proj, ACROSS, preferred_element_type=jnp.float32
    ).astype(jnp.bfloat16)
    return (expert_out, gate_pre, up_pre, hidden)


def backward_rows(grad_rows, gate_pre, up_pre, gate_proj, up_proj, down_proj):
    d_hidden = jnp.dot(grad_rows, down_proj, preferred_element_type=jnp.float32)
    sigmoid_gate = jax.nn.sigmoid(gate_pre)
    silu_gate = gate_pre * sigmoid_gate
    d_gate = (d_hidden * up_pre * sigmoid_gate * (1.0 + gate_pre * (1.0 - sigmoid_gate))).astype(
        jnp.bfloat16
    )
    d_up = (d_hidden * silu_gate).astype(jnp.bfloat16)
    d_rows = lax.dot_general(d_gate, gate_proj, ACROSS, preferred_element_type=jnp.float32)
    d_rows = d_rows + lax.dot_general(d_up, up_proj, ACROSS, preferred_element_type=jnp.float32)
    return (d_rows.astype(jnp.bfloat16), d_gate, d_up)


def pick_rows(source_rows, position, top_count):
    chosen = jnp.take(source_rows, position.reshape(-1), axis=0)
    return chosen.reshape(position.shape[0], top_count, source_rows.shape[1])


def capacity_of(tok_dev, top_count, experts):
    return min(tok_dev, (tok_dev * top_count * 4 + 3 * experts - 1) // (3 * experts))


def slot_plan(tokens, expert_ids, gate_probs, cotangent, gate_proj, up_proj, down_proj):
    experts = lax.axis_size("expert")
    tok_dev, top_count = expert_ids.shape
    model_width = tokens.shape[1]
    capacity = capacity_of(tok_dev, top_count, experts)
    slot_index = routing_slots(expert_ids, experts)
    position = expert_ids * capacity + slot_index
    placing = (
        position[None, :, :] == jnp.arange(experts * capacity, dtype=jnp.int32)[:, None, None]
    ).astype(jnp.float32)
    placer = jnp.sum(placing, axis=2)
    weighted = jnp.sum(placing * gate_probs[None, :, :], axis=2)
    row_send = (
        jnp.dot(placer.astype(jnp.bfloat16), tokens, preferred_element_type=jnp.float32)
        .astype(jnp.bfloat16)
        .reshape(experts, capacity, model_width)
    )
    grad_send = (
        jnp.dot(weighted, cotangent.astype(jnp.float32), precision=lax.Precision.HIGHEST)
        .astype(jnp.bfloat16)
        .reshape(experts, capacity, model_width)
    )
    full_gate, full_up, full_down = (
        lax.all_gather(gate_proj[0], "dp", axis=0, tiled=True),
        lax.all_gather(up_proj[0], "dp", axis=0, tiled=True),
        lax.all_gather(down_proj[0], "dp", axis=0, tiled=True),
    )

    def exchange(rows):
        return lax.all_to_all(
            rows.reshape(experts, capacity, model_width),
            "expert",
            split_axis=0,
            concat_axis=0,
            tiled=True,
        ).reshape(-1, model_width)

    rows_flat = exchange(row_send)
    expert_out, gate_pre, up_pre, hidden = forward_rows(rows_flat, full_gate, full_up, full_down)
    returned = exchange(expert_out)
    grads_flat = exchange(grad_send)
    d_rows, d_gate, d_up = backward_rows(
        grads_flat, gate_pre, up_pre, full_gate, full_up, full_down
    )
    grad_back = exchange(d_rows)
    picked = pick_rows(returned, position, top_count).astype(jnp.float32)
    mixed = jnp.sum(gate_probs[:, :, None] * picked, axis=1).astype(jnp.bfloat16)
    prob_grads = jnp.sum(cotangent.astype(jnp.float32)[:, None, :] * picked, axis=2)
    picked_grads = pick_rows(grad_back, position, top_count).astype(jnp.float32)
    token_grads = jnp.sum(picked_grads, axis=1).astype(jnp.bfloat16)
    hidden_units = hidden.shape[1]
    gate_term = lax.dot_general(rows_flat, d_gate, OVER_ROWS, preferred_element_type=jnp.float32)
    up_term = lax.dot_general(rows_flat, d_up, OVER_ROWS, preferred_element_type=jnp.float32)
    down_term = lax.dot_general(grads_flat, hidden, OVER_ROWS, preferred_element_type=jnp.float32)
    shares = lax.psum_scatter(
        jnp.concatenate([gate_term, up_term, down_term], axis=1),
        "dp",
        scatter_dimension=0,
        tiled=True,
    )
    grad_gate = shares[:, :hidden_units]
    grad_up = shares[:, hidden_units : 2 * hidden_units]
    grad_down = shares[:, 2 * hidden_units :]
    return (mixed, token_grads, prob_grads, grad_gate[None], grad_up[None], grad_down[None])


TILE = 256
SIDE = 128
F32 = jnp.float32
BF16 = jnp.bfloat16
VMEM = pl.BlockSpec(memory_space=pltpu.VMEM)


RING = (0, 2, 3, 1)


def flat_index(y, x, z, core):
    return ((y * 2 + x) * 4 + z) * 2 + core


def pairs(target):
    return [
        (flat_index(y, x, z, core), flat_index(*target(y, x, z, core)))
        for y in range(2)
        for x in range(2)
        for z in range(4)
        for core in range(2)
    ]


TO_X = pairs(lambda y, x, z, core: (y, 1 - x, z, core))
TO_Y = pairs(lambda y, x, z, core: (1 - y, x, z, core))
TO_CORE = pairs(lambda y, x, z, core: (y, x, z, 1 - core))
ALONG_Z = pairs(lambda y, x, z, core: (y, x, RING[(RING.index(z) + 1) % 4], core))


def send(array, where):
    return lax.ppermute(array, AXES, where)


def kernel_call(body, out_shape, **spec):
    return pl.pallas_call(
        body,
        out_shape=out_shape,
        compiler_params=pltpu.CompilerParams(vmem_limit_bytes=24 * 1024 * 1024),
        cost_estimate=pl.CostEstimate(flops=0, bytes_accessed=0, transcendentals=0),
        **spec,
    )


def shape(rows, columns, dtype):
    return jax.ShapeDtypeStruct((rows, columns), dtype)


def iota(rows, columns, axis):
    return lax.broadcasted_iota(jnp.int32, (rows, columns), axis)


def exact_parts(values, place):
    first = values.astype(BF16).astype(F32)
    rest = values - first
    second = rest.astype(BF16).astype(F32)
    third = rest - second
    parts = jnp.where(place < 8, first, jnp.where(place < 16, second, third))
    return jnp.where(place < 24, parts, 0.0).astype(BF16)


def block_at(relative, block):
    return pl.ds(pl.multiple_of((lax.axis_index("dp") ^ relative) * block, block), block)


def pack_kernel(tokens_ref, cot_ref, ids_ref, probs_ref, out_ref, for_x_ref, for_y_ref):
    rows, width = tokens_ref.shape
    block = width // 4
    for r in range(4):
        there = block_at(r, block)
        out_ref[:, r * block : (r + 1) * block] = tokens_ref[:, there]
        out_ref[:, width + r * block : width + (r + 1) * block] = cot_ref[:, there]
    place = iota(SIDE, rows, 0)
    prob = jnp.zeros((SIDE, rows), F32)
    for k in range(ids_ref.shape[0]):
        prob += jnp.where(place % 8 == ids_ref[k : k + 1, :], probs_ref[k : k + 1, :], 0.0)
    same = (iota(rows, rows, 0) == iota(rows, rows, 1)).astype(BF16)
    turned = lax.dot_general(same, exact_parts(prob, place), ACROSS, preferred_element_type=F32)
    out_ref[:, 2 * width :] = turned.astype(BF16)
    band = rows // 4
    across = for_x_ref.shape[1] // block
    for out, blocks in ((for_x_ref, (1, 3)), (for_y_ref, (2, 3))):
        out[...] = jnp.zeros_like(out)
        for index in range(8):
            down, right = index // across * band, index % across * block
            q = index // 2 * band
            out[down : down + band, right : right + block] = tokens_ref[
                q : q + band, block_at(blocks[index % 2], block)
            ]


def pack(tokens, cotangent, expert_ids, gate_probs, columns):
    rows, width = tokens.shape
    across = columns // (width // 4)
    side = shape(-(-8 // across) * (rows // 4), columns, BF16)
    return kernel_call(
        pack_kernel,
        (shape(rows, 2 * width + SIDE, BF16), side, side),
        in_specs=[VMEM] * 4,
        out_specs=(VMEM,) * 3,
    )(tokens, cotangent, expert_ids.T, gate_probs.T)


def side_rows(sides, rows, width):
    band, block = rows // 4, width // 4
    across = sides.shape[1] // block

    def at(index):
        down, right = index // across * band, index % across * block
        return sides[down : down + band, right : right + block]

    return jnp.concatenate([jnp.concatenate([at(2 * q), at(2 * q + 1)], axis=1) for q in range(4)])


def unpack_kernel(own_ref, core_ref, line_ref, ids_ref, mixed_out, back_out, prob_out):
    rows, width = mixed_out.shape
    block = width // 4

    def total(at):
        return own_ref[:, at].astype(F32) + core_ref[:, at].astype(F32) + line_ref[:, at].astype(F32)

    for r in range(4):
        there = block_at(r, block)
        start = r * block
        mixed_out[:, there] = total(slice(start, start + block)).astype(BF16)
        start += width
        back_out[:, there] = total(slice(start, start + block)).astype(BF16)
    lane = iota(8, SIDE, 1)
    adder = ((lane < 24) & (lane % 8 == iota(8, SIDE, 0))).astype(BF16)
    parts = total(slice(2 * width, 2 * width + SIDE)).astype(BF16)
    by_expert = lax.dot_general(adder, parts, ACROSS, preferred_element_type=F32)
    for k in range(ids_ref.shape[0]):
        hit = iota(8, rows, 0) == ids_ref[k : k + 1, :]
        prob_out[k : k + 1, :] = jnp.sum(jnp.where(hit, by_expert, 0.0), axis=0, keepdims=True)


def unpack(shares, arrived, line, expert_ids, width):
    rows, columns = line.shape
    own = shape(rows, width, BF16)
    ids = expert_ids.T
    first = pl.BlockSpec((rows, columns), lambda i: (0, 0))
    wide = pl.BlockSpec((rows, width), lambda i: (0, 0))
    small = pl.BlockSpec(ids.shape, lambda i: (0, 0))
    mixed, back, prob = kernel_call(
        unpack_kernel,
        (own, own, shape(*ids.shape, F32)),
        grid=(1,),
        in_specs=[first] * 3 + [small],
        out_specs=(wide, wide, small),
    )(shares, arrived, line, ids)
    return mixed, back, prob.T


def turn_kernel(own_ref, other_ref, out_ref):
    rows = own_ref.shape[0]
    out_ref[:, :rows] = own_ref[...].T
    out_ref[:, rows:] = other_ref[...].T


def turn(both, tiles, place_of):
    rows = both[0].shape[0]
    return kernel_call(
        turn_kernel,
        shape(tiles * TILE, 2 * rows, BF16),
        grid=(tiles,),
        in_specs=[pl.BlockSpec((rows, TILE), lambda i: (0, place_of(i)))] * 2,
        out_specs=pl.BlockSpec((TILE, 2 * rows), lambda i: (i, 0)),
    )(*both)


def times_pieces(rows_ref, pieces):
    total, start = None, 0
    for piece in pieces:
        depth = piece.shape[0]
        term = jnp.dot(rows_ref[:, start : start + depth], piece[...], preferred_element_type=F32)
        total = term if total is None else total + term
        start += depth
    return total


def early_kernel(own_rows, other_rows, own_ref, x_ref, y_ref, out_ref):
    half = own_rows.shape[0]
    out_ref[:half] = times_pieces(own_rows, (own_ref, x_ref, y_ref))
    out_ref[half:] = times_pieces(other_rows, (own_ref, x_ref, y_ref))


def early_products(whole, direct, width, which, columns):
    half = whole[0].shape[0]
    piece = pl.BlockSpec((width // 4, TILE), lambda j: (0, j))
    return kernel_call(
        early_kernel,
        shape(2 * half, columns, F32),
        grid=(columns // TILE,),
        in_specs=[pl.BlockSpec((half, width), lambda j: (0, which))] * 2 + [piece] * 3,
        out_specs=pl.BlockSpec((2 * half, TILE), lambda j: (0, j)),
    )(*whole, *direct)


def forward_kernel(*refs):
    both_rows, both_parts, earlies, gates, ups = (refs[i : i + 2] for i in range(0, 10, 2))
    scaled_ref, for_gate_ref, for_up_ref, hidden_ref = refs[10:]
    half = both_rows[0].shape[0]
    for index in range(2):
        at = slice(index * half, (index + 1) * half)
        gate_pre = earlies[0][at] + times_pieces(both_rows[index], gates)
        up_pre = earlies[1][at] + times_pieces(both_rows[index], ups)
        lane = iota(half, SIDE, 1)
        mine = (lane < 24) & (lane % 8 == lax.axis_index("expert"))
        parts = both_parts[index][...].astype(F32)
        prob = jnp.sum(jnp.where(mine, parts, 0.0), axis=1, keepdims=True)
        sigmoid_gate = 1.0 / (1.0 + jnp.exp(-gate_pre))
        silu_gate = gate_pre * sigmoid_gate
        hidden = silu_gate * up_pre
        hidden_ref[at] = hidden
        scaled_ref[at] = (hidden * prob).astype(BF16)
        slope = sigmoid_gate * (1.0 + gate_pre * (1.0 - sigmoid_gate))
        for_gate_ref[at] = prob * (up_pre * slope)
        for_up_ref[at] = prob * silu_gate


def forward(whole, early, corner, width, units):
    half = whole[0].shape[0]
    rows = 2 * half
    steps = units // TILE
    block = width // 4
    tile = pl.BlockSpec((rows, TILE), lambda j: (0, j))
    next_tile = pl.BlockSpec((rows, TILE), lambda j: (0, steps + j))
    return kernel_call(
        forward_kernel,
        (shape(rows, units, BF16),) + (shape(rows, units, F32),) * 3,
        grid=(steps,),
        in_specs=[pl.BlockSpec((half, block), lambda j: (0, 3))] * 2
        + [pl.BlockSpec((half, SIDE), lambda j: (0, 2 * width // SIDE))] * 2
        + [tile, next_tile]
        + [pl.BlockSpec((block // 2, TILE), lambda j: (0, j))] * 2
        + [pl.BlockSpec((block // 2, TILE), lambda j: (0, steps + j))] * 2,
        out_specs=(tile,) * 4,
    )(*whole, *whole, early, early, *corner, *corner)


def backward_kernel(own_ref, other_ref, early_ref, first_ref, last_ref, *refs):
    for_gate_ref, for_up_ref, hidden_ref, d_gate_ref, d_up_ref, dots_ref, sum_ref = refs
    step = pl.program_id(0)
    half = own_ref.shape[0]

    @pl.when(step == 0)
    def _():
        sum_ref[...] = jnp.zeros_like(sum_ref)

    for index, grads_ref in enumerate((own_ref, other_ref)):
        at = slice(index * half, (index + 1) * half)
        raw = early_ref[at] + times_pieces(grads_ref, (first_ref, last_ref))
        d_gate_ref[at] = (raw * for_gate_ref[at]).astype(BF16)
        d_up_ref[at] = (raw * for_up_ref[at]).astype(BF16)
        sum_ref[at] += jnp.sum(raw * hidden_ref[at], axis=1, keepdims=True)

    @pl.when(step == pl.num_programs(0) - 1)
    def _():
        lane = iota(2 * half, SIDE, 1)
        mine = lane % 8 == lax.axis_index("expert")
        dots_ref[...] = exact_parts(jnp.where(mine, sum_ref[...], 0.0), lane)


def backward(whole, early, corner, for_gate, for_up, hidden, width):
    rows, units = hidden.shape
    steps = units // TILE
    block = width // 4
    tile = pl.BlockSpec((rows, TILE), lambda j: (0, j))
    return kernel_call(
        backward_kernel,
        (shape(rows, units, BF16),) * 2 + (shape(rows, SIDE, BF16),),
        grid=(steps,),
        in_specs=[pl.BlockSpec((rows // 2, block), lambda j: (0, 7))] * 2
        + [tile]
        + [pl.BlockSpec((block // 2, TILE), lambda j: (0, j))] * 2
        + [tile] * 3,
        out_specs=(tile, tile, pl.BlockSpec((rows, SIDE), lambda j: (0, 0))),
        scratch_shapes=[pltpu.VMEM((rows, 1), F32)],
    )(*whole, early, *corner, for_gate, for_up, hidden)


def corner_grad_kernel(turned_ref, term_ref, to_x, to_y):
    step = pl.program_id(0)
    part = jnp.dot(turned_ref[...], term_ref[...], preferred_element_type=F32).astype(BF16)

    @pl.when(step == 0)
    def _():
        to_x[...] = part

    @pl.when(step == 1)
    def _():
        to_y[...] = part


def corner_grads(turned, first, term, width):
    rows, units = term.shape
    half = width // 8
    once = pl.BlockSpec((half, units), lambda i: (0, 0))
    return kernel_call(
        corner_grad_kernel,
        (shape(half, units, BF16),) * 2,
        grid=(2,),
        in_specs=[
            pl.BlockSpec((half, rows), lambda i: (first + 7 - i, 0)),
            pl.BlockSpec((rows, units), lambda i: (0, 0)),
        ],
        out_specs=(once, once),
    )(turned, term)


def later_grad_kernel(turned_ref, term_ref, for_x, for_y, own):
    step = pl.program_id(0)
    part = jnp.dot(turned_ref[...], term_ref[...], preferred_element_type=F32)

    for place, out in enumerate((for_x, for_y, own)):

        @pl.when(step // 2 == place)
        def _(out=out):
            out[...] = part


def later_grads(turned, first, term, width):
    rows, units = term.shape
    half = width // 8

    def at(start):
        return pl.BlockSpec((half, units), lambda i: (jnp.clip(i - start, 0, 1), 0))

    return kernel_call(
        later_grad_kernel,
        (shape(2 * half, units, F32),) * 3,
        grid=(6,),
        in_specs=[
            pl.BlockSpec((half, rows), lambda i: (first + (i + 2) % 6, 0)),
            pl.BlockSpec((rows, units), lambda i: (0, 0)),
        ],
        out_specs=(at(0), at(2), at(4)),
    )(turned, term)


def pair_grad_kernel(turned_ref, other_turned_ref, term_ref, other_term_ref, away, own):
    step = pl.program_id(0)
    part = jnp.dot(turned_ref[...], term_ref[...], preferred_element_type=F32)
    part += jnp.dot(other_turned_ref[...], other_term_ref[...], preferred_element_type=F32)

    @pl.when(step < 2)
    def _():
        away[...] = part.astype(BF16)

    @pl.when(step >= 2)
    def _():
        own[...] = part


def pair_grads(turned, first, gap, other_turned, other_first, term, other_term, width):
    rows, units = term.shape
    half = width // 8

    def at(start):
        return pl.BlockSpec((half, units), lambda i: (jnp.clip(i - start, 0, 1), 0))

    def tile(start, jump):
        return pl.BlockSpec(
            (half, rows), lambda i: (start + i % 2 + jnp.where(i < 2, 2 * jump, 0), 0)
        )

    return kernel_call(
        pair_grad_kernel,
        (shape(2 * half, units, BF16), shape(2 * half, units, F32)),
        grid=(4,),
        in_specs=[tile(first, gap), tile(other_first, 1)]
        + [pl.BlockSpec((rows, units), lambda i: (0, 0))] * 2,
        out_specs=(at(0), at(2)),
    )(turned, other_turned, term, other_term)


def back_kernel(scaled_ref, d_gate_ref, d_up_ref, dots_ref, *refs):
    downs, gate_ups, out_ref = refs[:5], refs[5:10], refs[10]
    units = scaled_ref.shape[1]
    width = (out_ref.shape[1] - SIDE) // 2

    def product(term, weight):
        return lax.dot_general(term[...], weight, ACROSS, preferred_element_type=F32)

    start = 0
    for down, gate_up in zip(downs, gate_ups):
        depth = down.shape[0]
        out_ref[:, start : start + depth] = product(scaled_ref, down[...]).astype(BF16)
        total = product(d_gate_ref, gate_up[:, :units]) + product(d_up_ref, gate_up[:, units:])
        out_ref[:, width + start : width + start + depth] = total.astype(BF16)
        start += depth
    out_ref[:, 2 * width :] = dots_ref[...]


def back_to_rows(half, scaled, d_gate, d_up, dots, downs, gate_ups, width):
    units = scaled.shape[1]
    rows = scaled.shape[0] // 2
    depth = width // 4
    term = pl.BlockSpec((rows, units), lambda i: (half, 0))

    def pieces(columns):
        return [
            pl.BlockSpec((part, columns), lambda i: (0, 0))
            for part in (depth, depth, depth, depth // 2, depth // 2)
        ]

    return kernel_call(
        back_kernel,
        shape(rows, 2 * width + SIDE, BF16),
        grid=(1,),
        in_specs=[term] * 3
        + [pl.BlockSpec((rows, SIDE), lambda i: (half, 0))]
        + pieces(units)
        + pieces(2 * units),
        out_specs=pl.BlockSpec((rows, 2 * width + SIDE), lambda i: (0, 0)),
    )(scaled, d_gate, d_up, dots, *downs, *gate_ups)


def total_kernel(counts, *refs):
    outs = refs[-len(counts) :]
    for count, out_ref in zip(counts, outs):
        terms, refs = refs[:count], refs[count:]
        out_ref[0] = terms[0][...] + sum(term[...].astype(F32) for term in terms[1:])


def totals(*groups):
    block, units = groups[0][0].shape
    step = block // 2
    rows = pl.BlockSpec((step, units), lambda i: (i, 0))
    counts = [len(group) for group in groups]

    def body(*refs):
        total_kernel(counts, *refs)

    return kernel_call(
        body,
        (jax.ShapeDtypeStruct((1, block, units), F32),) * len(groups),
        grid=(block // step,),
        in_specs=[rows] * sum(counts),
        out_specs=(pl.BlockSpec((1, step, units), lambda i: (0, i, 0)),) * len(groups),
    )(*[term for group in groups for term in group])


def send_corner(from_x, from_y, depth):
    half = depth // 2
    return [send(from_x[:half], TO_Y), send(from_y[half:depth], TO_X)]


def along_line(own, before=((), (), ())):
    slots = [own]
    for wait in before:
        slots.append(send(after(slots[-1], *wait), ALONG_Z))
    return slots


def from_both_cores(own_core, before):
    return own_core, send(after(own_core, before), TO_CORE)


def send_down(for_x, for_y, from_x, from_y):
    half = from_x.shape[0]
    for_x = jnp.concatenate([for_x[:half] + from_y.astype(F32), for_x[half:]])
    for_y = jnp.concatenate([for_y[:half], for_y[half:] + from_x.astype(F32)])
    return send(for_x.astype(BF16), TO_X), send(for_y.astype(BF16), TO_Y)


def swap_cores(own, other, before):
    block = own.shape[0] // 4
    second = send(after(other[block : 2 * block], before), TO_CORE)
    third = send(other[2 * block : 3 * block], TO_CORE)
    rest = send(jnp.concatenate([other[3 * block :], other[:block]]), TO_CORE)
    first = (own[block : 2 * block].astype(F32) + second.astype(F32)).astype(BF16)
    return first, third, rest


def sum_along_line(own, swapped, before):
    block = own.shape[0] // 4
    moving, third, rest = swapped
    for slot, wait in zip((2, 3, 0), before):
        moving = send(after(moving, wait), ALONG_Z)
        if slot:
            piece = third if slot == 2 else rest[:block]
            total = own[slot * block : (slot + 1) * block].astype(F32) + piece.astype(F32)
            moving = (total + moving.astype(F32)).astype(BF16)
    return rest[block:], moving


def after(arrays, *others):
    return lax.optimization_barrier((arrays, others))[0]


def dense_plan(tokens, expert_ids, gate_probs, cotangent, gate_proj, up_proj, down_proj):
    width = tokens.shape[1]
    units = gate_proj.shape[2]

    depth = gate_proj.shape[1]
    rows = tokens.shape[0]
    down = [down_proj[0], send(down_proj[0], TO_X), send(down_proj[0], TO_Y)]
    packed, for_x, for_y = pack(tokens, cotangent, expert_ids, gate_probs, 2 * units)
    gate_up = jnp.concatenate([gate_proj[0], up_proj[0]], axis=1)
    gate_up = lax.optimization_barrier(gate_up)
    to_x, to_y = jnp.concatenate([gate_up, for_x]), jnp.concatenate([gate_up, for_y])
    from_x, from_y = send(to_x, TO_X), send(to_y, TO_Y)
    direct = [to_x, from_x, from_y]
    line = along_line(packed, ((), (down,), ()))
    whole = from_both_cores(jnp.concatenate(line), from_y)
    side = [side_rows(from_y[depth:], rows, width), side_rows(from_x[depth:], rows, width)]
    gate_up_corner = send_corner(from_x, from_y, depth)
    down_corner = send_corner(*down[1:], depth)
    early_gate_up = early_products(whole, direct, width, 0, 2 * units)
    early_down = early_products(whole, down, width, 1, units)
    turned = turn(whole, 14, lambda i: jnp.where(i < 6, i, i + 2))
    extra = along_line(
        jnp.concatenate(side, axis=1), ((), (early_gate_up,), (early_down, turned))
    )
    early_gate_up, early_down, turned, gate_up_corner = lax.optimization_barrier(
        (early_gate_up, early_down, turned, gate_up_corner)
    )

    scaled, for_gate, for_up, hidden = forward(whole, early_gate_up, gate_up_corner, width, units)
    corner_sent = corner_grads(turned, 6, scaled, width)
    corner_x, corner_y = send(corner_sent[0], TO_X), send(corner_sent[1], TO_Y)
    hidden, scaled = after((hidden, scaled), corner_sent)
    d_gate, d_up, dots = backward(whole, early_down, down_corner, for_gate, for_up, hidden, width)
    other_gate = send(d_gate, TO_X)
    other_up = send(d_up, TO_Y)
    extra = jnp.concatenate(extra[:3] + [after(extra[3], down_corner)])
    pieces = (down + down_corner, direct + gate_up_corner)
    back_terms = (scaled, d_gate, d_up, dots, *pieces, width)
    other_shares = back_to_rows(1, *after(back_terms[:4], extra), *back_terms[4:])
    own_shares = back_to_rows(0, *after(back_terms[:4], other_shares), *back_terms[4:])
    swapped = swap_cores(own_shares, other_shares, (corner_x, corner_y))
    scaled = after(scaled, swapped[0], swapped[2])
    for_x, for_y, down_own = later_grads(turned, 6, scaled, width)
    down_back = send_down(for_x, for_y, corner_x, corner_y)
    other_turned = turn(from_both_cores(extra, corner_x), 8, lambda i: i)
    gate_away, gate_own = pair_grads(turned, 0, 2, other_turned, 4, d_gate, other_gate, width)
    gate_back = send(gate_away, TO_Y)
    up_away, up_own = pair_grads(turned, 0, 1, other_turned, 0, d_up, other_up, width)
    up_back = send(up_away, TO_X)
    down_back = after(down_back, gate_away, up_away)
    arrived, line = sum_along_line(
        own_shares, swapped, (other_turned, (other_gate, other_up), down_back)
    )
    (grad_down,) = totals((down_own, *down_back))
    outs = unpack(own_shares, arrived, line, expert_ids, width)
    gate_back, up_back = after((gate_back, up_back), outs, grad_down)
    grad_gate, grad_up = totals((gate_own, gate_back), (up_own, up_back))
    return (*outs, grad_gate, grad_up, grad_down)


def on_device(tokens, expert_ids, *rest):
    tok_dev, top_count = expert_ids.shape
    experts = lax.axis_size("expert")
    square_and_line = lax.axis_size("dp") == 4 and experts == 8
    if square_and_line and capacity_of(tok_dev, top_count, experts) == tok_dev:
        return dense_plan(tokens, expert_ids, *rest)
    return slot_plan(tokens, expert_ids, *rest)


def solution(mesh):
    by_token = P(AXES, None)
    by_expert = P("expert", "dp", None)
    return jax.shard_map(
        on_device,
        mesh=mesh,
        in_specs=(by_token,) * 4 + (by_expert,) * 3,
        out_specs=(by_token,) * 3 + (by_expert,) * 3,
        check_vma=False,
    )
```
